32 devices in a mesh: batch: 8 (over z, y), seq: 4 (over x, core).
Axes of the slice: x: 2, y: 2, z: 4, core: 2. Of those that a mesh axis runs over, the one named last changes fastest.
Arguments:
- tokens: bfloat16 [16, 2048, 512], P('batch', 'seq'), may hold values from -6 to 6
- memory: bfloat16 [16, 64, 512], P('batch', 'seq'), may hold values from -6 to 6
- lengths: int32 [16, 8], P('batch'), may hold values from 1 to 1538, 2048 in all within a row
- resets: int32 [16, 4], P('batch'), may hold values 0 or 1
- attn_in: bfloat16 [786432], P(('batch', 'seq')), may hold values from -0.25 to 0.25
- attn_out: bfloat16 [262144], P(('batch', 'seq')), may hold values from -1 to 1
- ffn_in: bfloat16 [1048576], P(('batch', 'seq')), may hold values from -0.25 to 0.25
- ffn_out: bfloat16 [1048576], P(('batch', 'seq')), may hold values from -0.125 to 0.125
- writer_in: bfloat16 [524288], P(('batch', 'seq')), may hold values from -0.1875 to 0.1875
- writer_value: bfloat16 [262144], P(('batch', 'seq')), may hold values from -2 to 2
- norm_gains: bfloat16 [1024], P(('batch', 'seq')), may hold values from 0.5 to 1.5
- memory_init: bfloat16 [32768], P(('batch', 'seq')), may hold values from -6 to 6
- out_cotangent: bfloat16 [16, 2048, 512], P('batch', 'seq'), may hold values from -6 to 6
- memory_cotangent: bfloat16 [16, 64, 512], P('batch', 'seq'), may hold values from -6 to 6
Outputs:
- output: bfloat16 [16, 2048, 512], P('batch', 'seq')
- new_memory: bfloat16 [16, 64, 512], P('batch', 'seq')
- tokens_grad: bfloat16 [16, 2048, 512], P('batch', 'seq')
- memory_grad: bfloat16 [16, 64, 512], P('batch', 'seq')
- attn_in_grad: float32 [786432], P(('batch', 'seq'))
- attn_out_grad: float32 [262144], P(('batch', 'seq'))
- ffn_in_grad: float32 [1048576], P(('batch', 'seq'))
- ffn_out_grad: float32 [1048576], P(('batch', 'seq'))
- writer_in_grad: float32 [524288], P(('batch', 'seq'))
- writer_value_grad: float32 [262144], P(('batch', 'seq'))
- norm_gains_grad: float32 [1024], P(('batch', 'seq'))
- memory_init_grad: float32 [32768], P(('batch', 'seq'))
The draws below stay inside these ranges and needn't reach their ends.
Inputs may be any that keep to these rules, and one draw needn't show every extreme that they name: `lengths`: each row sums to 2048; its longest document is exactly 1538 tokens.
All inputs are finite; a program needn't handle non-finite values. No bound on the sum of `resets` on one device may be relied on, other than what follows from the above.
Results may differ from the reference program's by a relative error of at most 0.028.
Values may be sent and summed in bfloat16 or wider, within the bound.
No kernel may reach another device: no remote copies, remote signals or barrier semaphores. Data moves between devices by JAX's collectives and lax.ppermute only.
A program may use at most 256 MiB of HBM per device.

```python
import math
import jax
import jax.numpy as jnp
import numpy as np
from jax import lax

D = 512
HEADS = 8
HEAD_DIM = 64
FF = 2048
SLOTS = 64
SEGMENT = 512
DOCS = 8
TOK_DEV = 512
LEN = 2048
SEQS = 16
SEGS = 4


def unit_field(key, shape):
    return jax.random.truncated_normal(key, -6.0, 6.0, shape, jnp.float32)


def draw_memory(key, part):
    key = jax.random.fold_in(key, 11)
    return unit_field(key, (SEQS, SLOTS, D)).astype(jnp.bfloat16)


def draw_memory_init(key, part):
    key = jax.random.fold_in(key, 23)
    return unit_field(key, (SLOTS * D,)).astype(jnp.bfloat16)


def set_ends(entries, stream_key, smallest, high):
    place = [jax.random.randint(jax.random.fold_in(stream_key, axis), (), 0, length) for axis, length in enumerate(entries.shape)]
    widest = entries.shape.index(max(entries.shape))
    beside = place[:widest] + [(place[widest] + 1) % entries.shape[widest]] + place[widest + 1:]
    return entries.at[tuple(place)].set(smallest).at[tuple(beside)].set(high)


def levels(key, dims, cuts, least, top_value):
    factor_of, own = 1.0, jax.random.fold_in(key, 6)
    for dim, parts in cuts:
        steps = jnp.exp(jax.random.uniform(jax.random.fold_in(own, dim), (parts,), jnp.float32, least / len(cuts), top_value / len(cuts)))
        factor_of = factor_of * jnp.repeat(steps, dims[dim] // parts).reshape([-1 if axis == dim else 1 for axis in range(len(dims))])
    return factor_of


def length_profile(amount, total, bound, slope):
    portions = [(1 << 20) // math.isqrt(standing ** slope) + 1 for standing in range(2, amount + 1)]
    spare, counts = total - bound - (amount - 1), [1] * (amount - 1)
    while spare > 0:
        candidates = [i for i in range(amount - 1) if counts[i] < bound]
        mass, left = sum([portions[i] for i in candidates]), spare
        for i in candidates:
            extra = min(bound - counts[i], max(1, left * portions[i] // mass), spare)
            counts[i] = counts[i] + extra
            spare = spare - extra
    return np.array([bound] + counts)


def ragged_sizes(stream_key, amount, total, limit, slope):
    if amount == 2:
        one = jax.random.randint(stream_key, (), max(1, total - limit), min(limit, total - 1) + 1)
        return jnp.stack([one, total - one])
    sizes = jnp.asarray(length_profile(amount, total, limit, slope), jnp.int32)
    pairs = (amount - 1) // 2
    donor, sink = sizes[1:1 + 2 * pairs:2], sizes[2:2 + 2 * pairs:2]
    room = jnp.minimum(donor - 1, limit - sink)
    shifted = jax.random.randint(jax.random.fold_in(stream_key, 1), (pairs,), 0, 1 << 20) % (room + 1)
    sizes = sizes.at[1:1 + 2 * pairs:2].set(donor - shifted).at[2:2 + 2 * pairs:2].set(sink + shifted)
    return sizes[jax.random.permutation(jax.random.fold_in(stream_key, 2), amount)]


def gaussian(rng, extent, deviation, reach, shards=(), held_as=jnp.bfloat16):
    drawn = jax.random.normal(rng, extent, jnp.float32) * deviation
    if len(shards) > 0:
        drawn = levels(rng, extent, shards, -0.22, 0.18) * drawn
    return jnp.clip(drawn, min=-reach, max=reach).astype(held_as)


def setup_inputs(seed: int = 0) -> dict:
    key_list = jax.random.split(jax.random.key(seed), 15)
    return {
        "tokens": gaussian(key_list[0], (SEQS, LEN, D), 1.0, 6.0, ((0, 8), (1, 4))),
        "memory": draw_memory(jax.random.fold_in(key_list[14], 71), 0),
        "lengths": jax.vmap(lambda own: ragged_sizes(own, DOCS, LEN, LEN - TOK_DEV + 2, 2))(jax.random.split(key_list[2], SEQS)).reshape((SEQS, DOCS)).astype(jnp.int32),
        "resets": set_ends((jax.random.randint(key_list[3], (SEQS, SEGS), 0, 2) < 1).astype(jnp.int32), jax.random.fold_in(key_list[3], 1), 0, 1),
        "attn_in": gaussian(key_list[4], (3 * D * D,), D ** -0.5, 0.25, ((0, 32),)),
        "attn_out": gaussian(key_list[5], (D * D,), (D // 16) ** -0.5, 1.0, ((0, 32),)),
        "ffn_in": gaussian(key_list[6], (D * FF,), D ** -0.5, 0.25, ((0, 32),)),
        "ffn_out": gaussian(key_list[7], (FF * D,), FF ** -0.5, 0.125, ((0, 32),)),
        "writer_in": gaussian(key_list[8], (2 * D * D,), (2 * D) ** -0.5, 0.1875, ((0, 32),)),
        "writer_value": gaussian(key_list[9], (D * D,), (D // 64) ** -0.5, 2.0, ((0, 32),)),
        "norm_gains": jnp.clip(1.0 + 0.1 * jax.random.normal(key_list[10], (2 * D,), jnp.float32), 0.5, 1.5).astype(jnp.bfloat16),
        "memory_init": draw_memory_init(jax.random.fold_in(key_list[14], 71), 0),
        "out_cotangent": gaussian(key_list[12], (SEQS, LEN, D), 1.0, 6.0, ((0, 8), (1, 4))),
        "memory_cotangent": gaussian(key_list[13], (SEQS, SLOTS, D), 1.0, 6.0, ((0, 8), (1, 4))),
    }


@jax.custom_vjp
def low(v):
    return lax.optimization_barrier(v.astype(jnp.bfloat16)).astype(jnp.float32)

@jax.custom_vjp
def low_back(v):
    return v

def low_keep(v):
    return (low(v), None)

def low_pass(kept, grad):
    return (grad,)

def back_keep(v):
    return (v, None)

def back_low(kept, grad):
    return (low(grad),)
low.defvjp(low_keep, low_pass)
low_back.defvjp(back_keep, back_low)
HIGHEST = lax.Precision.HIGHEST
MASKED = -1e+30

def matmul(former, latter):
    return jnp.dot(former, latter, precision=HIGHEST)

def normalize(values, gain):
    centred = values - lax.optimization_barrier(jnp.mean(values, axis=-1, keepdims=True))
    spread = lax.optimization_barrier(jnp.mean(centred * centred, axis=-1, keepdims=True))
    return centred * lax.rsqrt(spread + 1e-05) * gain

def split_into_heads(values):
    return values.reshape(values.shape[0], HEADS, HEAD_DIM).transpose(1, 0, 2)

def merge_head_axis(values):
    return values.transpose(1, 0, 2).reshape(values.shape[1], HEADS * HEAD_DIM)

def projected(values, weight):
    return low(low_back(matmul(values, weight)))

def forward(tokens, memory, attn_in, attn_out, ffn_in, ffn_out, writer_in, writer_value, norm_gains, memory_init, doc_ids, token_reset):
    logit_scale_factor = HEAD_DIM ** (-0.5)
    normed = low(normalize(tokens, norm_gains[0]))
    queries = split_into_heads(projected(normed, attn_in[0]))
    keys = split_into_heads(projected(normed, attn_in[1]))
    values = split_into_heads(projected(normed, attn_in[2]))
    slot_source = jnp.concatenate([memory, memory_init], axis=0)
    slot_keys = split_into_heads(projected(slot_source, attn_in[1]))
    slot_values = split_into_heads(projected(slot_source, attn_in[2]))
    slot_half = (jnp.arange(2 * SLOTS, dtype=jnp.int32) >= SLOTS).astype(jnp.int32)
    key_pos = jnp.arange(LEN, dtype=jnp.int32)
    block_rows = min(512, LEN)
    blocks = LEN // block_rows

    def attend(inputs):
        query_block, reset_block, doc_block, pos_block = inputs
        slot_scores = low_back(jnp.einsum('hbd,hsd->hbs', query_block, slot_keys, precision=HIGHEST) * logit_scale_factor)
        slot_scores = jnp.where((slot_half[None, :] == reset_block[:, None])[None], slot_scores, MASKED)
        token_scores = low_back(jnp.einsum('hbd,hkd->hbk', query_block, keys, precision=HIGHEST) * logit_scale_factor)
        allowed = (doc_block[:, None] == doc_ids[None, :]) & (key_pos[None, :] <= pos_block[:, None])
        token_scores = jnp.where(allowed[None], token_scores, MASKED)
        weights = low(jax.nn.softmax(jnp.concatenate([slot_scores, token_scores], axis=-1), axis=-1))
        return jnp.einsum('hbs,hsd->hbd', weights[:, :, :2 * SLOTS], slot_values, precision=HIGHEST) + jnp.einsum('hbk,hkd->hbd', weights[:, :, 2 * SLOTS:], values, precision=HIGHEST)
    query_blocks = queries.reshape(HEADS, blocks, block_rows, HEAD_DIM).transpose(1, 0, 2, 3)
    mixed = lax.map(jax.checkpoint(attend), (query_blocks, token_reset.reshape(blocks, block_rows), doc_ids.reshape(blocks, block_rows), key_pos.reshape(blocks, block_rows)))
    attended = mixed.transpose(1, 0, 2, 3).reshape(HEADS, LEN, HEAD_DIM)
    attended = low(low_back(merge_head_axis(attended)))
    branch = low_back(matmul(attended, attn_out))
    middle = tokens + branch
    normed_two = low(normalize(middle, norm_gains[1]))
    hidden_pre = low_back(matmul(normed_two, ffn_in))
    activated = low(jax.nn.gelu(hidden_pre))
    update = low_back(matmul(activated, ffn_out))
    output = middle + update
    out_rows = low(output)
    write_keys = split_into_heads(projected(out_rows, writer_in[1]))
    write_values = split_into_heads(projected(out_rows, writer_value))
    slot_queries = split_into_heads(projected(memory, writer_in[0]))
    token_self_keys = split_into_heads(projected(memory, writer_in[1]))
    self_values = split_into_heads(projected(memory, writer_value))
    self_scores = low_back(lax.optimization_barrier(jnp.sum(slot_queries * token_self_keys, axis=-1)) * logit_scale_factor)
    read_scores = low_back(jnp.einsum('hsd,hkd->hsk', slot_queries, write_keys, precision=HIGHEST) * logit_scale_factor)
    shares = low(jax.nn.softmax(jnp.concatenate([self_scores[:, :, None], read_scores], axis=-1), axis=-1))
    written = shares[:, :, :1] * self_values + jnp.einsum('hsk,hkd->hsd', shares[:, :, 1:], write_values, precision=HIGHEST)
    new_memory = memory + merge_head_axis(written)
    return (output, new_memory)

def reference(tokens, memory, lengths, resets, attn_in, attn_out, ffn_in, ffn_out, writer_in, writer_value, norm_gains, memory_init, out_cotangent, memory_cotangent):
    params = (attn_in.astype(jnp.float32).reshape(3, D, D), attn_out.astype(jnp.float32).reshape(D, D), ffn_in.astype(jnp.float32).reshape(D, FF), ffn_out.astype(jnp.float32).reshape(FF, D), writer_in.astype(jnp.float32).reshape(2, D, D), writer_value.astype(jnp.float32).reshape(D, D), norm_gains.astype(jnp.float32).reshape(2, D), memory_init.astype(jnp.float32).reshape(SLOTS, D))
    positions = jnp.arange(LEN, dtype=jnp.int32)
    segment_of = positions // SEGMENT
    segment_ids = jnp.arange(SEGS, dtype=jnp.int32)

    def per_sequence(totals, seq_item):
        seq_tokens, seq_memory, seq_lengths, seq_resets, seq_cot, mem_cot = seq_item
        doc_ends = jnp.cumsum(seq_lengths).astype(jnp.int32)
        doc_ids = lax.optimization_barrier(jnp.sum((positions[:, None] >= doc_ends[None, :]).astype(jnp.int32), axis=1)).astype(jnp.int32)
        token_reset = lax.optimization_barrier(jnp.sum(jnp.where(segment_of[:, None] == segment_ids[None, :], seq_resets[None, :], 0), axis=1)).astype(jnp.int32)

        def run(tok_in, mem_in, weights):
            return forward(tok_in, mem_in, *weights, doc_ids, token_reset)
        results, pull = jax.vjp(run, seq_tokens.astype(jnp.float32), seq_memory.astype(jnp.float32), params)
        tok_grad, mem_grad, weight_grads = pull((seq_cot.astype(jnp.float32), mem_cot.astype(jnp.float32)))
        totals = jax.tree.map(jnp.add, totals, weight_grads)
        return (totals, (results[0].astype(jnp.bfloat16), results[1].astype(jnp.bfloat16), tok_grad.astype(jnp.bfloat16), mem_grad.astype(jnp.bfloat16)))
    empty_grads = jax.tree.map(jnp.zeros_like, params)
    totals, per_seq = lax.scan(per_sequence, empty_grads, (tokens, memory, lengths, resets, out_cotangent, memory_cotangent))
    flattened = [grad_part.reshape(-1) for grad_part in totals]
    return (per_seq[0], per_seq[1], per_seq[2], per_seq[3], flattened[0], flattened[1], flattened[2], flattened[3], flattened[4], flattened[5], flattened[6], flattened[7])
```

```python
import functools
import math

import jax
import jax.numpy as jnp
from jax import lax
from jax.experimental import pallas as pl
from jax.experimental.pallas import tpu as pltpu
from jax.sharding import PartitionSpec as P

HEADS = 8
HEAD_DIM = 64
FF = 2048
SEGMENT = 512
MASKED = -1e30
LANES = 128
CORE_HEADS = HEADS // 2
CORE_WIDTH = CORE_HEADS * HEAD_DIM
SCALE = HEAD_DIM ** (-0.5)
EXP = math.log2(math.e) * SCALE
LOG2E = math.log2(math.e)
RESET_COL = 8
LOG_COL = 10
NT = (((1,), (1,)), ((), ()))
NN = (((1,), (0,)), ((), ()))
TN = (((0,), (0,)), ((), ()))
GELU_A = math.sqrt(2.0 / math.pi)
GELU_B = 0.044715
BF16 = jnp.bfloat16
F32 = jnp.float32


def dot(left, right, dims=NN):
    return lax.dot_general(left, right, dims, preferred_element_type=F32)


def params():
    return pltpu.CompilerParams(vmem_limit_bytes=56 << 20)


def whole(*shape):
    return pl.BlockSpec(shape, lambda *_: (0,) * len(shape))


def norm_parts(values):
    centred = values - jnp.mean(values, axis=-1, keepdims=True)
    scale = lax.rsqrt(jnp.mean(centred * centred, axis=-1, keepdims=True) + 1e-05)
    return centred * scale, scale


def norm_back(unit, scale, grad, gain):
    back = grad * gain
    return scale * (
        back
        - jnp.mean(back, axis=-1, keepdims=True)
        - unit * jnp.mean(back * unit, axis=-1, keepdims=True)
    )


def in_three(values):
    high = values.astype(BF16).astype(F32)
    rest = values - high
    middle = rest.astype(BF16).astype(F32)
    return high, middle, rest - middle


def put_log(column, values, others):
    high, middle, low = in_three(values)
    out = jnp.where(column == LOG_COL, high, others)
    out = jnp.where(column == LOG_COL + 1, middle, out)
    return jnp.where(column == LOG_COL + 2, low, out)


def aux_column(shape, parity):
    lane = lax.broadcasted_iota(jnp.int32, shape, 1)
    return lane - (1 - parity) * HEAD_DIM


def project_kernel(
    info, own, other, mem_own, mem_other, weight, init, gain,
    q_out, k_out, v_out, normed_out, ks_out, vs_out, rows_out,
):
    rank = pl.program_id(0)
    core = info[0]
    rows = own.shape[1]

    values = jnp.where(rank % 2 == core, own[0], other[0]).astype(F32)
    unit, _ = norm_parts(values)
    normed = (unit * gain[0:1, :].astype(F32)).astype(BF16)
    normed_out[...] = normed
    shape = (rows, LANES)
    position = rank * rows + lax.broadcasted_iota(jnp.int32, shape, 0)
    doc = jnp.zeros(shape, jnp.int32)
    for k in range(8):
        doc = doc + (position >= info[2 + k]).astype(jnp.int32)
    reset = info[10 + (rank * rows) // SEGMENT]
    for which, out in ((0, q_out), (1, k_out), (2, v_out)):
        result = dot(normed, weight[which])
        for pair in range(2):
            mine = result[:, pair * LANES : (pair + 1) * LANES]
            for parity in range(2):
                column = aux_column(shape, parity)
                inside = (column >= 0) & (column < HEAD_DIM)
                if which == 0:
                    side = jnp.where(column == doc, 1.0, 0.0)
                    side = jnp.where(column == RESET_COL, reset.astype(F32), side)
                    side = jnp.where(column == RESET_COL + 1, 1.0 - reset.astype(F32), side)
                elif which == 1:
                    side = jnp.where((column < 8) & (column != doc), MASKED, 0.0)
                    side = jnp.where((column >= LOG_COL) & (column < LOG_COL + 3), 1.0, side)
                else:
                    side = jnp.ones(shape, F32)
                out[2 * pair + parity] = jnp.where(inside, side, mine).astype(BF16)

    @pl.when(rank == 0)
    def _():
        part = mem_own.shape[1]
        for k in range(4):
            rows_out[k * part : (k + 1) * part, :] = jnp.where(
                core == k % 2, mem_own[k // 2], mem_other[k // 2]
            )
        slots = rows_out.shape[0]
        source = jnp.concatenate([rows_out[...], init[...]], axis=0)
        shape = (2 * slots, LANES)
        start = (lax.broadcasted_iota(jnp.int32, shape, 0) >= slots).astype(jnp.int32)
        for which, out in ((1, ks_out), (2, vs_out)):
            result = dot(source, weight[which])
            for pair in range(2):
                mine = result[:, pair * LANES : (pair + 1) * LANES]
                for parity in range(2):
                    column = aux_column(shape, parity)
                    inside = (column >= 0) & (column < HEAD_DIM)
                    if which == 1:
                        side = jnp.where(column == RESET_COL + start, MASKED, 0.0)
                        side = jnp.where((column >= LOG_COL) & (column < LOG_COL + 3), 1.0, side)
                    else:
                        side = jnp.ones(shape, F32)
                    out[2 * pair + parity] = jnp.where(inside, side, mine).astype(BF16)


def project(info, own, other, weight, init, gains, rows, slot_part):
    width = own.shape[2]
    slots = 4 * slot_part
    length = 4 * rows
    at = rows // slot_part
    tokens = pl.BlockSpec((1, rows, width), lambda r, _: (r // 2, 0, 0))
    memory = pl.BlockSpec((2, slot_part, width), lambda r, _: (0, at, 0))
    heads = pl.BlockSpec((CORE_HEADS, rows, LANES), lambda r, _: (0, r, 0))
    return pl.pallas_call(
        project_kernel,
        grid_spec=pltpu.PrefetchScalarGridSpec(
            num_scalar_prefetch=1,
            grid=(4,),
            in_specs=[
                tokens, tokens, memory, memory,
                whole(3, width, CORE_WIDTH), whole(slots, width), whole(2, width),
            ],
            out_specs=[
                heads, heads, heads,
                pl.BlockSpec((rows, width), lambda r, _: (r, 0)),
                whole(CORE_HEADS, 2 * slots, LANES), whole(CORE_HEADS, 2 * slots, LANES),
                whole(slots, width),
            ],
        ),
        out_shape=[
            *[jax.ShapeDtypeStruct((CORE_HEADS, length, LANES), BF16)] * 3,
            jax.ShapeDtypeStruct((length, width), BF16),
            *[jax.ShapeDtypeStruct((CORE_HEADS, 2 * slots, LANES), BF16)] * 2,
            jax.ShapeDtypeStruct((slots, width), BF16),
        ],
        compiler_params=params(),
        name="project",
    )(info, own, other, own, other, weight, init, gains)


def attend_kernel(block, q_ref, k_ref, v_ref, ks_ref, vs_ref, o_ref, q_out):
    length = q_ref.shape[1]
    parity = pl.program_id(1)
    column = aux_column((block, LANES), parity)
    keep = (column < 0) | (column >= HEAD_DIM)
    row = lax.broadcasted_iota(jnp.int32, (block, block), 0)
    key = lax.broadcasted_iota(jnp.int32, (block, block), 1)
    for i in range(length // block):
        low, high = i * block, (i + 1) * block
        q = q_ref[0, low:high, :]
        slot = dot(q, ks_ref[0], NT)
        scores = dot(q, k_ref[0, :high, :], NT)
        last = jnp.where(row >= key, scores[:, low:], MASKED)
        scores = jnp.concatenate([scores[:, :low], last], axis=1) if i else last
        top = jnp.maximum(
            jnp.max(scores, axis=1, keepdims=True), jnp.max(slot, axis=1, keepdims=True)
        )
        share = jnp.exp2((scores - top) * EXP).astype(BF16)
        slot_share = jnp.exp2((slot - top) * EXP).astype(BF16)
        total = dot(share, v_ref[0, :high, :]) + dot(slot_share, vs_ref[0])
        count = jnp.where(parity == 0, total[:, HEAD_DIM : HEAD_DIM + 1], total[:, 0:1])
        o_ref[low:high, :] = jnp.where(keep, (total / count).astype(BF16), o_ref[low:high, :])
        log = top + jnp.log2(count) * (1.0 / EXP)
        q_out[0, low:high, :] = put_log(column, -log, q.astype(F32)).astype(BF16)


def attend(q, k, v, ks, vs):
    heads, length, _ = q.shape
    count = ks.shape[1]
    head = pl.BlockSpec((1, length, LANES), lambda p, e: (2 * p + e, 0, 0))
    slot = pl.BlockSpec((1, count, LANES), lambda p, e: (2 * p + e, 0, 0))
    return pl.pallas_call(
        functools.partial(attend_kernel, 256),
        grid=(heads // 2, 2),
        in_specs=[head, head, head, slot, slot],
        out_specs=[pl.BlockSpec((length, LANES), lambda p, e: (0, p)), head],
        out_shape=[
            jax.ShapeDtypeStruct((length, CORE_WIDTH), BF16),
            jax.ShapeDtypeStruct(q.shape, BF16),
        ],
        compiler_params=params(),
        name="attend",
    )(q, k, v, ks, vs)


def attend_back_kernel(
    kb, qb, info, q_ref, k_ref, v_ref, ks_ref, vs_ref, own_ref, other_ref, o_ref,
    dq_ref, dk_ref, dv_ref, dks_ref, dvs_ref, d_ref, acc_ref,
):
    length = q_ref.shape[1]
    parity = pl.program_id(1)
    core = info[0]
    rows = own_ref.shape[1]
    column = aux_column((rows, LANES), parity)
    inside = (column < 0) | (column >= HEAD_DIM)
    for r in range(length // rows):
        low, high = r * rows, (r + 1) * rows
        d = jnp.where(core == r % 2, own_ref[r // 2], other_ref[r // 2]).astype(F32)
        delta = jnp.sum(
            jnp.where(inside, d * o_ref[low:high, :].astype(F32), 0.0), axis=1, keepdims=True
        )
        d_ref[low:high, :] = jnp.where(
            inside, d, put_log(column, -delta, jnp.zeros_like(d))
        ).astype(BF16)
    acc_ref[...] = jnp.zeros_like(acc_ref)

    def merged(ref, low, high, value):
        column = aux_column(value.shape, parity)
        keep = (column < 0) | (column >= HEAD_DIM)
        ref[low:high, :] = jnp.where(keep, value.astype(BF16), ref[low:high, :])

    count = ks_ref.shape[1]
    pieces = [(ks_ref, vs_ref, dks_ref, dvs_ref, 0, count, None)]
    pieces += [(k_ref, v_ref, dk_ref, dv_ref, j, j + kb, j) for j in range(0, length, kb)]
    for keys, values, dk_out, dv_out, start, stop, first in pieces:
        k = keys[0, start:stop, :]
        v = values[0, start:stop, :]
        turned = k.astype(F32).T.astype(BF16)
        dk = jnp.zeros((stop - start, LANES), F32)
        dv = jnp.zeros((stop - start, LANES), F32)
        low = first or 0
        while low < length:
            high = min((low // qb + 1) * qb, length)
            q = q_ref[0, low:high, :]
            d = d_ref[low:high, :]
            scores = dot(k, q, NT)
            share = jnp.exp2(scores * EXP)
            if first is not None and low < stop:
                key = first + lax.broadcasted_iota(jnp.int32, scores.shape, 0)
                position = low + lax.broadcasted_iota(jnp.int32, scores.shape, 1)
                share = jnp.where(key <= position, share, 0.0)
            ds = (share * dot(v, d, NT)).astype(BF16)
            dv = dv + dot(share.astype(BF16), d)
            dk = dk + dot(ds, q)
            acc_ref[:, low:high] += dot(turned, ds)
            low = high
        merged(dk_out, start, stop, dk * SCALE)
        merged(dv_out, start, stop, dv)
    merged(dq_ref, 0, length, acc_ref[...].T * SCALE)


def attend_back(info, q, k, v, ks, vs, own, other, o):
    heads, length, _ = q.shape
    count = ks.shape[1]
    rows = own.shape[1]
    head = pl.BlockSpec((1, length, LANES), lambda p, e, _: (2 * p + e, 0, 0))
    slot = pl.BlockSpec((1, count, LANES), lambda p, e, _: (2 * p + e, 0, 0))
    grads = pl.BlockSpec((2, rows, LANES), lambda p, e, _: (0, 0, p))
    pair = pl.BlockSpec((length, LANES), lambda p, e, _: (0, p))
    slot_pair = pl.BlockSpec((count, LANES), lambda p, e, _: (0, p))
    return pl.pallas_call(
        functools.partial(attend_back_kernel, 256, 1024),
        grid_spec=pltpu.PrefetchScalarGridSpec(
            num_scalar_prefetch=1,
            grid=(heads // 2, 2),
            in_specs=[head, head, head, slot, slot, grads, grads, pair],
            out_specs=[pair, pair, pair, slot_pair, slot_pair],
            scratch_shapes=[pltpu.VMEM((length, LANES), BF16), pltpu.VMEM((LANES, length), F32)],
        ),
        out_shape=[
            *[jax.ShapeDtypeStruct((length, CORE_WIDTH), BF16)] * 3,
            *[jax.ShapeDtypeStruct((count, CORE_WIDTH), BF16)] * 2,
        ],
        compiler_params=params(),
        name="attend_back",
    )(info, q, k, v, ks, vs, own, other, o)


def forward_kernel(
    info, tokens, own, other, w_out, w_up, w_down, w_write, w_value, gains,
    middle_out, normed_out, act_out, slope_out, result_out, keys_out, values_out,
):
    core = info[0]
    mine = pl.multiple_of(core * CORE_WIDTH, CORE_WIDTH)
    rest = pl.multiple_of((1 - core) * CORE_WIDTH, CORE_WIDTH)
    middle = (
        tokens[0].astype(F32)
        + dot(own[...], w_out[pl.ds(mine, CORE_WIDTH), :])
        + dot(other[0], w_out[pl.ds(rest, CORE_WIDTH), :])
    )
    middle_out[0] = middle
    unit, _ = norm_parts(middle)
    normed = (unit * gains[1:2, :].astype(F32)).astype(BF16)
    normed_out[0] = normed
    chunk = w_up.shape[2]
    for k in range(w_up.shape[0]):
        pre = dot(normed, w_up[k])
        square = pre * pre
        bend = jnp.tanh(GELU_A * (pre + GELU_B * (square * pre)))
        half = 0.5 * (1.0 + bend)
        act = (pre * half).astype(BF16)
        slope = half + 0.5 * pre * (1.0 - bend * bend) * (
            GELU_A * (1.0 + (3.0 * GELU_B) * square)
        )
        act_out[0, :, k * chunk : (k + 1) * chunk] = act
        slope_out[0, :, k * chunk : (k + 1) * chunk] = slope.astype(BF16)
    low = (middle + dot(act_out[0], w_down[...])).astype(BF16)
    result_out[0] = low
    keys_out[0] = dot(low, w_write[1]).astype(BF16)
    values_out[0] = dot(low, w_value[...]).astype(BF16)


def forward(info, tokens, o, other, weights, gains, rows):
    width = tokens.shape[2]
    w_out, w_up, w_down, w_write, w_value = weights
    block = pl.BlockSpec((1, rows, width), lambda i, _: (i, 0, 0))
    wide = pl.BlockSpec((1, rows, FF), lambda i, _: (i, 0, 0))
    shape = (2, rows, width)
    return pl.pallas_call(
        forward_kernel,
        grid_spec=pltpu.PrefetchScalarGridSpec(
            num_scalar_prefetch=1,
            grid=(2,),
            in_specs=[
                block,
                pl.BlockSpec((rows, CORE_WIDTH), lambda i, info: (2 * i + info[0], 0)),
                pl.BlockSpec((1, rows, CORE_WIDTH), lambda i, _: (i, 0, 0)),
                *[whole(*w.shape) for w in weights],
                whole(*gains.shape),
            ],
            out_specs=[block, block, wide, wide, block, block, block],
        ),
        out_shape=[
            jax.ShapeDtypeStruct(shape, F32),
            jax.ShapeDtypeStruct(shape, BF16),
            *[jax.ShapeDtypeStruct((2, rows, FF), BF16)] * 2,
            *[jax.ShapeDtypeStruct(shape, BF16)] * 3,
        ],
        compiler_params=params(),
        name="feed_forward",
    )(info, tokens, o, other, *weights, gains)


def backward_kernel(
    info, cot, d_keys, d_values, result, middle, normed, act, slope, own_a, own_b, other,
    w_out, w_up, w_down, w_write, w_value, gains, rows_ref, d_query, d_self_key, d_self_value,
    mem_cot,
    g_up, g_down, g_out, g_write, g_value, d_middle_out, d_own, d_other, g_gain, d_memory,
    d_result_ref, d_update_ref, d_normed_ref,
):
    step = pl.program_id(0)
    core = info[0]
    count, rows, width = result.shape
    total = count * rows
    mine = pl.multiple_of(core * CORE_WIDTH, CORE_WIDTH)
    rest = pl.multiple_of((1 - core) * CORE_WIDTH, CORE_WIDTH)

    @pl.when(step == 0)
    def _():
        dk = d_keys[...].reshape(total, width)
        dv = d_values[...].reshape(total, width)
        d_result = (
            cot[...].reshape(total, width).astype(F32)
            + dot(dk, w_write[1], NT)
            + dot(dv, w_value[...], NT)
        )
        d_result_ref[...] = d_result
        d_update_ref[...] = d_result.astype(BF16)
        d_normed_ref[...] = jnp.zeros_like(d_normed_ref)
        out = result[...].reshape(total, width)
        memory = rows_ref[...]
        g_write[0] = dot(memory, d_query[...], TN).astype(BF16)
        g_write[1] = (dot(out, dk, TN) + dot(memory, d_self_key[...], TN)).astype(BF16)
        g_value[...] = (dot(out, dv, TN) + dot(memory, d_self_value[...], TN)).astype(BF16)
        d_memory[...] = (
            mem_cot[...]
            + dot(d_query[...], w_write[0], NT)
            + dot(d_self_key[...], w_write[1], NT)
            + dot(d_self_value[...], w_value[...], NT)
        )

    d_update = d_update_ref[...]
    d_act = dot(d_update, w_down[...], NT)
    d_hidden = (d_act * slope[...].reshape(total, -1).astype(F32)).astype(BF16)
    g_down[...] = dot(act[...].reshape(total, -1), d_update, TN).astype(BF16)
    g_up[0] = dot(normed[...].reshape(total, width), d_hidden, TN).astype(BF16)
    d_normed_ref[...] += dot(d_hidden, w_up[0], NT)

    @pl.when(step == pl.num_programs(0) - 1)
    def _():
        gain = gains[1:2, :].astype(F32)
        unit, scale = norm_parts(middle[...].reshape(total, width))
        d_normed = d_normed_ref[...]
        g_gain[...] = jnp.sum(d_normed * unit, axis=0, keepdims=True)
        d_middle = d_result_ref[...] + norm_back(unit, scale, d_normed, gain)
        d_middle_out[...] = d_middle.reshape(count, rows, width)
        d_branch = d_middle.astype(BF16)
        d_own[...] = (
            dot(d_branch, w_out[pl.ds(mine, CORE_WIDTH), :], NT)
            .astype(BF16)
            .reshape(count, rows, CORE_WIDTH)
        )
        d_other[...] = (
            dot(d_branch, w_out[pl.ds(rest, CORE_WIDTH), :], NT)
            .astype(BF16)
            .reshape(count, rows, CORE_WIDTH)
        )
        g_out[pl.ds(mine, CORE_WIDTH), :] = (
            dot(own_a[...], d_branch[:rows], TN) + dot(own_b[...], d_branch[rows:], TN)
        ).astype(BF16)
        g_out[pl.ds(rest, CORE_WIDTH), :] = dot(
            other[...].reshape(total, CORE_WIDTH), d_branch, TN
        ).astype(BF16)


def backward(info, cot, d_keys, d_values, result, middle, normed, act, slope, o, other, weights,
             gains, memory, slot_grads, mem_cot, rows):
    width = result.shape[2]
    w_out, w_up, w_down, w_write, w_value = weights
    steps = w_up.shape[0]
    chunk = FF // steps
    all_rows = whole(2, rows, width)
    wide = pl.BlockSpec((2, rows, chunk), lambda i, _: (0, 0, i))
    slots = whole(*memory.shape)
    up = pl.BlockSpec((1, width, chunk), lambda i, _: (i, 0, 0))
    down = pl.BlockSpec((chunk, width), lambda i, _: (i, 0))
    half = whole(2, rows, CORE_WIDTH)
    return pl.pallas_call(
        backward_kernel,
        grid_spec=pltpu.PrefetchScalarGridSpec(
            num_scalar_prefetch=1,
            grid=(steps,),
            in_specs=[
                all_rows, all_rows, all_rows, all_rows, all_rows, all_rows, wide, wide,
                pl.BlockSpec((rows, CORE_WIDTH), lambda i, info: (info[0], 0)),
                pl.BlockSpec((rows, CORE_WIDTH), lambda i, info: (2 + info[0], 0)),
                half, whole(*w_out.shape), up, down, whole(*w_write.shape), whole(*w_value.shape),
                whole(*gains.shape), slots, slots, slots, slots, slots,
            ],
            out_specs=[
                up, down, whole(width, width), whole(2, width, width), whole(width, width),
                all_rows, half, half, whole(1, width), slots,
            ],
            scratch_shapes=[
                pltpu.VMEM((2 * rows, width), F32),
                pltpu.VMEM((2 * rows, width), BF16),
                pltpu.VMEM((2 * rows, width), F32),
            ],
        ),
        out_shape=[
            jax.ShapeDtypeStruct(w_up.shape, BF16),
            jax.ShapeDtypeStruct(w_down.shape, BF16),
            jax.ShapeDtypeStruct((width, width), BF16),
            jax.ShapeDtypeStruct((2, width, width), BF16),
            jax.ShapeDtypeStruct((width, width), BF16),
            jax.ShapeDtypeStruct((2, rows, width), F32),
            *[jax.ShapeDtypeStruct((2, rows, CORE_WIDTH), BF16)] * 2,
            jax.ShapeDtypeStruct((1, width), F32),
            jax.ShapeDtypeStruct(memory.shape, F32),
        ],
        compiler_params=params(),
        name="feed_forward_back",
    )(info, cot, d_keys, d_values, result, middle, normed, act, slope, o, o, other, *weights,
      gains, memory, *slot_grads, mem_cot)


def head_mask(shape, head):
    lane = lax.broadcasted_iota(jnp.int32, shape, 1)
    return (lane >= head * HEAD_DIM) & (lane < (head + 1) * HEAD_DIM)


def stacked_heads(values):
    return jnp.concatenate(
        [jnp.where(head_mask(values.shape, h), values, 0.0) for h in range(HEADS)], axis=0
    )


def joined_heads(stacked, slots):
    out = None
    for h in range(HEADS):
        part = stacked[h * slots : (h + 1) * slots, :]
        shape = (slots, HEADS * HEAD_DIM)
        part = jnp.broadcast_to(part, shape)
        out = part if out is None else jnp.where(head_mask(shape, h), part, out)
    return out


def column_of_heads(values):
    return jnp.concatenate(
        [values[:, h * HEAD_DIM : h * HEAD_DIM + 1] for h in range(HEADS)], axis=0
    )


def head_sums(values):
    return jnp.concatenate(
        [
            jnp.sum(jnp.where(head_mask(values.shape, h), values, 0.0), axis=1, keepdims=True)
            for h in range(HEADS)
        ],
        axis=0,
    )


def write_kernel(keys, values, memory, w_write, w_value, query_out, key_out, value_out, stats):
    slots = memory.shape[0]
    total = keys.shape[0] * keys.shape[1]
    rows = memory[...]
    query = dot(rows, w_write[0]).astype(BF16)
    query_out[...] = query
    key_out[...] = dot(rows, w_write[1]).astype(BF16)
    value_out[...] = dot(rows, w_value[...]).astype(BF16)
    stacked = stacked_heads(query.astype(F32)).astype(BF16)
    scores = dot(stacked, keys[...].reshape(total, -1), NT)
    top = jnp.max(scores, axis=1, keepdims=True)
    share = jnp.exp2((scores - top) * EXP)
    stats[0] = joined_heads(top, slots)
    stats[1] = joined_heads(jnp.sum(share, axis=1, keepdims=True), slots)
    stats[2] = joined_heads(dot(share.astype(BF16), values[...].reshape(total, -1)), slots)


def write(keys, values, memory, w_write, w_value):
    slots, width = memory.shape
    small = jax.ShapeDtypeStruct((slots, width), BF16)
    return pl.pallas_call(
        write_kernel,
        out_shape=[small, small, small, jax.ShapeDtypeStruct((3, slots, width), F32)],
        compiler_params=params(),
        name="write",
    )(keys, values, memory, w_write, w_value)


def write_back_kernel(
    info, own, other, query, key, value, memory, cot_own, cot_other, keys, values,
    new_out, d_keys, d_values, d_query, d_key, d_value, cot_mine,
):
    core = info[0]
    slots, width = memory.shape
    part = cot_own.shape[1]
    total = keys.shape[0] * keys.shape[1]
    cot = jnp.concatenate(
        [jnp.where(core == k % 2, cot_own[k // 2], cot_other[k // 2]) for k in range(4)], axis=0
    ).astype(F32)
    q = query[...].astype(F32)
    sk = key[...].astype(F32)
    sv = value[...].astype(F32)
    self_column = head_sums(q * sk)
    self_scores = joined_heads(self_column, slots)
    top = jnp.maximum(jnp.maximum(own[0], other[0]), self_scores)
    own_share = jnp.exp2((own[0] - top) * EXP)
    other_share = jnp.exp2((other[0] - top) * EXP)
    self_share = jnp.exp2((self_scores - top) * EXP)
    count = own[1] * own_share + other[1] * other_share + self_share
    written = (
        own[2] * own_share + other[2] * other_share + self_share.astype(BF16).astype(F32) * sv
    ) / count
    new_out[...] = (memory[...].astype(F32) + written).astype(BF16)
    log = top + jnp.log2(count) * (1.0 / EXP)
    log_column = column_of_heads(log)
    delta_column = head_sums(cot * written)
    delta = joined_heads(delta_column, slots)
    stacked = stacked_heads(q).astype(BF16)
    stacked_cot = stacked_heads(cot).astype(BF16)
    flat_keys = keys[...].reshape(total, width)
    share = jnp.exp2((dot(stacked, flat_keys, NT) - log_column) * EXP)
    d_share = dot(stacked_cot, values[...].reshape(total, width), NT)
    d_scores = (share * (d_share - delta_column)).astype(BF16)
    d_values[...] = dot(share.astype(BF16), stacked_cot, TN).astype(BF16).reshape(d_values.shape)
    d_keys[...] = (dot(d_scores, stacked, TN) * SCALE).astype(BF16).reshape(d_keys.shape)
    d_query_part = joined_heads(dot(d_scores, flat_keys), slots) * SCALE
    mine = (lax.broadcasted_iota(jnp.int32, (slots, width), 0) // part) % 2 == core
    self_probs = jnp.exp2((self_scores - log) * EXP)
    self_dp = joined_heads(head_sums(cot * sv), slots)
    self_ds = (self_probs * (self_dp - delta)).astype(BF16).astype(F32) * SCALE
    self_ds = jnp.where(mine, self_ds, 0.0)
    d_query[...] = (d_query_part + self_ds * sk).astype(BF16)
    d_key[...] = (self_ds * q).astype(BF16)
    d_value[...] = jnp.where(mine, self_probs.astype(BF16).astype(F32) * cot, 0.0).astype(BF16)
    cot_mine[...] = jnp.where(mine, cot, 0.0)


def write_back(info, own, other, query, key, value, memory, cot_own, cot_other, keys, values, rows):
    slots, width = memory.shape
    part = slots // 4
    at = rows // part
    small = jax.ShapeDtypeStruct((slots, width), BF16)
    cots = pl.BlockSpec((2, part, width), lambda i, _: (0, at, 0))
    flat = whole(slots, width)
    stats = whole(3, slots, width)
    big = whole(2, rows, width)
    return pl.pallas_call(
        write_back_kernel,
        grid_spec=pltpu.PrefetchScalarGridSpec(
            num_scalar_prefetch=1,
            grid=(1,),
            in_specs=[stats, stats, flat, flat, flat, flat, cots, cots, big, big],
            out_specs=[flat, big, big, flat, flat, flat, flat],
        ),
        out_shape=[
            small,
            *[jax.ShapeDtypeStruct((2, rows, width), BF16)] * 2,
            small, small, small,
            jax.ShapeDtypeStruct((slots, width), F32),
        ],
        compiler_params=params(),
        name="write_back",
    )(info, own, other, query, key, value, memory, cot_own, cot_other, keys, values)


def project_back_kernel(
    normed, dq, dk, dv, weight, memory, init, dks, dvs, d_normed_out, g_out, d_slots, acc_ref
):
    rank = pl.program_id(0)

    @pl.when(rank == 0)
    def _():
        source = jnp.concatenate([memory[...], init[...]], axis=0)
        acc_ref[0] = jnp.zeros(acc_ref.shape[1:], F32)
        acc_ref[1] = dot(source, dks[...], TN)
        acc_ref[2] = dot(source, dvs[...], TN)
        d_slots[...] = dot(dks[...], weight[1], NT) + dot(dvs[...], weight[2], NT)

    rows = normed[...]
    grads = (dq[...], dk[...], dv[...])
    d_normed_out[...] = (
        dot(grads[0], weight[0], NT) + dot(grads[1], weight[1], NT) + dot(grads[2], weight[2], NT)
    ).astype(BF16)
    for k in range(3):
        acc_ref[k] += dot(rows, grads[k], TN)

    @pl.when(rank == pl.num_programs(0) - 1)
    def _():
        g_out[...] = acc_ref[...].astype(BF16)


def project_back(normed, dq, dk, dv, weight, memory, init, dks, dvs, rows):
    length, width = normed.shape
    slots = memory.shape[0]
    block = pl.BlockSpec((rows, width), lambda r: (r, 0))
    half = pl.BlockSpec((rows, CORE_WIDTH), lambda r: (r, 0))
    return pl.pallas_call(
        project_back_kernel,
        grid=(length // rows,),
        in_specs=[
            block, half, half, half, whole(*weight.shape), whole(slots, width),
            whole(slots, width), whole(*dks.shape), whole(*dvs.shape),
        ],
        out_specs=[block, whole(*weight.shape), whole(2 * slots, width)],
        out_shape=[
            jax.ShapeDtypeStruct((length, width), BF16),
            jax.ShapeDtypeStruct(weight.shape, BF16),
            jax.ShapeDtypeStruct((2 * slots, width), F32),
        ],
        scratch_shapes=[pltpu.VMEM(weight.shape, F32)],
        compiler_params=params(),
        name="project_back",
    )(normed, dq, dk, dv, weight, memory, init, dks, dvs)


def inputs_back_kernel(tokens, mine, other, d_middle, gains, d_out, g_gain):
    step = pl.program_id(0)
    unit, scale = norm_parts(tokens[0].astype(F32))
    d_normed = mine[...].astype(F32) + other[0].astype(F32)
    gain = gains[0:1, :].astype(F32)
    d_out[0] = (d_middle[0] + norm_back(unit, scale, d_normed, gain)).astype(BF16)
    part = jnp.sum(d_normed * unit, axis=0, keepdims=True)

    @pl.when(step == 0)
    def _():
        g_gain[...] = part

    @pl.when(step > 0)
    def _():
        g_gain[...] += part


def inputs_back(info, tokens, d_normed, other, d_middle, gains, rows):
    width = tokens.shape[2]
    block = pl.BlockSpec((1, rows, width), lambda i, _: (i, 0, 0))
    return pl.pallas_call(
        lambda info, *refs: inputs_back_kernel(*refs),
        grid_spec=pltpu.PrefetchScalarGridSpec(
            num_scalar_prefetch=1,
            grid=(2,),
            in_specs=[
                block,
                pl.BlockSpec((rows, width), lambda i, info: (2 * i + info[0], 0)),
                block, block, whole(*gains.shape),
            ],
            out_specs=[block, whole(1, width)],
        ),
        out_shape=[
            jax.ShapeDtypeStruct((2, rows, width), BF16),
            jax.ShapeDtypeStruct((1, width), F32),
        ],
        compiler_params=params(),
        name="inputs_back",
    )(info, tokens, d_normed, other, d_middle, gains)


def swap(value, over_batch, over_seq):
    batch, seq = lax.axis_size("batch"), lax.axis_size("seq")
    pairs = [
        (i * seq + j, (i ^ over_batch) * seq + (j ^ over_seq))
        for i in range(batch)
        for j in range(seq)
    ]
    return lax.ppermute(value, ("batch", "seq"), pairs)


def chip_groups():
    batch = lax.axis_index("batch")
    chip = lax.axis_index("seq") // 2
    stages = [(4, 2 * (batch & 1) + chip, lambda k: (k >> 1, 2 * (k & 1)))]
    bits = lax.axis_size("batch").bit_length() - 1
    at = 1
    while at < bits:
        count = min(2, bits - at)
        stages.append(
            (1 << count, (batch >> at) & ((1 << count) - 1), lambda k, at=at: (k << at, 0))
        )
        at += count
    return stages


def in_order(pieces, own):
    bit = 1
    while bit < len(pieces):
        turned = (own & bit) > 0
        pieces = [jnp.where(turned, pieces[k ^ bit], pieces[k]) for k in range(len(pieces))]
        bit *= 2
    return jnp.stack(pieces)


def gather_chips(piece):
    stages = chip_groups()
    shape = piece.shape
    for size, own, peer in reversed(stages):
        piece = in_order([piece] + [swap(piece, *peer(k)) for k in range(1, size)], own)
    count = len(stages)
    piece = piece.transpose(*reversed(range(count)), *range(count, piece.ndim))
    return piece.reshape(-1, *shape)


def sum_to_chips(pieces):
    shape = pieces.shape[1:]
    stages = chip_groups()
    for k, (size, own, peer) in enumerate(stages):
        pieces = pieces.reshape(-1, size, *shape)
        parts = [
            lax.dynamic_index_in_dim(pieces, own ^ j, 1, keepdims=False) for j in range(size)
        ]
        total = parts[0].astype(F32)
        for j in range(1, size):
            total = total + swap(parts[j], *peer(j)).astype(F32)
        pieces = total if k == len(stages) - 1 else total.astype(BF16)
    return pieces.reshape(shape)


def by_core(core, mine, other, axis=0):
    return jnp.where(
        core == 0,
        jnp.concatenate([mine, other], axis=axis),
        jnp.concatenate([other, mine], axis=axis),
    )


def by_chip(chip, mine, other):
    return jnp.where(chip == 0, jnp.stack([mine, other]), jnp.stack([other, mine]))


def pick(array, index, axis=0):
    return lax.dynamic_index_in_dim(array, index, axis, keepdims=False)


def per_device(
    tokens, memory, lengths, resets, attn_in, attn_out, ffn_in, ffn_out, writer_in, writer_value,
    norm_gains, memory_init, out_cotangent, memory_cotangent,
):
    _, rows, width = tokens.shape
    devices = lax.axis_size("batch") * lax.axis_size("seq")
    rank = lax.axis_index("seq")
    chip, core = rank // 2, rank % 2
    slot_part = memory.shape[1]
    slots = 4 * slot_part
    chunks = FF // width

    ends = jnp.cumsum(pick(lengths, chip))
    info = jnp.concatenate([jnp.stack([core, chip]), ends, pick(resets, chip)]).astype(jnp.int32)

    def to_chip(big, small):
        mine = jnp.concatenate([pick(big, chip), pick(small, chip)], axis=0)
        away = jnp.concatenate([pick(big, 1 - chip), pick(small, 1 - chip)], axis=0)
        return by_chip(chip, mine, swap(away, 0, 2))

    misc = jnp.concatenate([memory_init, norm_gains])
    misc_rows = -(-misc.shape[0] // CORE_WIDTH)
    misc = jnp.pad(misc, (0, misc_rows * CORE_WIDTH - misc.shape[0])).reshape(misc_rows, CORE_WIDTH)
    attn_rows = attn_in.reshape(-1, 2, CORE_WIDTH)
    own_rows = attn_rows.shape[0]
    mine = jnp.concatenate([pick(attn_rows, core, 1), misc], axis=0)
    theirs = swap(jnp.concatenate([pick(attn_rows, 1 - core, 1), misc], axis=0), 0, 1)
    piece = jnp.concatenate(
        [
            by_core(core, mine[:own_rows], theirs[:own_rows]),
            by_core(core, mine[own_rows:], theirs[own_rows:]),
        ],
        axis=0,
    )
    gathered = gather_chips(piece)
    w_qkv = gathered[:, : 2 * own_rows].reshape(3, width, CORE_WIDTH)
    misc = gathered[:, 2 * own_rows :].reshape(devices, -1)
    init = misc[:, : memory_init.shape[0]].reshape(slots, width)
    gains = misc[:, memory_init.shape[0] :][:, : norm_gains.shape[0]].reshape(2, width)

    def columns(flat):
        return flat.reshape(-1, chunks, width).transpose(1, 0, 2).reshape(-1, width)

    parts = [
        attn_out.reshape(-1, width), columns(ffn_in), ffn_out.reshape(-1, width),
        writer_in.reshape(-1, width), writer_value.reshape(-1, width),
    ]
    sizes = [part.shape[0] for part in parts]
    cuts = [sum(sizes[:k]) for k in range(len(sizes) + 1)]
    packed = lax.all_gather(jnp.concatenate(parts, axis=0), ("batch", "seq"), axis=0)
    fields = [packed[:, cuts[k] : cuts[k + 1]] for k in range(len(sizes))]
    weights = (
        fields[0].reshape(width, width),
        fields[1].reshape(devices, chunks, -1, width).transpose(1, 0, 2, 3).reshape(chunks, width, width),
        fields[2].reshape(FF, width),
        fields[3].reshape(2, width, width),
        fields[4].reshape(width, width),
    )
    w_out, w_up, w_down, w_write, w_value = weights

    own = to_chip(tokens, memory)
    other = swap(own, 0, 1)
    q, k, v, normed, ks, vs, mem_rows = project(
        info, own, other, w_qkv, init, gains, rows, slot_part
    )
    cots = to_chip(out_cotangent, memory_cotangent)
    cots_other = swap(cots[:, rows:], 0, 1)
    cots_other = jnp.concatenate([jnp.zeros((2, rows, width), BF16), cots_other], axis=1)
    o, q_log = attend(q, k, v, ks, vs)
    o_other = swap(pick(o.reshape(2, 2, rows, CORE_WIDTH), 1 - core, 1), 0, 1)
    middle, normed_two, act, slope, result, keys, values = forward(
        info, own, o, o_other, weights, gains, rows
    )
    wq, sk, sv, stats = write(keys, values, mem_rows, w_write, w_value)
    stats_other = swap(stats, 0, 1)
    new_rows, d_keys, d_values, *slot_grads, cot_mine = write_back(
        info, stats, stats_other, wq, sk, sv, mem_rows, cots, cots_other, keys, values, rows
    )
    g_up, g_down, g_out, g_write, g_value, d_middle, d_own, d_away, g_gain_two, d_memory = backward(
        info, cots, d_keys, d_values, result, middle, normed_two, act, slope, o, o_other, weights,
        gains, mem_rows, slot_grads, cot_mine, rows,
    )
    d_other = swap(d_away, 0, 1)

    grads = jnp.concatenate(
        [
            g_out.reshape(devices, -1, width),
            g_up.reshape(chunks, devices, -1, width).transpose(1, 0, 2, 3).reshape(devices, -1, width),
            g_down.reshape(devices, -1, width),
            g_write.reshape(devices, -1, width),
            g_value.reshape(devices, -1, width),
        ],
        axis=1,
    ).reshape(devices // 2, 2, -1, width)
    kept = pick(grads, core, 1)
    arrived = swap(pick(grads, 1 - core, 1), 0, 1)
    summed = sum_to_chips((kept.astype(F32) + arrived.astype(F32)).astype(BF16))
    big = [summed[cuts[k] : cuts[k + 1]] for k in range(len(sizes))]
    big[1] = big[1].reshape(chunks, -1, width).transpose(1, 0, 2)

    dq, dk, dv, dks, dvs = attend_back(info, q_log, k, v, ks, vs, d_own, d_other, o)
    d_normed, g_qkv, d_slots = project_back(
        normed, dq, dk, dv, w_qkv, mem_rows, init, dks, dvs, rows
    )
    d_memory = (d_memory + d_slots[:slots]).reshape(2, 2, slot_part, width)
    d_away = jnp.concatenate(
        [
            pick(d_normed.reshape(2, 2, rows, width), 1 - core, 1),
            pick(d_memory, 1 - core, 1).astype(BF16),
        ],
        axis=1,
    )
    d_back = swap(d_away, 0, 1)
    d_tokens, g_gain_one = inputs_back(info, own, d_normed, d_back, d_middle, gains, rows)
    d_mem_mine = (pick(d_memory, core, 1) + d_back[:, rows:].astype(F32)).astype(BF16)

    g_misc = jnp.concatenate(
        [
            d_slots[slots:].reshape(devices, -1),
            jnp.concatenate([g_gain_one, g_gain_two]).reshape(devices, -1),
        ],
        axis=1,
    )
    g_misc = jnp.pad(g_misc, ((0, 0), (0, misc_rows * CORE_WIDTH - g_misc.shape[1])))
    g_small = jnp.concatenate(
        [
            g_qkv.reshape(devices // 2, 2 * own_rows, CORE_WIDTH),
            g_misc.reshape(devices // 2, 2 * misc_rows, CORE_WIDTH).astype(BF16),
        ],
        axis=1,
    )
    small = sum_to_chips(g_small)
    small_attn = small[: 2 * own_rows].reshape(2, own_rows, CORE_WIDTH)
    small_misc = small[2 * own_rows :].reshape(2, misc_rows, CORE_WIDTH)
    sent = jnp.concatenate([pick(small_attn, 1 - core), pick(small_misc, 1 - core)], axis=0)
    back = swap(sent, 0, 1)
    attn_grad = by_core(core, pick(small_attn, core), back[:own_rows], axis=1)
    misc_grad = (pick(small_misc, core) + back[own_rows:]).reshape(-1)

    def to_rank(big, small):
        mine = jnp.concatenate([pick(big, chip), pick(small, chip)], axis=0)
        away = jnp.concatenate([pick(big, 1 - chip), pick(small, 1 - chip)], axis=0)
        both = by_chip(chip, mine, swap(away, 0, 2))
        return both[:, :rows], both[:, rows:]

    new_mine = pick(new_rows.reshape(2, 2, slot_part, width), core, 1)
    output, new_memory = to_rank(result, new_mine)
    tokens_grad, memory_grad = to_rank(d_tokens, d_mem_mine)
    return (
        output,
        new_memory,
        tokens_grad,
        memory_grad,
        attn_grad.reshape(-1),
        *[part.reshape(-1) for part in big],
        misc_grad[memory_init.shape[0] :][: norm_gains.shape[0]],
        misc_grad[: memory_init.shape[0]],
    )


def solution(mesh):
    rows = P("batch", "seq", None)
    table = P("batch", None)
    flat = P(("batch", "seq"))
    return jax.shard_map(
        per_device,
        mesh=mesh,
        in_specs=(rows, rows, table, table, *[flat] * 8, rows, rows),
        out_specs=(rows, rows, rows, rows, *[flat] * 8),
        check_vma=False,
    )
```

```python
import functools
import math

import jax
import jax.numpy as jnp
from jax import lax
from jax.experimental import pallas as pl
from jax.experimental.pallas import tpu as pltpu
from jax.sharding import PartitionSpec as P

HEADS = 8
HEAD_DIM = 64
FF = 2048
SEGMENT = 512
MASKED = -1e30
LANES = 128
CORE_HEADS = HEADS // 2
CORE_WIDTH = CORE_HEADS * HEAD_DIM
SCALE = HEAD_DIM ** (-0.5)
EXP = math.log2(math.e) * SCALE
LOG2E = math.log2(math.e)
RESET_COL = 8
LOG_COL = 10
NT = (((1,), (1,)), ((), ()))
NN = (((1,), (0,)), ((), ()))
TN = (((0,), (0,)), ((), ()))
GELU_A = math.sqrt(2.0 / math.pi)
GELU_B = 0.044715
BF16 = jnp.bfloat16
F32 = jnp.float32


def dot(left, right, dims=NN):
    return lax.dot_general(left, right, dims, preferred_element_type=F32)


def streamed(kernel, name, info, arrays, outs, scratch=(), grid=(1,)):
    arrays = [a if isinstance(a, tuple) else (a, a.shape, [((), ())]) for a in arrays]
    count = sum(len(pieces) for _, _, pieces in arrays)

    def at(ref, place):
        return ref.at[place] if place else ref

    def body(info, *refs):
        n, m = len(arrays), len(outs)
        far, far_out, refs = refs[:n], refs[n : n + m], refs[n + m :]
        near, near_out, refs = refs[:n], refs[n : n + m], refs[n + m :]
        own, sems, out_sems = refs[:-2], refs[-2], refs[-1]
        step = pl.program_id(0)
        copies = []
        for k, (_, _, pieces) in enumerate(arrays):
            first = sum(map(len, copies))
            copies.append(
                [
                    pltpu.make_async_copy(at(far[k], a), at(near[k], b), sems.at[first + j])
                    for j, (a, b) in enumerate(pieces)
                ]
            )

        @pl.when(step == 0)
        def _():
            for group in copies:
                for copy in group:
                    copy.start()

        def need(k, j=0, when=0):
            pl.when(step == when)(copies[k][j].wait)

        def give(k, *place):
            pltpu.make_async_copy(
                at(near_out[k], place), at(far_out[k], place), out_sems.at[k]
            ).start()

        kernel(need, give, info, *near, *near_out, *own)

        @pl.when(step == pl.num_programs(0) - 1)
        def _():
            for k in range(m):
                pltpu.make_async_copy(near_out[k], far_out[k], out_sems.at[k]).wait()

    space = pl.BlockSpec(memory_space=pl.ANY)
    return pl.pallas_call(
        body,
        grid_spec=pltpu.PrefetchScalarGridSpec(
            num_scalar_prefetch=1,
            grid=grid,
            in_specs=[space] * len(arrays),
            out_specs=[space] * len(outs),
            scratch_shapes=[
                *[pltpu.VMEM(shape, array.dtype) for array, shape, _ in arrays],
                *[pltpu.VMEM(shape, kind) for shape, kind in outs],
                *scratch,
                pltpu.SemaphoreType.DMA((count,)),
                pltpu.SemaphoreType.DMA((len(outs),)),
            ],
        ),
        out_shape=[jax.ShapeDtypeStruct(shape, kind) for shape, kind in outs],
        compiler_params=pltpu.CompilerParams(vmem_limit_bytes=58 << 20),
        name=name,
    )(info, *[array for array, _, _ in arrays])


def norm_parts(values):
    centred = values - jnp.mean(values, axis=-1, keepdims=True)
    scale = lax.rsqrt(jnp.mean(centred * centred, axis=-1, keepdims=True) + 1e-05)
    return centred * scale, scale


def norm_back(unit, scale, grad, gain):
    back = grad * gain
    return scale * (
        back
        - jnp.mean(back, axis=-1, keepdims=True)
        - unit * jnp.mean(back * unit, axis=-1, keepdims=True)
    )


def in_three(values):
    high = values.astype(BF16).astype(F32)
    rest = values - high
    middle = rest.astype(BF16).astype(F32)
    return high, middle, rest - middle


def put_log(column, values, others):
    high, middle, low = in_three(values)
    out = jnp.where(column == LOG_COL, high, others)
    out = jnp.where(column == LOG_COL + 1, middle, out)
    return jnp.where(column == LOG_COL + 2, low, out)


def aux_column(shape, parity):
    lane = lax.broadcasted_iota(jnp.int32, shape, 1)
    return lane - (1 - parity) * HEAD_DIM


OWNERS = 32
OUT, VALUE, WRITE, UP, DOWN = range(5)
FIELDS = (16, 16, 32, 64, 64)
CUTS = tuple(sum(FIELDS[:k]) for k in range(len(FIELDS) + 1))
PACKED = CUTS[-1]
CHUNKS = 4
PART = FIELDS[UP] // CHUNKS


def flat_rows(block):
    return block.reshape(-1, block.shape[-1])


def take(packed, field):
    return flat_rows(packed[:, CUTS[field] : CUTS[field + 1], :])


def take_up(packed, chunk):
    if isinstance(chunk, int):
        at = CUTS[UP] + chunk * PART
    else:
        at = pl.multiple_of(CUTS[UP] + chunk * PART, PART)
    return flat_rows(packed[:, pl.ds(at, PART), :])


def take_down(packed, chunk):
    count = OWNERS // CHUNKS
    return flat_rows(packed[pl.ds(chunk * count, count), CUTS[DOWN] : CUTS[DOWN + 1], :])


def put(core, kept, away, value, owner, owners, at, rows):
    split = value.reshape(owners // 2, 2, rows, value.shape[-1])
    place = (pl.ds(owner, owners // 2), pl.ds(at, rows), slice(None))
    kept[place] = jnp.where(core == 0, split[:, 0], split[:, 1]).astype(BF16)
    away[place] = jnp.where(core == 0, split[:, 1], split[:, 0]).astype(BF16)


def by_head(out, place, pair, mine, side):
    lane = lax.broadcasted_iota(jnp.int32, mine.shape, 1)
    out[2 * pair, place, :] = jnp.where(lane < HEAD_DIM, mine, side).astype(BF16)
    out[2 * pair + 1, place, :] = jnp.where(lane < HEAD_DIM, side, mine).astype(BF16)


def choose(rank, core, chip, mine, recv, mine_other, recv_other):
    here = jnp.where(rank // 2 == chip, mine, recv)
    there = jnp.where(rank // 2 == chip, mine_other, recv_other)
    return jnp.where(rank % 2 == core, here, there)


def qkv_weight(packed, which):
    pairs = packed.shape[0]
    width = 2 * CORE_WIDTH
    rows = 3 * width // pairs
    if width % rows == 0:
        return flat_rows(packed[which * width // rows : (which + 1) * width // rows, :rows, :])
    return flat_rows(packed[:, :rows, :])[which * width : (which + 1) * width]


def project_step(
    need, give, info, rank, packed, init, gain, sources,
    q_out, k_out, v_out, normed_out, ks_out, vs_out, rows_out, tokens_out, scale_out, w_ref,
):
    core, chip = info[0], info[1]
    rows = normed_out.shape[0] // 4
    shape = (rows, LANES)
    column = lax.broadcasted_iota(jnp.int32, (1, LANES), 1) % HEAD_DIM

    @pl.when(rank == 0)
    def _():
        need(0)
        for which in range(3):
            w_ref[which] = qkv_weight(packed, which)
        for k in range(1, 7):
            need(k)
        slots = rows_out.shape[0]
        part = slots // 4
        for k in range(4):
            rows_out[k * part : (k + 1) * part, :] = choose(
                k, core, chip, *[ref[rows:, :] for ref in sources]
            )
        source = jnp.concatenate([rows_out[...], init[...]], axis=0)
        shape = (2 * slots, LANES)
        start = (lax.broadcasted_iota(jnp.int32, shape, 0) >= slots).astype(jnp.int32)
        ones = jnp.where((column >= LOG_COL) & (column < LOG_COL + 3), 1.0, 0.0)
        side = jnp.where(column == RESET_COL + start, MASKED, ones)
        keys = dot(source, w_ref[1])
        values = dot(source, w_ref[2])
        whole = slice(0, 2 * slots)
        for pair in range(CORE_HEADS // 2):
            lanes = slice(pair * LANES, (pair + 1) * LANES)
            by_head(ks_out, whole, pair, keys[:, lanes], side)
            by_head(vs_out, whole, pair, values[:, lanes], jnp.ones(shape, F32))
        for k in (KS, VS, ROWS):
            give(k)

    values = choose(rank, core, chip, *[ref[:rows, :] for ref in sources])

    @pl.when(rank % 2 == core)
    def _():
        tokens_out[rank // 2] = values
        give(TOKENS, rank // 2)

    unit, scale = norm_parts(values.astype(F32))
    normed = (unit * gain[0:1, :].astype(F32)).astype(BF16)
    place = pl.ds(pl.multiple_of(rank * rows, rows), rows)
    normed_out[place, :] = normed
    give(NORMED, place)
    scale_out[place, :] = jnp.broadcast_to(scale, (rows, LANES))
    give(SCALES, place)
    low = jnp.zeros((1, LANES), jnp.int32)
    high = jnp.zeros((1, LANES), jnp.int32)
    for k in range(8):
        low = jnp.where(column == k, info[1 + k] if k else 0, low)
        high = jnp.where(column == k, info[2 + k], high)
    reset = info[10 + (rank * rows) // SEGMENT]
    position = rank * rows + lax.broadcasted_iota(jnp.int32, shape, 0)
    here = (position >= low) & (position < high)
    fixed = jnp.where(column == RESET_COL + 1 - reset, 1.0, 0.0)
    q_side = jnp.where(here, 1.0, jnp.broadcast_to(fixed, shape))
    ones = jnp.where((column >= LOG_COL) & (column < LOG_COL + 3), 1.0, 0.0)
    others = jnp.where(column < 8, MASKED, ones)
    k_side = jnp.where(here, 0.0, jnp.broadcast_to(others, shape))
    for which, out, side in ((0, q_out, q_side), (1, k_out, k_side), (2, v_out, jnp.ones(shape, F32))):
        result = dot(normed, w_ref[which])
        for pair in range(CORE_HEADS // 2):
            by_head(out, place, pair, result[:, pair * LANES : (pair + 1) * LANES], side)


    @pl.when(rank == 3)
    def _():
        give(K)
        give(V)


Q_LOG, K, V, KS, VS, NORMED, TOKENS, ROWS, O, O_AWAY, SCALES = range(11)


def attend_step(block, give, info, head, q_ref, k_ref, v_ref, ks_ref, vs_ref, q_out, o_ref, away):
    core = info[0]
    length = q_ref.shape[1]
    rows = away.shape[2]
    pair, parity = head // 2, head % 2
    column = aux_column((block, LANES), parity)
    keep = (column < 0) | (column >= HEAD_DIM)
    row = lax.broadcasted_iota(jnp.int32, (block, block), 0)
    key = lax.broadcasted_iota(jnp.int32, (block, block), 1)
    for i in range(length // block):
        low, high = i * block, (i + 1) * block
        q = q_ref[head, low:high, :]
        slot = dot(q, ks_ref[head], NT)
        scores = dot(q, k_ref[head, :high, :], NT)
        last = jnp.where(row >= key, scores[:, low:], MASKED)
        scores = jnp.concatenate([scores[:, :low], last], axis=1) if i else last
        top = jnp.maximum(
            jnp.max(scores, axis=1, keepdims=True), jnp.max(slot, axis=1, keepdims=True)
        )
        share = jnp.exp2((scores - top) * EXP).astype(BF16)
        slot_share = jnp.exp2((slot - top) * EXP).astype(BF16)
        total = dot(share, v_ref[head, :high, :]) + dot(slot_share, vs_ref[head])
        count = jnp.where(parity == 0, total[:, HEAD_DIM : HEAD_DIM + 1], total[:, 0:1])
        o_ref[pair, low:high, :] = jnp.where(
            keep, (total / count).astype(BF16), o_ref[pair, low:high, :]
        )
        log = top + jnp.log2(count) * (1.0 / EXP)
        q_out[head, low:high, :] = put_log(column, -log, q.astype(F32)).astype(BF16)
    give(Q_LOG, head)

    @pl.when(parity == 1)
    def _():
        for rank in range(4):

            @pl.when(core != rank % 2)
            def _():
                away[rank // 2, pair] = o_ref[pair, rank * rows : (rank + 1) * rows, :]

        give(O, pair)
        give(O_AWAY, slice(None), pair)


def read_kernel(
    need, give, info, packed, init, gain, mine, recv, mine_other, recv_other,
    q_log, k, v, ks, vs, normed, tokens, rows, o, o_away, scales, q, w_ref,
):
    step = pl.program_id(0)

    @pl.when(step < 4)
    def _():
        project_step(
            need, give, info, step, packed, init, gain, (mine, recv, mine_other, recv_other),
            q, k, v, normed, ks, vs, rows, tokens, scales, w_ref,
        )

    @pl.when(step >= 4)
    def _():
        attend_step(256, give, info, step - 4, q, k, v, ks, vs, q_log, o, o_away)


def read(info, sources, packed, init, gains, rows):
    total, width = sources[0].shape
    slots = 4 * (total - rows)
    length = 4 * rows
    heads = ((CORE_HEADS, length, LANES), BF16)
    slot = ((CORE_HEADS, 2 * slots, LANES), BF16)
    return streamed(
        read_kernel, "read", info, (packed, init, gains, *sources),
        (heads, heads, heads, slot, slot, ((length, width), BF16), ((2, rows, width), BF16),
         ((slots, width), BF16), ((2, length, LANES), BF16), ((2, 2, rows, LANES), BF16), ((length, LANES), F32)),
        [pltpu.VMEM((CORE_HEADS, length, LANES), BF16), pltpu.VMEM((3, width, CORE_WIDTH), BF16)],
        grid=(4 + CORE_HEADS,),
    )


def attend_back_kernel(
    kb, qb, first_head, info, q_ref, k_ref, v_ref, ks_ref, vs_ref, own_ref, other_ref, o_ref,
    dq_ref, dk_ref, dv_ref, dks_ref, dvs_ref, d_ref, acc_ref,
):
    length = q_ref.shape[1]
    step = pl.program_id(0)
    head = first_head + step
    pair, parity = head // 2, head % 2
    core = info[0]
    rows = own_ref.shape[2]
    column = aux_column((rows, LANES), parity)
    inside = (column < 0) | (column >= HEAD_DIM)
    for r in range(length // rows):
        low, high = r * rows, (r + 1) * rows
        d = jnp.where(core == r % 2, own_ref[r // 2, pair], other_ref[r // 2, pair]).astype(F32)
        delta = jnp.sum(
            jnp.where(inside, d * o_ref[pair, low:high, :].astype(F32), 0.0), axis=1, keepdims=True
        )
        d_ref[low:high, :] = jnp.where(
            inside, d, put_log(column, -delta, jnp.zeros_like(d))
        ).astype(BF16)
    acc_ref[...] = jnp.zeros_like(acc_ref)

    count = ks_ref.shape[1]
    pieces = [(ks_ref, vs_ref, dks_ref, dvs_ref, 0, count, None)]
    pieces += [(k_ref, v_ref, dk_ref, dv_ref, j, j + kb, j) for j in range(0, length, kb)]
    for keys, values, dk_out, dv_out, start, stop, first in pieces:
        k = keys[step, start:stop, :]
        v = values[step, start:stop, :]
        turned = k.astype(F32).T.astype(BF16)
        dk = jnp.zeros((stop - start, LANES), F32)
        dv = jnp.zeros((stop - start, LANES), F32)
        low = first or 0
        while low < length:
            high = min((low // qb + 1) * qb, length)
            q = q_ref[step, low:high, :]
            d = d_ref[low:high, :]
            scores = dot(k, q, NT)
            share = jnp.exp2(scores * EXP)
            if first is not None and low < stop:
                key = first + lax.broadcasted_iota(jnp.int32, scores.shape, 0)
                position = low + lax.broadcasted_iota(jnp.int32, scores.shape, 1)
                share = jnp.where(key <= position, share, 0.0)
            ds = (share * dot(v, d, NT)).astype(BF16)
            dv = dv + dot(share.astype(BF16), d)
            dk = dk + dot(ds, q)
            acc_ref[:, low:high] += dot(turned, ds)
            low = high
        dk_out[step, start:stop, :] = (dk * SCALE).astype(BF16)
        dv_out[step, start:stop, :] = dv.astype(BF16)
    dq_ref[step] = (acc_ref[...].T * SCALE).astype(BF16)


def of_heads(array, first, heads):
    shape = (heads, *array.shape[1:])
    return array, shape, [((first + j,), (j,)) for j in range(heads)]


def some_heads_kernel(first, need, give, info, *refs):
    step = pl.program_id(0)
    for k in (5, 6, 7):
        need(k)
    for k in range(5):
        for j in range(refs[k].shape[0]):
            need(k, j, j)
    attend_back_kernel(256, 1024, first, info, *refs)
    for k in range(5):
        give(k, step)


def attend_back(info, first, heads, q, k, v, ks, vs, own, other, o):
    _, length, _ = q.shape
    out = ((heads, length, LANES), BF16)
    slot_out = ((heads, ks.shape[1], LANES), BF16)
    arrays = [of_heads(array, first, heads) for array in (q, k, v, ks, vs)]
    return streamed(
        functools.partial(some_heads_kernel, first), "attend_back", info,
        (*arrays, own, other, o), (out, out, out, slot_out, slot_out),
        [pltpu.VMEM((length, LANES), BF16), pltpu.VMEM((LANES, length), F32)], grid=(heads,),
    )


def side_by_side(tiles):
    return jnp.concatenate(tiles, axis=1)


MIDDLE, NORMED_TWO, ACT, SLOPE, RESULT, KEYS, VALUES, AWAY, WQ, SK, SV, STATS = range(12)


def forward_kernel(
    need, give, info, own, other, tokens_ref, gains, packed, memory,
    middle_out, normed_out, act_out, slope_out, result_out, keys_out, values_out, away_out,
    query_out, key_out, value_out, stats,
):
    core, chip = info[0], info[1]
    half = CORE_WIDTH // FIELDS[OUT]
    for k in range(4):
        need(k)
    need(4, OUT)
    w_own = flat_rows(packed[pl.ds(core * half, half), : FIELDS[OUT], :])
    w_other = flat_rows(packed[pl.ds((1 - core) * half, half), : FIELDS[OUT], :])
    step = pl.program_id(0)
    rows = normed_out.shape[1]
    block = 2 * rows // pl.num_programs(0)
    which, at = step // (rows // block), pl.multiple_of(step % (rows // block) * block, block)
    place = (which, pl.ds(at, block))
    tokens = tokens_ref[place]
    start = pl.multiple_of((2 * which + core) * rows + at, block)
    o_own = side_by_side([own[pair, pl.ds(start, block), :] for pair in range(2)])
    o_other = side_by_side([other[which, pair, pl.ds(at, block), :] for pair in range(2)])
    middle = tokens.astype(F32) + (dot(o_own, w_own) + dot(o_other, w_other))
    middle_out[place] = middle
    unit, _ = norm_parts(middle)
    normed = (unit * gains[1:2, :].astype(F32)).astype(BF16)
    normed_out[place] = normed
    width = normed.shape[1]
    need(4, UP)
    for k in range(CHUNKS):
        pre = dot(normed, take_up(packed, k))
        square = pre * pre
        half = 0.5 + 0.5 * jnp.tanh(pre * (GELU_A + (GELU_A * GELU_B) * square))
        turn = (half - half * half) * (2.0 * GELU_A + (6.0 * GELU_A * GELU_B) * square)
        act_out[(k, *place)] = (pre * half).astype(BF16)
        slope_out[(k, *place)] = (half + pre * turn).astype(BF16)
    acts = side_by_side([act_out[(k, *place)] for k in range(CHUNKS)])
    need(4, DOWN)
    low = (middle + dot(acts, take(packed, DOWN))).astype(BF16)
    result_out[place] = low

    @pl.when(which != chip)
    def _():
        away_out[pl.ds(at, block), :] = low
        give(AWAY, pl.ds(at, block))

    need(4, WRITE)
    need(4, VALUE)
    need(5)
    keys_out[place] = dot(low, flat_rows(packed[OWNERS // 2 :, CUTS[WRITE] : CUTS[WRITE + 1], :])).astype(BF16)
    values_out[place] = dot(low, take(packed, VALUE)).astype(BF16)


    for k in (MIDDLE, NORMED_TWO, RESULT, KEYS, VALUES):
        give(k, *place)
    for k in (ACT, SLOPE):
        give(k, slice(None), *place)

    @pl.when(step == pl.num_programs(0) - 1)
    def _():
        write_step(keys_out, values_out, memory, packed, query_out, key_out, value_out, stats)
        for k in (WQ, SK, SV, STATS):
            give(k)


def fields_of(packed):
    pieces = [(slice(None), slice(CUTS[k], CUTS[k + 1])) for k in range(len(FIELDS))]
    return packed, packed.shape, [(piece, piece) for piece in pieces]


def forward(info, tokens, o, other, packed, gains, memory):
    _, rows, width = tokens.shape
    slots = memory.shape[0]
    small = ((2, rows, width), BF16)
    wide = ((CHUNKS, 2, rows, FF // CHUNKS), BF16)
    slot = ((slots, width), BF16)
    return streamed(
        forward_kernel, "feed_forward", info, (o, other, tokens, gains, fields_of(packed), memory),
        (((2, rows, width), F32), small, wide, wide, small, small, small, ((rows, width), BF16),
         slot, slot, slot, ((3, slots, width), F32)),
        grid=(4,),
    )


KEPT, SENT, D_MIDDLE, D_OWN, D_OTHER, G_GAIN, D_MEMORY, NEW_ROWS = range(8)


def backward_kernel(
    need, give, info, stats, stats_other, query, key, value, rows_ref, cot_mine, cot_recv,
    cot_other, keys, values, packed, result, normed, act, slope, middle, own, other, gains,
    kept, away, d_middle_out, d_own, d_other, g_gain, d_memory, new_out,
    d_keys, d_values, d_query, d_self_key, d_self_value, mem_cot,
    d_result_ref, d_update_ref, d_normed_ref,
):
    step = pl.program_id(0)
    core, chip = info[0], info[1]
    count, rows, width = result.shape
    total = count * rows
    half = CORE_WIDTH // FIELDS[OUT]

    @pl.when(step == 0)
    def _():
        for k in range(11):
            need(k)
        write_back_step(
            info, stats, stats_other, query, key, value, rows_ref, cot_mine, cot_recv, cot_other,
            keys, values, new_out, d_keys, d_values, d_query, d_self_key, d_self_value, mem_cot,
        )
        give(NEW_ROWS)
        need(11, WRITE)
        need(11, VALUE)
        need(12)

    @pl.when(step == 0)
    def _():
        dk = d_keys[...].reshape(total, width)
        dv = d_values[...].reshape(total, width)
        w_query = flat_rows(packed[: OWNERS // 2, CUTS[WRITE] : CUTS[WRITE + 1], :])
        w_key = flat_rows(packed[OWNERS // 2 :, CUTS[WRITE] : CUTS[WRITE + 1], :])
        w_value = take(packed, VALUE)
        first, second = cot_mine[:rows, :].astype(F32), cot_recv[:rows, :].astype(F32)
        cot = jnp.concatenate(
            [jnp.where(chip == 0, first, second), jnp.where(chip == 0, second, first)], axis=0
        )
        d_result = cot + (dot(dk, w_key, NT) + dot(dv, w_value, NT))
        d_result_ref[...] = d_result
        d_update_ref[...] = d_result.astype(BF16)
        d_normed_ref[...] = jnp.zeros_like(d_normed_ref)
        out = result[...].reshape(total, width)
        memory = rows_ref[...]
        put(core, kept, away, dot(memory, d_query[...], TN), 0, OWNERS // 2, CUTS[WRITE], FIELDS[WRITE])
        put(
            core, kept, away, dot(out, dk, TN) + dot(memory, d_self_key[...], TN),
            OWNERS // 4, OWNERS // 2, CUTS[WRITE], FIELDS[WRITE],
        )
        put(
            core, kept, away, dot(out, dv, TN) + dot(memory, d_self_value[...], TN),
            0, OWNERS, CUTS[VALUE], FIELDS[VALUE],
        )
        d_memory[...] = mem_cot[...] + (
            dot(d_query[...], w_query, NT)
            + dot(d_self_key[...], w_key, NT)
            + dot(d_self_value[...], w_value, NT)
        )
        give(D_MEMORY)
        need(11, DOWN)
        need(11, UP)
        need(13)

    for j in range(CHUNKS):
        need(14, j, j)
        need(15, j, j)
    d_update = d_update_ref[...]
    d_act = dot(d_update, take_down(packed, step), NT)
    d_hidden = (d_act * slope[step].reshape(total, -1).astype(F32)).astype(BF16)
    g_down = dot(act[step].reshape(total, -1), d_update, TN)
    owners = OWNERS // CHUNKS
    put(core, kept, away, g_down, step * (owners // 2), owners, CUTS[DOWN], FIELDS[DOWN])
    g_up = dot(normed[...].reshape(total, width), d_hidden, TN)
    at = pl.multiple_of(CUTS[UP] + step * PART, PART)
    put(core, kept, away, g_up, 0, OWNERS, at, PART)
    d_normed_ref[...] += dot(d_hidden, take_up(packed, step), NT)

    @pl.when(step == pl.num_programs(0) - 1)
    def _():
        for k in (16, 17, 18, 19):
            need(k, 0, CHUNKS - 1)
        need(11, OUT, CHUNKS - 1)
        gain = gains[1:2, :].astype(F32)
        unit, scale = norm_parts(middle[...].reshape(total, width))
        d_normed = d_normed_ref[...]
        g_gain[...] = jnp.sum(d_normed * unit, axis=0, keepdims=True)
        d_middle = d_result_ref[...] + norm_back(unit, scale, d_normed, gain)
        d_middle_out[...] = d_middle.reshape(count, rows, width)
        give(D_MIDDLE)
        give(G_GAIN)
        d_branch = d_middle.astype(BF16)
        for start, out in ((core * half, d_own), ((1 - core) * half, d_other)):
            weight = flat_rows(packed[pl.ds(start, half), : FIELDS[OUT], :])
            back = dot(d_branch, weight, NT).astype(BF16)
            for k in range(count):
                for pair in range(2):
                    lanes = slice(pair * LANES, (pair + 1) * LANES)
                    out[k, pair] = back[k * rows : (k + 1) * rows, lanes]
        give(D_OWN)
        give(D_OTHER)
        own_rows = jnp.concatenate(
            [
                side_by_side(
                    [
                        own[pair, pl.ds(pl.multiple_of((2 * k + core) * rows, rows), rows), :]
                        for pair in range(2)
                    ]
                )
                for k in range(count)
            ],
            axis=0,
        )
        other_rows = jnp.concatenate([side_by_side([other[k, 0], other[k, 1]]) for k in range(count)], axis=0)
        g_own = dot(own_rows, d_branch, TN)
        g_other = dot(other_rows, d_branch, TN)
        put(core, kept, away, g_own, core * (half // 2), half, 0, FIELDS[OUT])
        put(core, kept, away, g_other, (1 - core) * (half // 2), half, 0, FIELDS[OUT])
        give(SENT)
        give(KEPT)


def by_chunk(array):
    return array, array.shape, [((j,), (j,)) for j in range(CHUNKS)]


def backward(info, stats, stats_other, writer, memory, cots, cot_other, keys, values, packed,
             result, normed, act, slope, middle, o, other, gains):
    _, rows, width = result.shape
    slots = memory.shape[0]
    grads = ((OWNERS // 2, PACKED, width), BF16)
    half = ((2, 2, rows, LANES), BF16)
    slot = pltpu.VMEM((slots, width), BF16)
    return streamed(
        backward_kernel, "feed_forward_back", info,
        (stats, stats_other, *writer, memory, *cots, cot_other, keys, values, fields_of(packed),
         result, normed, by_chunk(act), by_chunk(slope), middle, o, other, gains),
        (grads, grads, ((2, rows, width), F32), half, half, ((1, width), F32),
         ((slots, width), F32), ((slots, width), BF16)),
        [pltpu.VMEM((2, rows, width), BF16), pltpu.VMEM((2, rows, width), BF16), slot, slot, slot,
         pltpu.VMEM((slots, width), F32),
         pltpu.VMEM((2 * rows, width), F32), pltpu.VMEM((2 * rows, width), BF16),
         pltpu.VMEM((2 * rows, width), F32)],
        grid=(CHUNKS,),
    )


def head_mask(shape, head):
    lane = lax.broadcasted_iota(jnp.int32, shape, 1)
    return (lane >= head * HEAD_DIM) & (lane < (head + 1) * HEAD_DIM)


def stacked_heads(values):
    return jnp.concatenate(
        [jnp.where(head_mask(values.shape, h), values, 0.0) for h in range(HEADS)], axis=0
    )


def joined_heads(stacked, slots):
    out = None
    for h in range(HEADS):
        part = stacked[h * slots : (h + 1) * slots, :]
        shape = (slots, HEADS * HEAD_DIM)
        part = jnp.broadcast_to(part, shape)
        out = part if out is None else jnp.where(head_mask(shape, h), part, out)
    return out


def column_of_heads(values):
    return jnp.concatenate(
        [values[:, h * HEAD_DIM : h * HEAD_DIM + 1] for h in range(HEADS)], axis=0
    )


def head_sums(values):
    return jnp.concatenate(
        [
            jnp.sum(jnp.where(head_mask(values.shape, h), values, 0.0), axis=1, keepdims=True)
            for h in range(HEADS)
        ],
        axis=0,
    )


def write_step(keys, values, memory, packed, query_out, key_out, value_out, stats):
    slots = memory.shape[0]
    total = keys.shape[0] * keys.shape[1]
    rows = memory[...]
    w_write = take(packed, WRITE)
    query = dot(rows, w_write[: w_write.shape[0] // 2]).astype(BF16)
    query_out[...] = query
    key_out[...] = dot(rows, w_write[w_write.shape[0] // 2 :]).astype(BF16)
    value_out[...] = dot(rows, take(packed, VALUE)).astype(BF16)
    stacked = stacked_heads(query.astype(F32)).astype(BF16)
    scores = dot(stacked, keys[...].reshape(total, -1), NT)
    top = jnp.max(scores, axis=1, keepdims=True)
    share = jnp.exp2((scores - top) * EXP)
    stats[0] = joined_heads(top, slots)
    stats[1] = joined_heads(jnp.sum(share, axis=1, keepdims=True), slots)
    stats[2] = joined_heads(dot(share.astype(BF16), values[...].reshape(total, -1)), slots)


def write_back_step(
    info, own, other, query, key, value, memory, cot_mine, cot_recv, cot_other, keys, values,
    new_out, d_keys, d_values, d_query, d_key, d_value, cot_out,
):
    core, chip = info[0], info[1]
    slots, width = memory.shape
    part = slots // 4
    rows = keys.shape[1]
    total = keys.shape[0] * rows
    sources = (cot_mine[rows:, :], cot_recv[rows:, :], cot_other[:part, :], cot_other[part:, :])
    cot = jnp.concatenate([choose(k, core, chip, *sources) for k in range(4)], axis=0).astype(F32)
    q = query[...].astype(F32)
    sk = key[...].astype(F32)
    sv = value[...].astype(F32)
    self_column = head_sums(q * sk)
    self_scores = joined_heads(self_column, slots)
    top = jnp.maximum(jnp.maximum(own[0], other[0]), self_scores)
    own_share = jnp.exp2((own[0] - top) * EXP)
    other_share = jnp.exp2((other[0] - top) * EXP)
    self_share = jnp.exp2((self_scores - top) * EXP)
    count = own[1] * own_share + other[1] * other_share + self_share
    written = (
        own[2] * own_share + other[2] * other_share + self_share.astype(BF16).astype(F32) * sv
    ) / count
    new_out[...] = (memory[...].astype(F32) + written).astype(BF16)
    log = top + jnp.log2(count) * (1.0 / EXP)
    log_column = column_of_heads(log)
    delta_column = head_sums(cot * written)
    delta = joined_heads(delta_column, slots)
    stacked = stacked_heads(q).astype(BF16)
    stacked_cot = stacked_heads(cot).astype(BF16)
    flat_keys = keys[...].reshape(total, width)
    share = jnp.exp2((dot(stacked, flat_keys, NT) - log_column) * EXP)
    d_share = dot(stacked_cot, values[...].reshape(total, width), NT)
    d_scores = (share * (d_share - delta_column)).astype(BF16)
    d_values[...] = dot(share.astype(BF16), stacked_cot, TN).astype(BF16).reshape(d_values.shape)
    d_keys[...] = (dot(d_scores, stacked, TN) * SCALE).astype(BF16).reshape(d_keys.shape)
    d_query_part = joined_heads(dot(d_scores, flat_keys), slots) * SCALE
    mine = (lax.broadcasted_iota(jnp.int32, (slots, width), 0) // part) % 2 == core
    self_probs = jnp.exp2((self_scores - log) * EXP)
    self_dp = joined_heads(head_sums(cot * sv), slots)
    self_ds = (self_probs * (self_dp - delta)).astype(BF16).astype(F32) * SCALE
    self_ds = jnp.where(mine, self_ds, 0.0)
    d_query[...] = (d_query_part + self_ds * sk).astype(BF16)
    d_key[...] = (self_ds * q).astype(BF16)
    d_value[...] = jnp.where(mine, self_probs.astype(BF16).astype(F32) * cot, 0.0).astype(BF16)
    cot_out[...] = jnp.where(mine, cot, 0.0)


def merged_heads(heads, place):
    tiles = [ref[k, place, :] for ref in heads for k in range(ref.shape[0])]
    lane = lax.broadcasted_iota(jnp.int32, tiles[0].shape, 1)
    return side_by_side(
        [jnp.where(lane < HEAD_DIM, tiles[2 * p], tiles[2 * p + 1]) for p in range(len(tiles) // 2)]
    )


def inputs_back_step(
    info, dq_parts, dk_parts, dv_parts, packed, normed, scales, gain, d_middle,
    mine_out, away_out, g_gain, merged,
):
    core = info[0]
    rows = mine_out.shape[1]
    weights = [qkv_weight(packed, k) for k in range(3)]
    gain = gain[0:1, :].astype(F32)
    gain_sum = None
    for rank in range(4):
        place = pl.ds(rank * rows, rows)
        total = None
        for k, parts in enumerate((dq_parts, dk_parts, dv_parts)):
            grads = merged_heads(parts, place)
            merged[k, place, :] = grads
            term = dot(grads, weights[k], NT)
            total = term if total is None else total + term
        unit = normed[place, :].astype(F32) * (1.0 / gain)
        part = jnp.sum(total * unit, axis=0, keepdims=True)
        gain_sum = part if gain_sum is None else gain_sum + part
        back = norm_back(unit, scales[place, 0:1], total, gain)

        @pl.when(core == rank % 2)
        def _():
            mine_out[rank // 2] = d_middle[rank // 2] + back

        @pl.when(core != rank % 2)
        def _():
            away_out[rank // 2] = back.astype(BF16)

    g_gain[...] = gain_sum


def weights_back_step(
    info, normed, merged, packed, memory, init, d_memory, dks_parts, dvs_parts,
    g_out, d_init, d_mine, d_away,
):
    source = jnp.concatenate([memory[...], init[...]], axis=0)
    everything = slice(0, source.shape[0])
    dks = merged_heads(dks_parts, everything)
    dvs = merged_heads(dvs_parts, everything)
    d_slots = dot(dks, qkv_weight(packed, 1), NT) + dot(dvs, qkv_weight(packed, 2), NT)
    slots = memory.shape[0]
    part = slots // 4
    d_init[...] = d_slots[slots:]
    total = d_memory[...] + d_slots[:slots]
    for k in range(2):
        even = total[2 * k * part : (2 * k + 1) * part]
        odd = total[(2 * k + 1) * part : (2 * k + 2) * part]
        d_mine[k * part : (k + 1) * part, :] = jnp.where(info[0] == 0, even, odd)
        d_away[k * part : (k + 1) * part, :] = jnp.where(info[0] == 0, odd, even)
    rows = normed[...]
    g_out[0] = dot(rows, merged[0], TN).astype(BF16)
    g_out[1] = (dot(rows, merged[1], TN) + dot(source, dks, TN)).astype(BF16)
    g_out[2] = (dot(rows, merged[2], TN) + dot(source, dvs, TN)).astype(BF16)


def last_heads_kernel(first, need, give, info, *refs):
    heads, refs = refs[:8], refs[8:]
    packed, refs = refs[0], refs[1:]
    earlier, refs = (refs[:5], refs[5:10]), refs[10:]
    normed, scales, gain, d_middle, memory, init, d_memory, refs = *refs[:7], refs[7:]
    d_mine, d_away, g_out, d_init, m_mine, m_away, g_gain, refs = *refs[:7], refs[7:]
    results, merged, scratch = refs[:5], refs[5], refs[6:]
    for k in (5, 6, 7):
        need(k)
    for k in range(5):
        for j in range(heads[k].shape[0]):
            need(k, j, j)
    attend_back_kernel(256, 1024, first, info, *heads, *results, *scratch)

    @pl.when(pl.program_id(0) == pl.num_programs(0) - 1)
    def _():
        for k in range(8, 26):
            need(k, 0, pl.num_programs(0) - 1)
        parts = [(earlier[0][k], earlier[1][k], results[k]) for k in range(5)]
        inputs_back_step(
            info, *parts[:3], packed, normed, scales, gain, d_middle, d_mine, d_away, g_gain, merged
        )
        for k in (0, 1, 6):
            give(k)
        weights_back_step(
            info, normed, merged, packed, memory, init, d_memory, *parts[3:], g_out, d_init,
            m_mine, m_away,
        )
        for k in range(2, 6):
            give(k)


def last_heads(info, first, heads, q, k, v, ks, vs, own, other, o, packed, grads_a, grads_b,
               normed, scales, gains, d_middle, memory, init, d_memory):
    length, width = normed.shape
    slots = memory.shape[0]
    arrays = [of_heads(array, first, heads) for array in (q, k, v, ks, vs)]
    part = (d_middle.shape, F32)
    away = (d_middle.shape, BF16)
    half = ((slots // 2, width), F32)
    out = pltpu.VMEM((heads, length, LANES), BF16)
    slot_out = pltpu.VMEM((heads, ks.shape[1], LANES), BF16)
    return streamed(
        functools.partial(last_heads_kernel, first), "last_heads", info,
        (*arrays, own, other, o, packed, *grads_a, *grads_b, normed, scales, gains, d_middle,
         memory, init, d_memory),
        (part, away, ((3, width, CORE_WIDTH), BF16), ((slots, width), F32), half, half,
         ((1, width), F32)),
        [out, out, out, slot_out, slot_out, pltpu.VMEM((3, length, CORE_WIDTH), BF16),
         pltpu.VMEM((length, LANES), BF16), pltpu.VMEM((LANES, length), F32)],
        grid=(heads,),
    )


def inputs_back_kernel(
    need, give, info, mine, other, mem_mine, mem_other, new_rows, d_out, away_out, mem_out
):
    core, chip = info[0], info[1]
    count, rows, _ = mine.shape
    for k in range(count):
        need(0, k)
        need(1, k)
        back = (mine[k] + other[k].astype(F32)).astype(BF16)
        d_out[k] = back
        give(0, k)

        @pl.when(chip != k)
        def _():
            away_out[:rows, :] = back

    for j in range(2, 5):
        need(j)
    part = mem_mine.shape[0] // 2
    grads = (mem_mine[...] + mem_other[...]).astype(BF16)
    news = [
        jnp.where(
            core == 0,
            new_rows[2 * k * part : (2 * k + 1) * part, :],
            new_rows[(2 * k + 1) * part : (2 * k + 2) * part, :],
        )
        for k in range(2)
    ]
    first, second = grads[:part], grads[part:]
    mem_out[:part, :] = jnp.where(chip == 0, first, second)
    mem_out[part:, :] = jnp.where(chip == 0, news[0], news[1])
    away_out[rows : rows + part, :] = jnp.where(chip == 0, second, first)
    away_out[rows + part :, :] = jnp.where(chip == 0, news[1], news[0])
    for k in (1, 2):
        give(k)


def inputs_back(info, mine, other, mem_mine, mem_other, new_rows):
    _, rows, width = mine.shape
    slots = new_rows.shape[0]
    halves = [(array, array.shape, [((j,), (j,)) for j in range(2)]) for array in (mine, other)]
    return streamed(
        inputs_back_kernel, "inputs_back", info, (*halves, mem_mine, mem_other, new_rows),
        ((mine.shape, BF16), ((rows + slots // 2, width), BF16), ((slots // 2, width), BF16)),
    )


def swap(value, over_batch, over_seq):
    batch, seq = lax.axis_size("batch"), lax.axis_size("seq")
    pairs = [
        (i * seq + j, (i ^ over_batch) * seq + (j ^ over_seq))
        for i in range(batch)
        for j in range(seq)
    ]
    return lax.ppermute(value, ("batch", "seq"), pairs)


def chip_groups():
    batch = lax.axis_index("batch")
    chip = lax.axis_index("seq") // 2
    stages = [(4, 2 * (batch & 1) + chip, lambda k: (k >> 1, 2 * (k & 1)))]
    bits = lax.axis_size("batch").bit_length() - 1
    at = 1
    while at < bits:
        count = min(2, bits - at)
        stages.append(
            (1 << count, (batch >> at) & ((1 << count) - 1), lambda k, at=at: (k << at, 0))
        )
        at += count
    return stages


def in_order(pieces, own):
    bit = 1
    while bit < len(pieces):
        turned = (own & bit) > 0
        pieces = [jnp.where(turned, pieces[k ^ bit], pieces[k]) for k in range(len(pieces))]
        bit *= 2
    return jnp.stack(pieces)


def gather_chips(piece):
    stages = chip_groups()
    shape = piece.shape
    for size, own, peer in reversed(stages):
        piece = in_order([piece] + [swap(piece, *peer(k)) for k in range(1, size)], own)
    count = len(stages)
    piece = piece.transpose(*reversed(range(count)), *range(count, piece.ndim))
    return piece.reshape(-1, *shape)


def spread(pieces, stage):
    size, own, _ = stage
    pieces = pieces.reshape(-1, size, *pieces.shape[-2:])
    return [lax.dynamic_index_in_dim(pieces, own ^ j, 1, keepdims=False) for j in range(size)]


def sent(parts, stage):
    size, _, peer = stage
    return [parts[0]] + [swap(parts[j], *peer(j)) for j in range(1, size)]


def added(parts, kind):
    total = parts[0].astype(F32)
    for part in parts[1:]:
        total = total + part.astype(F32)
    return total.astype(kind)


def split_half(pieces, index):
    return tuple(lax.dynamic_index_in_dim(pieces, k, -3, keepdims=False) for k in (index, 1 - index))


def split_square(pieces, chip):
    half = pieces.shape[1] // 2
    pieces = pieces.reshape(-1, 2, 2, *pieces.shape[1:])
    over_x = split_half(pieces[:, :, :, :half], chip)
    turned = pieces[:, :, :, half:].swapaxes(1, 2)
    return over_x, split_half(turned, lax.axis_index("batch") & 1)


def after(values, *others):
    return lax.optimization_barrier((values, others))[0]


def by_core(core, mine, other, axis=0):
    return jnp.where(
        core == 0,
        jnp.concatenate([mine, other], axis=axis),
        jnp.concatenate([other, mine], axis=axis),
    )


def by_chip(chip, mine, other):
    return jnp.where(chip == 0, jnp.stack([mine, other]), jnp.stack([other, mine]))


def pick(array, index, axis=0):
    return lax.dynamic_index_in_dim(array, index, axis, keepdims=False)


def to_owners(fields, devices):
    many = devices // OWNERS
    out = []
    for k, field in enumerate(fields):
        if many > 1:
            groups = CHUNKS if k == UP else 1
            field = field.reshape(OWNERS, many, groups, -1, field.shape[-1])
            field = field.transpose(0, 2, 1, 3, 4).reshape(OWNERS, -1, field.shape[-1])
        out.append(field)
    return jnp.concatenate(out, axis=1)


def from_owners(packed, devices):
    many = devices // OWNERS
    out = []
    for k in range(len(FIELDS)):
        field = packed[:, CUTS[k] : CUTS[k + 1]]
        groups = CHUNKS if k == UP else 1
        field = field.reshape(OWNERS, groups, many, -1, field.shape[-1])
        out.append(field.transpose(0, 2, 1, 3, 4).reshape(devices, -1, field.shape[-1]))
    return jnp.concatenate(out, axis=1)


def per_device(
    tokens, memory, lengths, resets, attn_in, attn_out, ffn_in, ffn_out, writer_in, writer_value,
    norm_gains, memory_init, out_cotangent, memory_cotangent,
):
    _, rows, width = tokens.shape
    devices = lax.axis_size("batch") * lax.axis_size("seq")
    rank = lax.axis_index("seq")
    chip, core = rank // 2, rank % 2
    slot_part = memory.shape[1]
    slots = 4 * slot_part
    stages = chip_groups()

    ends = jnp.cumsum(pick(lengths, chip))
    info = jnp.concatenate([jnp.stack([core, chip]), ends, pick(resets, chip)]).astype(jnp.int32)

    def to_chip(big, small):
        mine = jnp.concatenate([pick(big, chip), pick(small, chip)], axis=0)
        away = jnp.concatenate([pick(big, 1 - chip), pick(small, 1 - chip)], axis=0)
        return mine, swap(away, 0, 2)

    misc = jnp.concatenate([memory_init, norm_gains])
    misc_rows = -(-misc.shape[0] // CORE_WIDTH)
    misc = jnp.pad(misc, (0, misc_rows * CORE_WIDTH - misc.shape[0])).reshape(misc_rows, CORE_WIDTH)
    attn_rows = attn_in.reshape(-1, 2, CORE_WIDTH)
    own_rows = attn_rows.shape[0]
    mine = jnp.concatenate([pick(attn_rows, core, 1), misc], axis=0)
    theirs = swap(jnp.concatenate([pick(attn_rows, 1 - core, 1), misc], axis=0), 0, 1)
    piece = jnp.concatenate(
        [
            by_core(core, mine[:own_rows], theirs[:own_rows]),
            by_core(core, mine[own_rows:], theirs[own_rows:]),
        ],
        axis=0,
    )
    gathered = gather_chips(piece)
    misc = gathered[:, 2 * own_rows :].reshape(devices, -1)
    init = misc[:, : memory_init.shape[0]].reshape(slots, width)
    gains = misc[:, memory_init.shape[0] :][:, : norm_gains.shape[0]].reshape(2, width)
    w_qkv = gathered
    if devices != OWNERS:
        w_qkv = gathered[:, : 2 * own_rows].reshape(OWNERS // 2, -1, CORE_WIDTH)

    columns = ffn_in.reshape(-1, CHUNKS, width).transpose(1, 0, 2).reshape(-1, width)
    parts = [
        attn_out.reshape(-1, width), writer_value.reshape(-1, width),
        writer_in.reshape(-1, width), columns, ffn_out.reshape(-1, width),
    ]
    sizes = [part.shape[0] for part in parts]
    cuts = [sum(sizes[:k]) for k in range(len(sizes) + 1)]
    packed = lax.all_gather(jnp.concatenate(parts, axis=0), ("batch", "seq"), axis=0)
    if devices != OWNERS:
        packed = to_owners([packed[:, cuts[k] : cuts[k + 1]] for k in range(len(sizes))], devices)

    own, recv = to_chip(tokens, memory)
    sources = (own, recv, swap(own, 0, 1), swap(recv, 0, 1))
    q_log, k, v, ks, vs, normed, own_tokens, mem_rows, o, o_away, scales = read(
        info, sources, w_qkv, init, gains, rows
    )
    out_cotangent, memory_cotangent = after((out_cotangent, memory_cotangent), recv)
    cots = to_chip(out_cotangent, memory_cotangent)
    cot_other = swap(jnp.concatenate([cot[rows:] for cot in after(cots, o)], axis=0), 0, 1)
    o_other = swap(o_away, 0, 1)
    middle, normed_two, act, slope, result, keys, values, result_away, *writer, stats = forward(
        info, own_tokens, o, o_other, packed, gains, mem_rows
    )
    came = swap(result_away, 0, 2)
    stats_other = swap(stats, 0, 1)
    kept, away, d_middle, d_own, d_away, g_gain_two, d_memory, new_rows = backward(
        info, stats, stats_other, writer, mem_rows, cots, cot_other, keys, values, packed, result,
        normed_two, act, slope, middle, o, o_other, gains,
    )
    d_other, came = after((swap(d_away, 0, 1), came), came)
    if devices != OWNERS:
        both = by_core(core, kept[:, None], away[:, None], axis=1).reshape(OWNERS, PACKED, width)
        both = from_owners(both, devices).reshape(devices // 2, 2, -1, width)
        kept, away = pick(both, core, 1), pick(both, 1 - core, 1)
    arrived = swap(after(away, d_other), 0, 1)

    heads = (q_log, k, v, ks, vs)
    grads_a = attend_back(info, 0, 1, *heads, d_own, d_other, o)
    kept, arrived = (split_square(array, chip) for array in after((kept, arrived), grads_a))
    square = [(added((a, b), BF16), added((c, d), BF16)) for (a, c), (b, d) in zip(kept, arrived)]
    d_own_b = after(d_own, square)
    moved = [swap(away, *peer) for (_, away), peer in zip(square, ((0, 2), (1, 0)))]
    grads_b = attend_back(info, 1, 2, *heads, d_own_b, d_other, o)
    moved = after(moved, grads_b)
    square = [split_half(added((own, new), BF16), index) for (own, _), new, index in zip(
        square, moved, (lax.axis_index("batch") & 1, chip))]
    moved = [swap(away, *peer) for (_, away), peer in zip(square, ((1, 0), (0, 2)))]
    grads_b = after(grads_b, [away for _, away in square])
    d_mine, d_away, g_qkv, d_init, mem_mine, mem_away, g_gain_one = last_heads(
        info, 3, 1, *heads, d_own, d_other, o, w_qkv, grads_a, grads_b, normed, scales, gains,
        d_middle, mem_rows, init, d_memory,
    )
    moved = after(moved, g_qkv)
    d_sent = swap(after(d_away, moved), 0, 1)
    m_sent = swap(after(mem_away, moved), 0, 1)

    g_misc = jnp.concatenate(
        [
            d_init.reshape(devices, -1),
            jnp.concatenate([g_gain_one, g_gain_two]).reshape(devices, -1),
        ],
        axis=1,
    )
    g_misc = jnp.pad(g_misc, ((0, 0), (0, misc_rows * CORE_WIDTH - g_misc.shape[1])))
    small = jnp.concatenate(
        [
            g_qkv.reshape(devices // 2, 2 * own_rows, CORE_WIDTH),
            g_misc.reshape(devices // 2, 2 * misc_rows, CORE_WIDTH).astype(BF16),
        ],
        axis=1,
    )
    small_parts = sent(spread(after(small, moved), stages[0]), stages[0])
    parts = [jnp.concatenate([added((own, new), BF16) for (own, _), new in zip(square, moved)], axis=1)]
    for stage in stages[1:]:
        parts = sent(spread(added(parts, BF16), stage), stage)
    d_sent = after(d_sent, parts[0])
    d_tokens, d_tokens_away, mem_out = inputs_back(info, d_mine, d_sent, mem_mine, m_sent, new_rows)
    home = swap(after(d_tokens_away, small_parts), 0, 2)
    parts, small_parts = after(parts, d_tokens), after(small_parts, d_tokens)
    for stage in stages[1:]:
        small_parts = sent(spread(added(small_parts, BF16), stage), stage)
    small_parts = after(small_parts, home)
    summed = added(parts, F32).reshape(-1, width)
    small = added(small_parts, F32).reshape(-1, CORE_WIDTH)
    big = [summed[cuts[k] : cuts[k + 1]] for k in range(len(sizes))]
    big[UP] = big[UP].reshape(CHUNKS, -1, width).transpose(1, 0, 2)
    small_attn = small[: 2 * own_rows].reshape(2, own_rows, CORE_WIDTH)
    small_misc = small[2 * own_rows :].reshape(2, misc_rows, CORE_WIDTH)
    back = swap(
        jnp.concatenate([pick(small_attn, 1 - core), pick(small_misc, 1 - core)], axis=0), 0, 1
    )
    attn_grad = by_core(core, pick(small_attn, core), back[:own_rows], axis=1)
    misc_grad = (pick(small_misc, core) + back[own_rows:]).reshape(-1)

    def at_home(both, new):
        return lax.dynamic_update_index_in_dim(both, new, 1 - chip, 0)

    mem_came = home[rows:]
    return (
        at_home(result, came),
        by_chip(chip, mem_out[slot_part:], mem_came[slot_part:]),
        at_home(d_tokens, home[:rows]),
        by_chip(chip, mem_out[:slot_part], mem_came[:slot_part]),
        attn_grad.reshape(-1),
        *[big[k].reshape(-1) for k in (OUT, UP, DOWN, WRITE, VALUE)],
        misc_grad[memory_init.shape[0] :][: norm_gains.shape[0]],
        misc_grad[: memory_init.shape[0]],
    )


def solution(mesh):
    rows = P("batch", "seq", None)
    table = P("batch", None)
    flat = P(("batch", "seq"))
    return jax.shard_map(
        per_device,
        mesh=mesh,
        in_specs=(rows, rows, table, table, *[flat] * 8, rows, rows),
        out_specs=(rows, rows, rows, rows, *[flat] * 8),
        check_vma=False,
    )
```

```python
import functools
import math

import jax
import jax.numpy as jnp
from jax import lax
from jax.experimental import pallas as pl
from jax.experimental.pallas import tpu as pltpu
from jax.sharding import PartitionSpec as P

HEADS = 8
HEAD_DIM = 64
FF = 2048
SEGMENT = 512
MASKED = -1e30
LANES = 128
CORE_HEADS = HEADS // 2
CORE_WIDTH = CORE_HEADS * HEAD_DIM
SCALE = HEAD_DIM ** (-0.5)
EXP = math.log2(math.e) * SCALE
LOG2E = math.log2(math.e)
RESET_COL = 8
LOG_COL = 10
NT = (((1,), (1,)), ((), ()))
NN = (((1,), (0,)), ((), ()))
TN = (((0,), (0,)), ((), ()))
GELU_A = math.sqrt(2.0 / math.pi)
GELU_B = 0.044715
BF16 = jnp.bfloat16
F32 = jnp.float32


def dot(left, right, dims=NN):
    return lax.dot_general(left, right, dims, preferred_element_type=F32)


def streamed(kernel, name, info, arrays, outs, scratch=(), grid=(1,), late=()):
    arrays = [a if isinstance(a, tuple) else (a, a.shape, [((), ())]) for a in arrays]
    count = sum(len(pieces) for _, _, pieces in arrays)

    def at(ref, place):
        return ref.at[place] if place else ref

    def body(info, *refs):
        n, m = len(arrays), len(outs)
        far, far_out, refs = refs[:n], refs[n : n + m], refs[n + m :]
        near, near_out, refs = refs[:n], refs[n : n + m], refs[n + m :]
        own, sems, out_sems = refs[:-2], refs[-2], refs[-1]
        step = pl.program_id(0)
        copies = []
        for k, (_, _, pieces) in enumerate(arrays):
            first = sum(map(len, copies))
            copies.append(
                [
                    pltpu.make_async_copy(at(far[k], a), at(near[k], b), sems.at[first + j])
                    for j, (a, b) in enumerate(pieces)
                ]
            )

        @pl.when(step == 0)
        def _():
            ranked = [(j + 100 * (k in late), k, j) for k in range(n) for j in range(len(copies[k]))]
            for _, k, j in sorted(ranked):
                copies[k][j].start()

        def need(k, j=0, when=0):
            if when is None:
                copies[k][j].wait()
            else:
                pl.when(step == when)(copies[k][j].wait)

        def give(k, *place):
            pltpu.make_async_copy(
                at(near_out[k], place), at(far_out[k], place), out_sems.at[k]
            ).start()

        kernel(need, give, info, *near, *near_out, *own)

        @pl.when(step == pl.num_programs(0) - 1)
        def _():
            for k in range(m):
                pltpu.make_async_copy(near_out[k], far_out[k], out_sems.at[k]).wait()

    space = pl.BlockSpec(memory_space=pl.ANY)
    return pl.pallas_call(
        body,
        grid_spec=pltpu.PrefetchScalarGridSpec(
            num_scalar_prefetch=1,
            grid=grid,
            in_specs=[space] * len(arrays),
            out_specs=[space] * len(outs),
            scratch_shapes=[
                *[pltpu.VMEM(shape, array.dtype) for array, shape, _ in arrays],
                *[pltpu.VMEM(shape, kind) for shape, kind in outs],
                *scratch,
                pltpu.SemaphoreType.DMA((count,)),
                pltpu.SemaphoreType.DMA((len(outs),)),
            ],
        ),
        out_shape=[jax.ShapeDtypeStruct(shape, kind) for shape, kind in outs],
        compiler_params=pltpu.CompilerParams(vmem_limit_bytes=58 << 20),
        name=name,
    )(info, *[array for array, _, _ in arrays])


def norm_parts(values):
    centred = values - jnp.mean(values, axis=-1, keepdims=True)
    scale = lax.rsqrt(jnp.mean(centred * centred, axis=-1, keepdims=True) + 1e-05)
    return centred * scale, scale


def norm_back(unit, scale, grad, gain):
    back = grad * gain
    return scale * (
        back
        - jnp.mean(back, axis=-1, keepdims=True)
        - unit * jnp.mean(back * unit, axis=-1, keepdims=True)
    )


def in_three(values):
    high = values.astype(BF16).astype(F32)
    rest = values - high
    middle = rest.astype(BF16).astype(F32)
    return high, middle, rest - middle


def put_log(column, values, others):
    high, middle, low = in_three(values)
    out = jnp.where(column == LOG_COL, high, others)
    out = jnp.where(column == LOG_COL + 1, middle, out)
    return jnp.where(column == LOG_COL + 2, low, out)


def aux_column(shape, parity):
    lane = lax.broadcasted_iota(jnp.int32, shape, 1)
    return lane - (1 - parity) * HEAD_DIM


OWNERS = 32
OUT, VALUE, WRITE, DOWN, UP = range(5)
FIELDS = (16, 16, 32, 64, 64)
CUTS = tuple(sum(FIELDS[:k]) for k in range(len(FIELDS) + 1))
PACKED = CUTS[-1]
CHUNKS = 4
PART = FIELDS[UP] // CHUNKS


def flat_rows(block):
    return block.reshape(-1, block.shape[-1])


def take(packed, field):
    return flat_rows(packed[:, CUTS[field] : CUTS[field + 1], :])


def take_up(packed, chunk):
    if isinstance(chunk, int):
        at = CUTS[UP] + chunk * PART
    else:
        at = pl.multiple_of(CUTS[UP] + chunk * PART, PART)
    return flat_rows(packed[:, pl.ds(at, PART), :])


def take_down(packed, chunk):
    count = OWNERS // CHUNKS
    return flat_rows(packed[pl.ds(chunk * count, count), CUTS[DOWN] : CUTS[DOWN + 1], :])


def put(core, kept, away, value, owner, owners, at, rows):
    split = value.reshape(owners // 2, 2, rows, value.shape[-1])
    place = (pl.ds(owner, owners // 2), pl.ds(at, rows), slice(None))
    kept[place] = jnp.where(core == 0, split[:, 0], split[:, 1]).astype(BF16)
    away[place] = jnp.where(core == 0, split[:, 1], split[:, 0]).astype(BF16)


def by_head(out, place, pair, mine, side):
    lane = lax.broadcasted_iota(jnp.int32, mine.shape, 1)
    out[2 * pair, place, :] = jnp.where(lane < HEAD_DIM, mine, side).astype(BF16)
    out[2 * pair + 1, place, :] = jnp.where(lane < HEAD_DIM, side, mine).astype(BF16)


def choose(rank, core, chip, mine, recv, mine_other, recv_other):
    here = jnp.where(rank // 2 == chip, mine, recv)
    there = jnp.where(rank // 2 == chip, mine_other, recv_other)
    return jnp.where(rank % 2 == core, here, there)


def qkv_weight(packed, which):
    pairs = packed.shape[0]
    width = 2 * CORE_WIDTH
    rows = 3 * width // pairs
    if width % rows == 0:
        return flat_rows(packed[which * width // rows : (which + 1) * width // rows, :rows, :])
    return flat_rows(packed[:, :rows, :])[which * width : (which + 1) * width]


def project_step(
    need, give, info, rank, packed, init, gain, sources,
    q_out, k_out, v_out, normed_out, ks_out, vs_out, rows_out, tokens_out, scale_out, w_ref,
):
    core, chip = info[0], info[1]
    rows = normed_out.shape[0] // 4
    shape = (rows, LANES)
    column = lax.broadcasted_iota(jnp.int32, (1, LANES), 1) % HEAD_DIM

    @pl.when(rank == 0)
    def _():
        need(0)
        for which in range(3):
            w_ref[which] = qkv_weight(packed, which)
        for k in range(1, 7):
            need(k)
        slots = rows_out.shape[0]
        part = slots // 4
        for k in range(4):
            rows_out[k * part : (k + 1) * part, :] = choose(
                k, core, chip, *[ref[rows:, :] for ref in sources]
            )
        source = jnp.concatenate([rows_out[...], init[...]], axis=0)
        shape = (2 * slots, LANES)
        start = (lax.broadcasted_iota(jnp.int32, shape, 0) >= slots).astype(jnp.int32)
        ones = jnp.where((column >= LOG_COL) & (column < LOG_COL + 3), 1.0, 0.0)
        side = jnp.where(column == RESET_COL + start, MASKED, ones)
        keys = dot(source, w_ref[1])
        values = dot(source, w_ref[2])
        whole = slice(0, 2 * slots)
        for pair in range(CORE_HEADS // 2):
            lanes = slice(pair * LANES, (pair + 1) * LANES)
            by_head(ks_out, whole, pair, keys[:, lanes], side)
            by_head(vs_out, whole, pair, values[:, lanes], jnp.ones(shape, F32))
        for k in (KS, VS, ROWS):
            give(k)

    values = choose(rank, core, chip, *[ref[:rows, :] for ref in sources])

    @pl.when(rank % 2 == core)
    def _():
        tokens_out[rank // 2] = values
        give(TOKENS, rank // 2)

    unit, scale = norm_parts(values.astype(F32))
    normed = (unit * gain[0:1, :].astype(F32)).astype(BF16)
    place = pl.ds(pl.multiple_of(rank * rows, rows), rows)
    normed_out[place, :] = normed
    give(NORMED, place)
    scale_out[place, :] = jnp.broadcast_to(scale, (rows, LANES))
    give(SCALES, place)
    low = jnp.zeros((1, LANES), jnp.int32)
    high = jnp.zeros((1, LANES), jnp.int32)
    for k in range(8):
        low = jnp.where(column == k, info[1 + k] if k else 0, low)
        high = jnp.where(column == k, info[2 + k], high)
    reset = info[10 + (rank * rows) // SEGMENT]
    position = rank * rows + lax.broadcasted_iota(jnp.int32, shape, 0)
    here = (position >= low) & (position < high)
    fixed = jnp.where(column == RESET_COL + 1 - reset, 1.0, 0.0)
    q_side = jnp.where(here, 1.0, jnp.broadcast_to(fixed, shape))
    ones = jnp.where((column >= LOG_COL) & (column < LOG_COL + 3), 1.0, 0.0)
    others = jnp.where(column < 8, MASKED, ones)
    k_side = jnp.where(here, 0.0, jnp.broadcast_to(others, shape))
    for which, out, side in ((0, q_out, q_side), (1, k_out, k_side), (2, v_out, jnp.ones(shape, F32))):
        result = dot(normed, w_ref[which])
        for pair in range(CORE_HEADS // 2):
            by_head(out, place, pair, result[:, pair * LANES : (pair + 1) * LANES], side)


    @pl.when(rank == 3)
    def _():
        give(K)
        give(V)


Q_LOG, K, V, KS, VS, NORMED, TOKENS, ROWS, O, O_AWAY, SCALES, SHARES = range(12)
KEY_BLOCK = 256


def attend_step(block, give, info, head, q_ref, k_ref, v_ref, ks_ref, vs_ref, q_out, o_ref, away):
    core = info[0]
    length = q_ref.shape[1]
    rows = away.shape[2]
    pair, parity = head // 2, head % 2
    column = aux_column((block, LANES), parity)
    keep = (column < 0) | (column >= HEAD_DIM)
    row = lax.broadcasted_iota(jnp.int32, (block, block), 0)
    key = lax.broadcasted_iota(jnp.int32, (block, block), 1)
    for i in range(length // block):
        low, high = i * block, (i + 1) * block
        q = q_ref[head, low:high, :]
        slot = dot(q, ks_ref[head], NT)
        scores = dot(q, k_ref[head, :high, :], NT)
        last = jnp.where(row >= key, scores[:, low:], MASKED)
        scores = jnp.concatenate([scores[:, :low], last], axis=1) if i else last
        top = jnp.maximum(
            jnp.max(scores, axis=1, keepdims=True), jnp.max(slot, axis=1, keepdims=True)
        )
        share = jnp.exp2((scores - top) * EXP).astype(BF16)
        slot_share = jnp.exp2((slot - top) * EXP).astype(BF16)
        total = dot(share, v_ref[head, :high, :]) + dot(slot_share, vs_ref[head])
        count = jnp.where(parity == 0, total[:, HEAD_DIM : HEAD_DIM + 1], total[:, 0:1])
        o_ref[pair, low:high, :] = jnp.where(
            keep, (total / count).astype(BF16), o_ref[pair, low:high, :]
        )
        log = top + jnp.log2(count) * (1.0 / EXP)
        q_out[head, low:high, :] = put_log(column, -log, q.astype(F32)).astype(BF16)
    give(Q_LOG, head)

    @pl.when(parity == 1)
    def _():
        for rank in range(4):

            @pl.when(core != rank % 2)
            def _():
                away[rank // 2, pair] = o_ref[pair, rank * rows : (rank + 1) * rows, :]

        give(O, pair)
        give(O_AWAY, slice(None), pair)


def share_blocks(slots, length):
    return [(slots, length), *[(KEY_BLOCK, length - low) for low in range(0, length, KEY_BLOCK)]]


def shares_step(give, head, q_log, k_ref, ks_ref, shares):
    q = q_log[head]
    shares[0][head] = jnp.exp2(dot(ks_ref[head], q, NT) * EXP).astype(BF16)
    for j in range(len(shares) - 1):
        low = j * KEY_BLOCK
        scores = dot(k_ref[head, low : low + KEY_BLOCK, :], q[low:, :], NT)
        share = jnp.exp2(scores * EXP)
        key = lax.broadcasted_iota(jnp.int32, (KEY_BLOCK, KEY_BLOCK), 0)
        position = lax.broadcasted_iota(jnp.int32, (KEY_BLOCK, KEY_BLOCK), 1)
        first = jnp.where(key <= position, share[:, :KEY_BLOCK], 0.0)
        shares[j + 1][head, :, :KEY_BLOCK] = first.astype(BF16)
        if share.shape[1] > KEY_BLOCK:
            shares[j + 1][head, :, KEY_BLOCK:] = share[:, KEY_BLOCK:].astype(BF16)
    for j in range(len(shares)):
        give(SHARES + j, head)


def read_kernel(
    need, give, info, packed, init, gain, mine, recv, mine_other, recv_other,
    q_log, k, v, ks, vs, normed, tokens, rows, o, o_away, scales, *refs,
):
    shares, q, w_ref = refs[:-2], refs[-2], refs[-1]
    step = pl.program_id(0)

    @pl.when(step < 4)
    def _():
        project_step(
            need, give, info, step, packed, init, gain, (mine, recv, mine_other, recv_other),
            q, k, v, normed, ks, vs, rows, tokens, scales, w_ref,
        )

    @pl.when((step >= 4) & (step < 4 + CORE_HEADS))
    def _():
        attend_step(256, give, info, step - 4, q, k, v, ks, vs, q_log, o, o_away)

    @pl.when(step >= 4 + CORE_HEADS)
    def _():
        shares_step(give, step - 4 - CORE_HEADS, q_log, k, ks, shares)


def read(info, sources, packed, init, gains, rows):
    total, width = sources[0].shape
    slots = 4 * (total - rows)
    length = 4 * rows
    heads = ((CORE_HEADS, length, LANES), BF16)
    slot = ((CORE_HEADS, 2 * slots, LANES), BF16)
    return streamed(
        read_kernel, "read", info, (packed, init, gains, *sources),
        (heads, heads, heads, slot, slot, ((length, width), BF16), ((2, rows, width), BF16),
         ((slots, width), BF16), ((2, length, LANES), BF16), ((2, 2, rows, LANES), BF16), ((length, LANES), F32),
         *[((CORE_HEADS, *block), BF16) for block in share_blocks(2 * slots, length)]),
        [pltpu.VMEM((CORE_HEADS, length, LANES), BF16), pltpu.VMEM((3, width, CORE_WIDTH), BF16)],
        grid=(4 + 2 * CORE_HEADS,),
    )


def attend_back_kernel(
    qb, first_head, info, own_ref, other_ref, o_ref, q_ref, k_ref, v_ref, ks_ref, vs_ref, shares,
    dq_ref, dk_ref, dv_ref, dks_ref, dvs_ref, d_ref, acc_ref, wait=lambda _: None,
):
    length = q_ref.shape[1]
    step = pl.program_id(0)
    head = first_head + step
    pair, parity = head // 2, head % 2
    core = info[0]
    rows = own_ref.shape[2]
    column = aux_column((rows, LANES), parity)
    inside = (column < 0) | (column >= HEAD_DIM)
    for r in range(length // rows):
        low, high = r * rows, (r + 1) * rows
        d = jnp.where(core == r % 2, own_ref[r // 2, pair], other_ref[r // 2, pair]).astype(F32)
        delta = jnp.sum(
            jnp.where(inside, d * o_ref[pair, low:high, :].astype(F32), 0.0), axis=1, keepdims=True
        )
        d_ref[low:high, :] = jnp.where(
            inside, d, put_log(column, -delta, jnp.zeros_like(d))
        ).astype(BF16)
    acc_ref[...] = jnp.zeros_like(acc_ref)

    def tiles(k, v, shares, first):
        turned = k.astype(F32).T.astype(BF16)
        dk = jnp.zeros((k.shape[0], LANES), F32)
        dv = jnp.zeros((k.shape[0], LANES), F32)
        low = first
        while low < length:
            high = min((low // qb + 1) * qb, length)
            q = q_ref[step, low:high, :]
            d = d_ref[low:high, :]
            share = shares[step, :, low - first : high - first]
            ds = (share.astype(F32) * dot(v, d, NT)).astype(BF16)
            dv = dv + dot(share, d)
            dk = dk + dot(ds, q)
            acc_ref[:, low:high] += dot(turned, ds)
            low = high
        return dk, dv

    wait(0)
    dk, dv = tiles(ks_ref[step], vs_ref[step], shares[0], 0)
    dks_ref[step] = (dk * SCALE).astype(BF16)
    dvs_ref[step] = dv.astype(BF16)
    for j in range(len(shares) - 1):
        low = j * KEY_BLOCK
        place = slice(low, low + KEY_BLOCK)
        wait(j + 1)
        dk, dv = tiles(k_ref[step, place, :], v_ref[step, place, :], shares[j + 1], low)
        dk_ref[step, place, :] = (dk * SCALE).astype(BF16)
        dv_ref[step, place, :] = dv.astype(BF16)
    dq_ref[step] = (acc_ref[...].T * SCALE).astype(BF16)


def back_scratch(length):
    return [pltpu.VMEM((length, LANES), BF16), pltpu.VMEM((LANES, length), F32)]


def of_heads(array, first, heads):
    shape = (heads, *array.shape[1:])
    return array, shape, [((first + j,), (j,)) for j in range(heads)]


def of_pairs(array, axis, first, heads):
    before = (slice(None),) * axis
    pieces = [((*before, p),) * 2 for p in range(first // 2, (first + heads - 1) // 2 + 1)]
    return array, array.shape, pieces


def head_arrays(first, heads, q, k, v, ks, vs, shares, own, other, o):
    return [
        of_pairs(own, 1, first, heads), of_pairs(other, 1, first, heads),
        of_pairs(o, 0, first, heads),
        *[of_heads(array, first, heads) for array in (q, k, v, ks, vs, *shares)],
    ]


def need_heads(need, first, heads, arrays):
    for k in range(3):
        for j in range((first + heads - 1) // 2 - first // 2 + 1):
            need(k, j)
    for j in range(heads):

        @pl.when(pl.program_id(0) == j)
        def _():
            for k in range(3, arrays):
                need(k, j, None)


def some_heads_kernel(first, heads, need, give, info, *refs):
    count = len(refs) - 7
    wait = lambda _: None
    if heads == 1:
        for k in range(3):
            need(k, 0, None)

        def wait(j):
            for k in (8 + j,) if j else range(3, 9):
                need(k, 0, None)
    else:
        need_heads(need, first, heads, count)
    attend_back_kernel(1024, first, info, *refs[:8], refs[8:count], *refs[count:], wait=wait)
    for k in range(5):
        give(k, pl.program_id(0))


def attend_back(info, first, heads, q, k, v, ks, vs, shares, own, other, o):
    _, length, _ = q.shape
    out = ((heads, length, LANES), BF16)
    slot_out = ((heads, ks.shape[1], LANES), BF16)
    return streamed(
        functools.partial(some_heads_kernel, first, heads), "attend_back", info,
        head_arrays(first, heads, q, k, v, ks, vs, shares, own, other, o),
        (out, out, out, slot_out, slot_out), back_scratch(length), grid=(heads,),
    )


def side_by_side(tiles):
    return jnp.concatenate(tiles, axis=1)


MIDDLE, NORMED_TWO, ACT, SLOPE, RESULT, KEYS, VALUES, AWAY, WQ, SK, SV, STATS = range(12)


def forward_kernel(
    need, give, info, own, other, tokens_ref, gains, packed, memory,
    middle_out, normed_out, act_out, slope_out, result_out, keys_out, values_out, away_out,
    query_out, key_out, value_out, stats,
):
    refs = (
        own, other, tokens_ref, gains, packed, memory, middle_out, normed_out, act_out, slope_out,
        result_out, keys_out, values_out, away_out,
    )
    step = pl.program_id(0)
    pl.when(step == 0)(lambda: forward_step(lambda k, j=0: need(k, j, None), give, info, *refs))
    pl.when(step > 0)(lambda: forward_step(lambda *_: None, give, info, *refs))

    @pl.when(step == pl.num_programs(0) - 1)
    def _():
        write_step(keys_out, values_out, memory, packed, query_out, key_out, value_out, stats)
        for k in (WQ, SK, SV, STATS):
            give(k)


def forward_step(
    need, give, info, own, other, tokens_ref, gains, packed, memory,
    middle_out, normed_out, act_out, slope_out, result_out, keys_out, values_out, away_out,
):
    core, chip = info[0], info[1]
    half = CORE_WIDTH // FIELDS[OUT]
    for k in range(4):
        need(k)
    need(4, OUT)
    w_own = flat_rows(packed[pl.ds(core * half, half), : FIELDS[OUT], :])
    w_other = flat_rows(packed[pl.ds((1 - core) * half, half), : FIELDS[OUT], :])
    step = pl.program_id(0)
    rows = normed_out.shape[1]
    block = 2 * rows // pl.num_programs(0)
    which, at = step // (rows // block), pl.multiple_of(step % (rows // block) * block, block)
    place = (which, pl.ds(at, block))
    tokens = tokens_ref[place]
    start = pl.multiple_of((2 * which + core) * rows + at, block)
    o_own = side_by_side([own[pair, pl.ds(start, block), :] for pair in range(2)])
    o_other = side_by_side([other[which, pair, pl.ds(at, block), :] for pair in range(2)])
    middle = tokens.astype(F32) + (dot(o_own, w_own) + dot(o_other, w_other))
    middle_out[place] = middle
    unit, _ = norm_parts(middle)
    normed = (unit * gains[1:2, :].astype(F32)).astype(BF16)
    normed_out[place] = normed
    width = normed.shape[1]
    for k in range(CHUNKS):
        need(4, UP + k)
        pre = dot(normed, take_up(packed, k))
        square = pre * pre
        half = 0.5 + 0.5 * jnp.tanh(pre * (GELU_A + (GELU_A * GELU_B) * square))
        turn = (half - half * half) * (2.0 * GELU_A + (6.0 * GELU_A * GELU_B) * square)
        act_out[(k, *place)] = (pre * half).astype(BF16)
        slope_out[(k, *place)] = (half + pre * turn).astype(BF16)
    acts = side_by_side([act_out[(k, *place)] for k in range(CHUNKS)])
    need(4, DOWN)
    low = (middle + dot(acts, take(packed, DOWN))).astype(BF16)
    result_out[place] = low

    @pl.when(which != chip)
    def _():
        away_out[pl.ds(at, block), :] = low
        give(AWAY, pl.ds(at, block))

    need(4, WRITE)
    need(4, VALUE)
    need(5)
    keys_out[place] = dot(low, flat_rows(packed[OWNERS // 2 :, CUTS[WRITE] : CUTS[WRITE + 1], :])).astype(BF16)
    values_out[place] = dot(low, take(packed, VALUE)).astype(BF16)


    for k in (MIDDLE, NORMED_TWO, RESULT, KEYS, VALUES):
        give(k, *place)
    for k in (ACT, SLOPE):
        give(k, slice(None), *place)


def fields_of(packed):
    cuts = [*CUTS[:UP], *[CUTS[UP] + k * PART for k in range(CHUNKS + 1)]]
    pieces = [(slice(None), slice(cuts[k], cuts[k + 1])) for k in range(len(cuts) - 1)]
    return packed, packed.shape, [(piece, piece) for piece in pieces]


def forward(info, tokens, o, other, packed, gains, memory):
    _, rows, width = tokens.shape
    slots = memory.shape[0]
    small = ((2, rows, width), BF16)
    wide = ((CHUNKS, 2, rows, FF // CHUNKS), BF16)
    slot = ((slots, width), BF16)
    return streamed(
        forward_kernel, "feed_forward", info, (o, other, tokens, gains, fields_of(packed), memory),
        (((2, rows, width), F32), small, wide, wide, small, small, small, ((rows, width), BF16),
         slot, slot, slot, ((3, slots, width), F32)),
        grid=(4,),
    )


KEPT, SENT, D_MIDDLE, D_OWN, D_OTHER, G_GAIN, D_MEMORY, NEW_ROWS = range(8)


def backward_kernel(
    need, give, info, stats, stats_other, query, key, value, rows_ref, cot_mine, cot_recv,
    cot_other, keys, values, packed, result, normed, act, slope, middle, own, other, gains,
    kept, away, d_middle_out, d_own, d_other, g_gain, d_memory, new_out,
    d_keys, d_values, d_query, d_self_key, d_self_value, mem_cot,
    d_result_ref, d_update_ref, d_normed_ref,
):
    step = pl.program_id(0)
    core, chip = info[0], info[1]
    count, rows, width = result.shape
    total = count * rows
    half = CORE_WIDTH // FIELDS[OUT]

    @pl.when(step == 0)
    def _():
        for k in range(11):
            need(k)
        write_back_step(
            info, stats, stats_other, query, key, value, rows_ref, cot_mine, cot_recv, cot_other,
            keys, values, new_out, d_keys, d_values, d_query, d_self_key, d_self_value, mem_cot,
        )
        give(NEW_ROWS)
        need(11, WRITE)
        need(11, VALUE)
        need(12)

    @pl.when(step == 0)
    def _():
        dk = d_keys[...].reshape(total, width)
        dv = d_values[...].reshape(total, width)
        w_query = flat_rows(packed[: OWNERS // 2, CUTS[WRITE] : CUTS[WRITE + 1], :])
        w_key = flat_rows(packed[OWNERS // 2 :, CUTS[WRITE] : CUTS[WRITE + 1], :])
        w_value = take(packed, VALUE)
        first, second = cot_mine[:rows, :].astype(F32), cot_recv[:rows, :].astype(F32)
        cot = jnp.concatenate(
            [jnp.where(chip == 0, first, second), jnp.where(chip == 0, second, first)], axis=0
        )
        d_result = cot + (dot(dk, w_key, NT) + dot(dv, w_value, NT))
        d_result_ref[...] = d_result
        d_update_ref[...] = d_result.astype(BF16)
        d_normed_ref[...] = jnp.zeros_like(d_normed_ref)
        out = result[...].reshape(total, width)
        memory = rows_ref[...]
        put(core, kept, away, dot(memory, d_query[...], TN), 0, OWNERS // 2, CUTS[WRITE], FIELDS[WRITE])
        put(
            core, kept, away, dot(out, dk, TN) + dot(memory, d_self_key[...], TN),
            OWNERS // 4, OWNERS // 2, CUTS[WRITE], FIELDS[WRITE],
        )
        put(
            core, kept, away, dot(out, dv, TN) + dot(memory, d_self_value[...], TN),
            0, OWNERS, CUTS[VALUE], FIELDS[VALUE],
        )
        d_memory[...] = mem_cot[...] + (
            dot(d_query[...], w_query, NT)
            + dot(d_self_key[...], w_key, NT)
            + dot(d_self_value[...], w_value, NT)
        )
        give(D_MEMORY)
        for k in (SENT, KEPT):
            give(k, slice(None), slice(CUTS[VALUE], CUTS[WRITE + 1]))
        need(11, DOWN)
        for k in range(CHUNKS):
            need(11, UP + k)
        need(13)

    for j in range(CHUNKS):
        need(14, j, j)
        need(15, j, j)
    d_update = d_update_ref[...]
    d_act = dot(d_update, take_down(packed, step), NT)
    d_hidden = (d_act * slope[step].reshape(total, -1).astype(F32)).astype(BF16)
    g_down = dot(act[step].reshape(total, -1), d_update, TN)
    owners = OWNERS // CHUNKS
    put(core, kept, away, g_down, step * (owners // 2), owners, CUTS[DOWN], FIELDS[DOWN])
    g_up = dot(normed[...].reshape(total, width), d_hidden, TN)
    at = pl.multiple_of(CUTS[UP] + step * PART, PART)
    put(core, kept, away, g_up, 0, OWNERS, at, PART)
    for k in (SENT, KEPT):
        give(k, slice(None), pl.ds(at, PART))
        give(k, pl.ds(step * (owners // 2), owners // 2), slice(CUTS[DOWN], CUTS[DOWN + 1]))
    d_normed_ref[...] += dot(d_hidden, take_up(packed, step), NT)

    @pl.when(step == pl.num_programs(0) - 1)
    def _():
        for k in (16, 17, 18, 19):
            need(k, 0, CHUNKS - 1)
        need(11, OUT, CHUNKS - 1)
        gain = gains[1:2, :].astype(F32)
        unit, scale = norm_parts(middle[...].reshape(total, width))
        d_normed = d_normed_ref[...]
        g_gain[...] = jnp.sum(d_normed * unit, axis=0, keepdims=True)
        d_middle = d_result_ref[...] + norm_back(unit, scale, d_normed, gain)
        d_middle_out[...] = d_middle.reshape(count, rows, width)
        give(D_MIDDLE)
        give(G_GAIN)
        d_branch = d_middle.astype(BF16)
        for start, out in ((core * half, d_own), ((1 - core) * half, d_other)):
            weight = flat_rows(packed[pl.ds(start, half), : FIELDS[OUT], :])
            back = dot(d_branch, weight, NT).astype(BF16)
            for k in range(count):
                for pair in range(2):
                    lanes = slice(pair * LANES, (pair + 1) * LANES)
                    out[k, pair] = back[k * rows : (k + 1) * rows, lanes]
        give(D_OWN)
        give(D_OTHER)
        own_rows = jnp.concatenate(
            [
                side_by_side(
                    [
                        own[pair, pl.ds(pl.multiple_of((2 * k + core) * rows, rows), rows), :]
                        for pair in range(2)
                    ]
                )
                for k in range(count)
            ],
            axis=0,
        )
        other_rows = jnp.concatenate([side_by_side([other[k, 0], other[k, 1]]) for k in range(count)], axis=0)
        g_own = dot(own_rows, d_branch, TN)
        g_other = dot(other_rows, d_branch, TN)
        put(core, kept, away, g_own, core * (half // 2), half, 0, FIELDS[OUT])
        put(core, kept, away, g_other, (1 - core) * (half // 2), half, 0, FIELDS[OUT])
        for k in (SENT, KEPT):
            give(k, slice(None), slice(CUTS[OUT], CUTS[OUT + 1]))


def by_chunk(array):
    return array, array.shape, [((j,), (j,)) for j in range(CHUNKS)]


def backward(info, stats, stats_other, writer, memory, cots, cot_other, keys, values, packed,
             result, normed, act, slope, middle, o, other, gains):
    _, rows, width = result.shape
    slots = memory.shape[0]
    grads = ((OWNERS // 2, PACKED, width), BF16)
    half = ((2, 2, rows, LANES), BF16)
    slot = pltpu.VMEM((slots, width), BF16)
    return streamed(
        backward_kernel, "feed_forward_back", info,
        (stats, stats_other, *writer, memory, *cots, cot_other, keys, values, fields_of(packed),
         result, normed, by_chunk(act), by_chunk(slope), middle, o, other, gains),
        (grads, grads, ((2, rows, width), F32), half, half, ((1, width), F32),
         ((slots, width), F32), ((slots, width), BF16)),
        [pltpu.VMEM((2, rows, width), BF16), pltpu.VMEM((2, rows, width), BF16), slot, slot, slot,
         pltpu.VMEM((slots, width), F32),
         pltpu.VMEM((2 * rows, width), F32), pltpu.VMEM((2 * rows, width), BF16),
         pltpu.VMEM((2 * rows, width), F32)],
        grid=(CHUNKS,),
    )


def head_mask(shape, head):
    lane = lax.broadcasted_iota(jnp.int32, shape, 1)
    return (lane >= head * HEAD_DIM) & (lane < (head + 1) * HEAD_DIM)


def stacked_heads(values):
    return jnp.concatenate(
        [jnp.where(head_mask(values.shape, h), values, 0.0) for h in range(HEADS)], axis=0
    )


def joined_heads(stacked, slots):
    out = None
    for h in range(HEADS):
        part = stacked[h * slots : (h + 1) * slots, :]
        shape = (slots, HEADS * HEAD_DIM)
        part = jnp.broadcast_to(part, shape)
        out = part if out is None else jnp.where(head_mask(shape, h), part, out)
    return out


def column_of_heads(values):
    return jnp.concatenate(
        [values[:, h * HEAD_DIM : h * HEAD_DIM + 1] for h in range(HEADS)], axis=0
    )


def head_sums(values):
    return jnp.concatenate(
        [
            jnp.sum(jnp.where(head_mask(values.shape, h), values, 0.0), axis=1, keepdims=True)
            for h in range(HEADS)
        ],
        axis=0,
    )


def write_step(keys, values, memory, packed, query_out, key_out, value_out, stats):
    slots = memory.shape[0]
    total = keys.shape[0] * keys.shape[1]
    rows = memory[...]
    w_write = take(packed, WRITE)
    query = dot(rows, w_write[: w_write.shape[0] // 2]).astype(BF16)
    query_out[...] = query
    key_out[...] = dot(rows, w_write[w_write.shape[0] // 2 :]).astype(BF16)
    value_out[...] = dot(rows, take(packed, VALUE)).astype(BF16)
    stacked = stacked_heads(query.astype(F32)).astype(BF16)
    scores = dot(stacked, keys[...].reshape(total, -1), NT)
    top = jnp.max(scores, axis=1, keepdims=True)
    share = jnp.exp2((scores - top) * EXP)
    stats[0] = joined_heads(top, slots)
    stats[1] = joined_heads(jnp.sum(share, axis=1, keepdims=True), slots)
    stats[2] = joined_heads(dot(share.astype(BF16), values[...].reshape(total, -1)), slots)


def write_back_step(
    info, own, other, query, key, value, memory, cot_mine, cot_recv, cot_other, keys, values,
    new_out, d_keys, d_values, d_query, d_key, d_value, cot_out,
):
    core, chip = info[0], info[1]
    slots, width = memory.shape
    part = slots // 4
    rows = keys.shape[1]
    total = keys.shape[0] * rows
    sources = (cot_mine[rows:, :], cot_recv[rows:, :], cot_other[:part, :], cot_other[part:, :])
    cot = jnp.concatenate([choose(k, core, chip, *sources) for k in range(4)], axis=0).astype(F32)
    q = query[...].astype(F32)
    sk = key[...].astype(F32)
    sv = value[...].astype(F32)
    self_column = head_sums(q * sk)
    self_scores = joined_heads(self_column, slots)
    top = jnp.maximum(jnp.maximum(own[0], other[0]), self_scores)
    own_share = jnp.exp2((own[0] - top) * EXP)
    other_share = jnp.exp2((other[0] - top) * EXP)
    self_share = jnp.exp2((self_scores - top) * EXP)
    count = own[1] * own_share + other[1] * other_share + self_share
    written = (
        own[2] * own_share + other[2] * other_share + self_share.astype(BF16).astype(F32) * sv
    ) / count
    new_out[...] = (memory[...].astype(F32) + written).astype(BF16)
    log = top + jnp.log2(count) * (1.0 / EXP)
    log_column = column_of_heads(log)
    delta_column = head_sums(cot * written)
    delta = joined_heads(delta_column, slots)
    stacked = stacked_heads(q).astype(BF16)
    stacked_cot = stacked_heads(cot).astype(BF16)
    flat_keys = keys[...].reshape(total, width)
    share = jnp.exp2((dot(stacked, flat_keys, NT) - log_column) * EXP)
    d_share = dot(stacked_cot, values[...].reshape(total, width), NT)
    d_scores = (share * (d_share - delta_column)).astype(BF16)
    d_values[...] = dot(share.astype(BF16), stacked_cot, TN).astype(BF16).reshape(d_values.shape)
    d_keys[...] = (dot(d_scores, stacked, TN) * SCALE).astype(BF16).reshape(d_keys.shape)
    d_query_part = joined_heads(dot(d_scores, flat_keys), slots) * SCALE
    mine = (lax.broadcasted_iota(jnp.int32, (slots, width), 0) // part) % 2 == core
    self_probs = jnp.exp2((self_scores - log) * EXP)
    self_dp = joined_heads(head_sums(cot * sv), slots)
    self_ds = (self_probs * (self_dp - delta)).astype(BF16).astype(F32) * SCALE
    self_ds = jnp.where(mine, self_ds, 0.0)
    d_query[...] = (d_query_part + self_ds * sk).astype(BF16)
    d_key[...] = (self_ds * q).astype(BF16)
    d_value[...] = jnp.where(mine, self_probs.astype(BF16).astype(F32) * cot, 0.0).astype(BF16)
    cot_out[...] = jnp.where(mine, cot, 0.0)


def merged_heads(heads, place):
    tiles = [ref[k, place, :] for ref in heads for k in range(ref.shape[0])]
    lane = lax.broadcasted_iota(jnp.int32, tiles[0].shape, 1)
    return side_by_side(
        [jnp.where(lane < HEAD_DIM, tiles[2 * p], tiles[2 * p + 1]) for p in range(len(tiles) // 2)]
    )


def inputs_back_step(
    info, dq_parts, dk_parts, dv_parts, packed, normed, scales, gain, d_middle,
    mine_out, away_out, g_gain, merged,
):
    core = info[0]
    rows = mine_out.shape[1]
    weights = [qkv_weight(packed, k) for k in range(3)]
    gain = gain[0:1, :].astype(F32)
    gain_sum = None
    for rank in range(4):
        place = pl.ds(rank * rows, rows)
        total = None
        for k, parts in enumerate((dq_parts, dk_parts, dv_parts)):
            grads = merged_heads(parts, place)
            merged[k, place, :] = grads
            term = dot(grads, weights[k], NT)
            total = term if total is None else total + term
        unit = normed[place, :].astype(F32) * (1.0 / gain)
        part = jnp.sum(total * unit, axis=0, keepdims=True)
        gain_sum = part if gain_sum is None else gain_sum + part
        back = norm_back(unit, scales[place, 0:1], total, gain)

        @pl.when(core == rank % 2)
        def _():
            mine_out[rank // 2] = d_middle[rank // 2] + back

        @pl.when(core != rank % 2)
        def _():
            away_out[rank // 2] = back.astype(BF16)

    g_gain[...] = gain_sum


ATTN_ROWS, INIT_ROWS, GAIN_ROWS, SMALL_ROWS = 96, 8, 4, 112


def weights_back_step(
    info, normed, merged, packed, memory, init, d_memory, g_gain, g_gain_two, dks_parts, dvs_parts,
    small, d_mine, d_away, g_ref, misc,
):
    source = jnp.concatenate([memory[...], init[...]], axis=0)
    everything = slice(0, source.shape[0])
    dks = merged_heads(dks_parts, everything)
    dvs = merged_heads(dvs_parts, everything)
    d_slots = dot(dks, qkv_weight(packed, 1), NT) + dot(dvs, qkv_weight(packed, 2), NT)
    slots = memory.shape[0]
    part = slots // 4
    total = d_memory[...] + d_slots[:slots]
    for k in range(2):
        even = total[2 * k * part : (2 * k + 1) * part]
        odd = total[(2 * k + 1) * part : (2 * k + 2) * part]
        d_mine[k * part : (k + 1) * part, :] = jnp.where(info[0] == 0, even, odd)
        d_away[k * part : (k + 1) * part, :] = jnp.where(info[0] == 0, odd, even)
    rows = normed[...]
    width = rows.shape[1]
    g_ref[:width, :] = dot(rows, merged[0], TN).astype(BF16)
    g_ref[width : 2 * width, :] = (dot(rows, merged[1], TN) + dot(source, dks, TN)).astype(BF16)
    g_ref[2 * width :, :] = (dot(rows, merged[2], TN) + dot(source, dvs, TN)).astype(BF16)
    pairs = OWNERS // 2
    small[:, :ATTN_ROWS, :] = g_ref[...].reshape(pairs, ATTN_ROWS, CORE_WIDTH)
    misc[...] = jnp.zeros_like(misc)
    each = slots // pairs
    for h in range(2):
        lanes = slice(h * CORE_WIDTH, (h + 1) * CORE_WIDTH)
        for k in range(slots):
            misc[k // each, 2 * (k % each) + h : 2 * (k % each) + h + 1, :] = d_slots[
                slots + k : slots + k + 1, lanes
            ]
        for k, gain in enumerate((g_gain, g_gain_two)):
            at = INIT_ROWS + 2 * k + h
            misc[:, at : at + 1, :] = jnp.broadcast_to(gain[:, lanes][None], (pairs, 1, CORE_WIDTH))
    small[:, ATTN_ROWS:, :] = misc[...].astype(BF16)


def last_heads_kernel(first, count, arrays, need, give, info, *refs):
    heads, refs = refs[:arrays], refs[arrays:]
    packed, refs = refs[0], refs[1:]
    earlier, refs = refs[:5], refs[5:]
    normed, scales, gain, d_middle, memory, init, d_memory, g_gain_two, refs = *refs[:8], refs[8:]
    d_mine, d_away, small, m_mine, m_away, refs = *refs[:5], refs[5:]
    results, merged, g_gain, g_ref, misc, scratch = refs[:5], *refs[5:9], refs[9:]
    need_heads(need, first, count, arrays)
    attend_back_kernel(1024, first, info, *heads[:8], heads[8:], *results, *scratch)

    @pl.when(pl.program_id(0) == pl.num_programs(0) - 1)
    def _():
        for k in range(arrays, arrays + 14):
            need(k, 0, pl.num_programs(0) - 1)
        parts = [(earlier[k], results[k]) for k in range(5)]
        inputs_back_step(
            info, *parts[:3], packed, normed, scales, gain, d_middle, d_mine, d_away, g_gain, merged
        )
        for k in range(2):
            give(k)
        weights_back_step(
            info, normed, merged, packed, memory, init, d_memory, g_gain, g_gain_two, *parts[3:],
            small, m_mine, m_away, g_ref, misc,
        )
        for k in range(2, 5):
            give(k)


def last_heads(info, first, heads, q, k, v, ks, vs, shares, own, other, o, packed, earlier,
               normed, scales, gains, d_middle, memory, init, d_memory, g_gain_two):
    length, width = normed.shape
    slots = memory.shape[0]
    part = (d_middle.shape, F32)
    away = (d_middle.shape, BF16)
    half = ((slots // 2, width), F32)
    out = pltpu.VMEM((heads, length, LANES), BF16)
    slot_out = pltpu.VMEM((heads, ks.shape[1], LANES), BF16)
    count = 8 + len(shares)
    return streamed(
        functools.partial(last_heads_kernel, first, heads, count), "last_heads", info,
        (*head_arrays(first, heads, q, k, v, ks, vs, shares, own, other, o), packed, *earlier,
         normed, scales, gains, d_middle, memory, init, d_memory, g_gain_two),
        (part, away, ((OWNERS // 2, SMALL_ROWS, CORE_WIDTH), BF16), half, half),
        [out, out, out, slot_out, slot_out, pltpu.VMEM((3, length, CORE_WIDTH), BF16),
         pltpu.VMEM((1, width), F32), pltpu.VMEM((3 * width, CORE_WIDTH), BF16),
         pltpu.VMEM((OWNERS // 2, SMALL_ROWS - ATTN_ROWS, CORE_WIDTH), F32), *back_scratch(length)],
        grid=(heads,), late=range(count, count + 14),
    )


def inputs_back_kernel(
    need, give, info, mine, other, mem_mine, mem_other, new_rows, d_out, away_out, mem_out
):
    core, chip = info[0], info[1]
    count, rows, _ = mine.shape
    for k in range(count):
        need(0, k)
        need(1, k)
        back = (mine[k] + other[k].astype(F32)).astype(BF16)
        d_out[k] = back
        give(0, k)

        @pl.when(chip != k)
        def _():
            away_out[:rows, :] = back

    for j in range(2, 5):
        need(j)
    part = mem_mine.shape[0] // 2
    grads = (mem_mine[...] + mem_other[...]).astype(BF16)
    news = [
        jnp.where(
            core == 0,
            new_rows[2 * k * part : (2 * k + 1) * part, :],
            new_rows[(2 * k + 1) * part : (2 * k + 2) * part, :],
        )
        for k in range(2)
    ]
    first, second = grads[:part], grads[part:]
    mem_out[:part, :] = jnp.where(chip == 0, first, second)
    mem_out[part:, :] = jnp.where(chip == 0, news[0], news[1])
    away_out[rows : rows + part, :] = jnp.where(chip == 0, second, first)
    away_out[rows + part :, :] = jnp.where(chip == 0, news[1], news[0])
    for k in (1, 2):
        give(k)


def inputs_back(info, mine, other, mem_mine, mem_other, new_rows):
    _, rows, width = mine.shape
    slots = new_rows.shape[0]
    halves = [(array, array.shape, [((j,), (j,)) for j in range(2)]) for array in (mine, other)]
    return streamed(
        inputs_back_kernel, "inputs_back", info, (*halves, mem_mine, mem_other, new_rows),
        ((mine.shape, BF16), ((rows + slots // 2, width), BF16), ((slots // 2, width), BF16)),
    )


def swap(value, over_batch, over_seq):
    batch, seq = lax.axis_size("batch"), lax.axis_size("seq")
    pairs = [
        (i * seq + j, (i ^ over_batch) * seq + (j ^ over_seq))
        for i in range(batch)
        for j in range(seq)
    ]
    return lax.ppermute(value, ("batch", "seq"), pairs)


def chip_groups():
    batch = lax.axis_index("batch")
    chip = lax.axis_index("seq") // 2
    stages = [(4, 2 * (batch & 1) + chip, lambda k: (k >> 1, 2 * (k & 1)))]
    bits = lax.axis_size("batch").bit_length() - 1
    at = 1
    while at < bits:
        count = min(2, bits - at)
        stages.append(
            (1 << count, (batch >> at) & ((1 << count) - 1), lambda k, at=at: (k << at, 0))
        )
        at += count
    return stages


def in_order(pieces, own):
    bit = 1
    while bit < len(pieces):
        turned = (own & bit) > 0
        pieces = [jnp.where(turned, pieces[k ^ bit], pieces[k]) for k in range(len(pieces))]
        bit *= 2
    return jnp.stack(pieces)


def gather_chips(piece):
    stages = chip_groups()
    shape = piece.shape
    for size, own, peer in reversed(stages):
        piece = in_order([piece] + [swap(piece, *peer(k)) for k in range(1, size)], own)
    count = len(stages)
    piece = piece.transpose(*reversed(range(count)), *range(count, piece.ndim))
    return piece.reshape(-1, *shape)


def square_groups():
    batch, seq = lax.axis_size("batch"), lax.axis_size("seq")
    return [
        [(2 * r + y) * seq + 2 * x + core for y in range(2) for x in range(2)]
        for r in range(batch // 2)
        for core in range(2)
    ]


def line_groups():
    batch, seq = lax.axis_size("batch"), lax.axis_size("seq")
    return [
        [(2 * r + y) * seq + s for r in range(batch // 2)] for y in range(2) for s in range(seq)
    ]


def sent_lines(rows, stages):
    parts = [rows]
    for stage in stages[1:]:
        parts = sent(spread(added(parts, BF16), stage), stage)
    return parts


def sum_scattered(rows, groups):
    return lax.psum_scatter(
        rows, ("batch", "seq"), scatter_dimension=0, tiled=True, axis_index_groups=groups
    )


def spread(pieces, stage):
    size, own, _ = stage
    pieces = pieces.reshape(-1, size, *pieces.shape[-2:])
    return [lax.dynamic_index_in_dim(pieces, own ^ j, 1, keepdims=False) for j in range(size)]


def sent(parts, stage):
    size, _, peer = stage
    return [parts[0]] + [swap(parts[j], *peer(j)) for j in range(1, size)]


def added(parts, kind):
    total = parts[0].astype(F32)
    for part in parts[1:]:
        total = total + part.astype(F32)
    return total.astype(kind)


def after(values, *others):
    return lax.optimization_barrier((values, others))[0]


def by_core(core, mine, other, axis=0):
    return jnp.where(
        core == 0,
        jnp.concatenate([mine, other], axis=axis),
        jnp.concatenate([other, mine], axis=axis),
    )


def by_chip(chip, mine, other):
    return jnp.where(chip == 0, jnp.stack([mine, other]), jnp.stack([other, mine]))


def pick(array, index, axis=0):
    return lax.dynamic_index_in_dim(array, index, axis, keepdims=False)


def to_owners(fields, devices):
    many = devices // OWNERS
    out = []
    for k, field in enumerate(fields):
        if many > 1:
            groups = CHUNKS if k == UP else 1
            field = field.reshape(OWNERS, many, groups, -1, field.shape[-1])
            field = field.transpose(0, 2, 1, 3, 4).reshape(OWNERS, -1, field.shape[-1])
        out.append(field)
    return jnp.concatenate(out, axis=1)


def from_owners(packed, devices):
    many = devices // OWNERS
    out = []
    for k in range(len(FIELDS)):
        field = packed[:, CUTS[k] : CUTS[k + 1]]
        groups = CHUNKS if k == UP else 1
        field = field.reshape(OWNERS, groups, many, -1, field.shape[-1])
        out.append(field.transpose(0, 2, 1, 3, 4).reshape(devices, -1, field.shape[-1]))
    return jnp.concatenate(out, axis=1)


def per_device(
    tokens, memory, lengths, resets, attn_in, attn_out, ffn_in, ffn_out, writer_in, writer_value,
    norm_gains, memory_init, out_cotangent, memory_cotangent,
):
    _, rows, width = tokens.shape
    devices = lax.axis_size("batch") * lax.axis_size("seq")
    rank = lax.axis_index("seq")
    chip, core = rank // 2, rank % 2
    slot_part = memory.shape[1]
    slots = 4 * slot_part
    stages = chip_groups()

    ends = jnp.cumsum(pick(lengths, chip))
    info = jnp.concatenate([jnp.stack([core, chip]), ends, pick(resets, chip)]).astype(jnp.int32)

    def to_chip(big, small):
        mine = jnp.concatenate([pick(big, chip), pick(small, chip)], axis=0)
        away = jnp.concatenate([pick(big, 1 - chip), pick(small, 1 - chip)], axis=0)
        return mine, swap(away, 0, 2)

    misc = jnp.concatenate([memory_init, norm_gains])
    misc_rows = -(-misc.shape[0] // CORE_WIDTH)
    misc = jnp.pad(misc, (0, misc_rows * CORE_WIDTH - misc.shape[0])).reshape(misc_rows, CORE_WIDTH)
    attn_rows = attn_in.reshape(-1, 2, CORE_WIDTH)
    own_rows = attn_rows.shape[0]
    mine = jnp.concatenate([pick(attn_rows, core, 1), misc], axis=0)
    theirs = swap(jnp.concatenate([pick(attn_rows, 1 - core, 1), misc], axis=0), 0, 1)
    piece = jnp.concatenate(
        [
            by_core(core, mine[:own_rows], theirs[:own_rows]),
            by_core(core, mine[own_rows:], theirs[own_rows:]),
        ],
        axis=0,
    )
    gathered = gather_chips(piece)
    misc = gathered[:, 2 * own_rows :].reshape(devices, -1)
    init = misc[:, : memory_init.shape[0]].reshape(slots, width)
    gains = misc[:, memory_init.shape[0] :][:, : norm_gains.shape[0]].reshape(2, width)
    w_qkv = gathered
    if devices != OWNERS:
        w_qkv = gathered[:, : 2 * own_rows].reshape(OWNERS // 2, -1, CORE_WIDTH)

    columns = ffn_in.reshape(-1, CHUNKS, width).transpose(1, 0, 2).reshape(-1, width)
    fields = [attn_out, writer_value, writer_in, ffn_out, ffn_in]
    sizes = [field.shape[0] // width for field in fields]
    parts = [jnp.concatenate(fields[:UP]).reshape(-1, width), columns]
    cuts = [sum(sizes[:k]) for k in range(len(sizes) + 1)]
    packed = lax.all_gather(jnp.concatenate(parts, axis=0), ("batch", "seq"), axis=0)
    if devices != OWNERS:
        packed = to_owners([packed[:, cuts[k] : cuts[k + 1]] for k in range(len(sizes))], devices)

    own, recv = to_chip(tokens, memory)
    sources = (own, recv, swap(own, 0, 1), swap(recv, 0, 1))
    q_log, k, v, ks, vs, normed, own_tokens, mem_rows, o, o_away, scales, *shares = read(
        info, sources, w_qkv, init, gains, rows
    )
    out_cotangent, memory_cotangent = after((out_cotangent, memory_cotangent), recv)
    cots = to_chip(out_cotangent, memory_cotangent)
    cot_other = swap(jnp.concatenate([cot[rows:] for cot in after(cots, o)], axis=0), 0, 1)
    o_other = swap(o_away, 0, 1)
    middle, normed_two, act, slope, result, keys, values, result_away, *writer, stats = forward(
        info, own_tokens, o, o_other, packed, gains, mem_rows
    )
    came = swap(result_away, 0, 2)
    stats_other = swap(stats, 0, 1)
    kept, away, d_middle, d_own, d_away, g_gain_two, d_memory, new_rows = backward(
        info, stats, stats_other, writer, mem_rows, cots, cot_other, keys, values, packed, result,
        normed_two, act, slope, middle, o, o_other, gains,
    )
    d_other, came = after((swap(d_away, 0, 1), came), came)
    if devices != OWNERS:
        both = by_core(core, kept[:, None], away[:, None], axis=1).reshape(OWNERS, PACKED, width)
        both = from_owners(both, devices).reshape(devices // 2, 2, -1, width)
        kept, away = pick(both, core, 1), pick(both, 1 - core, 1)
    arrived = swap(after(away, d_other), 0, 1)

    heads = (q_log, k, v, ks, vs, shares)
    grads_a = attend_back(info, 0, 1, *heads, d_own, d_other, o)
    kept, arrived = after((kept, arrived), grads_a)
    square = [added(pair, BF16) for pair in zip(spread(kept, stages[0]), spread(arrived, stages[0]))]
    d_own = after(d_own, square)
    square = sent(square, stages[0])
    d_mine, d_away, small, mem_mine, mem_away = last_heads(
        info, 1, 3, *heads, d_own, d_other, o, w_qkv, grads_a, normed, scales, gains,
        d_middle, mem_rows, init, d_memory, g_gain_two,
    )
    d_sent = swap(d_away, 0, 1)
    m_sent = swap(mem_away, 0, 1)

    init_size = memory_init.shape[0]
    init_rows = 2 * init_size // CORE_WIDTH
    cut_init, cut_gain = 2 * own_rows, 2 * own_rows + init_rows
    if devices != OWNERS:
        pairs = devices // 2
        small = jnp.concatenate(
            [
                small[:, :ATTN_ROWS].reshape(pairs, -1, CORE_WIDTH),
                small[:, ATTN_ROWS : ATTN_ROWS + INIT_ROWS].reshape(pairs, -1, CORE_WIDTH),
                jnp.repeat(small[:, ATTN_ROWS + INIT_ROWS :], pairs // (OWNERS // 2), axis=0),
            ],
            axis=1,
        )
    small_parts = sent(spread(small, stages[0]), stages[0])
    parts = sent_lines(added(after(square, small), BF16), stages)
    d_sent = after(d_sent, parts[0])
    d_tokens, d_tokens_away, mem_out = inputs_back(info, d_mine, d_sent, mem_mine, m_sent, new_rows)
    home = swap(after(d_tokens_away, small_parts), 0, 2)
    parts, small_parts = after(parts, d_tokens), after(small_parts, d_tokens)
    for stage in stages[1:]:
        small_parts = sent(spread(added(small_parts, BF16), stage), stage)
    small_parts = after(small_parts, home)
    summed = added(parts, F32).reshape(-1, width)
    small = added(small_parts, F32).reshape(-1, CORE_WIDTH)
    big = [summed[cuts[k] : cuts[k + 1]] for k in range(len(sizes))]
    big[UP] = big[UP].reshape(CHUNKS, -1, width).transpose(1, 0, 2)
    small_attn = small[:cut_init].reshape(2, own_rows, CORE_WIDTH)
    small_init = small[cut_init:cut_gain].reshape(2, init_size)
    if init_rows % 2 == 0:
        small_init = small[cut_init:cut_gain].reshape(2, init_rows // 2, CORE_WIDTH)
    small_gain = small[cut_gain : cut_gain + GAIN_ROWS]
    if init_rows % 2 == 0:
        back = swap(
            jnp.concatenate(
                [pick(small_attn, 1 - core), pick(small_init, 1 - core), small_gain], axis=0
            ),
            0, 1,
        )
        init_back = back[own_rows : own_rows + init_rows // 2]
        gain_back = back[own_rows + init_rows // 2 :]
    else:
        back = swap(pick(small_attn, 1 - core), 0, 1)
        init_back = swap(pick(small_init, 1 - core), 0, 1)
        gain_back = swap(small_gain, 0, 1)
    attn_grad = by_core(core, pick(small_attn, core), back[:own_rows], axis=1)
    init_grad = (pick(small_init, core) + init_back).reshape(-1)
    device = lax.axis_index("batch") * lax.axis_size("seq") + rank
    gain_size = norm_gains.shape[0]
    gain_grad = lax.dynamic_slice_in_dim(
        (small_gain + gain_back).reshape(-1), device * gain_size, gain_size, 0
    )

    def at_home(both, new):
        return lax.dynamic_update_index_in_dim(both, new, 1 - chip, 0)

    mem_came = home[rows:]
    return (
        at_home(result, came),
        by_chip(chip, mem_out[slot_part:], mem_came[slot_part:]),
        at_home(d_tokens, home[:rows]),
        by_chip(chip, mem_out[:slot_part], mem_came[:slot_part]),
        attn_grad.reshape(-1),
        *[big[k].reshape(-1) for k in (OUT, UP, DOWN, WRITE, VALUE)],
        gain_grad,
        init_grad,
    )


def solution(mesh):
    rows = P("batch", "seq", None)
    table = P("batch", None)
    flat = P(("batch", "seq"))
    return jax.shard_map(
        per_device,
        mesh=mesh,
        in_specs=(rows, rows, table, table, *[flat] * 8, rows, rows),
        out_specs=(rows, rows, rows, rows, *[flat] * 8),
        check_vma=False,
    )
```

```python
import functools
import math

import jax
import jax.numpy as jnp
from jax import lax
from jax.experimental import pallas as pl
from jax.experimental.pallas import tpu as pltpu
from jax.sharding import PartitionSpec as P

HEADS = 8
HEAD_DIM = 64
FF = 2048
SEGMENT = 512
MASKED = -1e30
LANES = 128
CORE_HEADS = HEADS // 2
CORE_WIDTH = CORE_HEADS * HEAD_DIM
SCALE = HEAD_DIM ** (-0.5)
EXP = math.log2(math.e) * SCALE
LOG2E = math.log2(math.e)
RESET_COL = 8
LOG_COL = 10
NT = (((1,), (1,)), ((), ()))
NN = (((1,), (0,)), ((), ()))
TN = (((0,), (0,)), ((), ()))
GELU_A = math.sqrt(2.0 / math.pi)
GELU_B = 0.044715
BF16 = jnp.bfloat16
F32 = jnp.float32


def dot(left, right, dims=NN):
    return lax.dot_general(left, right, dims, preferred_element_type=F32)


def streamed(kernel, name, info, arrays, outs, scratch=(), grid=(1,), late=(), by_piece=False):
    arrays = [a if isinstance(a, tuple) else (a, a.shape, [((), ())]) for a in arrays]
    count = sum(len(pieces) for _, _, pieces in arrays)

    def at(ref, place):
        return ref.at[place] if place else ref

    def body(info, *refs):
        n, m = len(arrays), len(outs)
        far, far_out, refs = refs[:n], refs[n : n + m], refs[n + m :]
        near, near_out, refs = refs[:n], refs[n : n + m], refs[n + m :]
        own, sems, out_sems = refs[:-2], refs[-2], refs[-1]
        step = pl.program_id(0)
        copies = []
        for k, (_, _, pieces) in enumerate(arrays):
            first = sum(map(len, copies))
            copies.append(
                [
                    pltpu.make_async_copy(at(far[k], a), at(near[k], b), sems.at[first + j])
                    for j, (a, b) in enumerate(pieces)
                ]
            )

        @pl.when(step == 0)
        def _():
            ranked = [
                (100 * (k in late) + j * by_piece, k, j) for k in range(n) for j in range(len(copies[k]))
            ]
            for _, k, j in sorted(ranked):
                copies[k][j].start()

        def need(k, j=0, when=0):
            if when is None:
                copies[k][j].wait()
            else:
                pl.when(step == when)(copies[k][j].wait)

        def give(k, *place):
            pltpu.make_async_copy(
                at(near_out[k], place), at(far_out[k], place), out_sems.at[k]
            ).start()

        kernel(need, give, info, *near, *near_out, *own)

        @pl.when(step == pl.num_programs(0) - 1)
        def _():
            for k in range(m):
                pltpu.make_async_copy(near_out[k], far_out[k], out_sems.at[k]).wait()

    space = pl.BlockSpec(memory_space=pl.ANY)
    return pl.pallas_call(
        body,
        grid_spec=pltpu.PrefetchScalarGridSpec(
            num_scalar_prefetch=1,
            grid=grid,
            in_specs=[space] * len(arrays),
            out_specs=[space] * len(outs),
            scratch_shapes=[
                *[pltpu.VMEM(shape, array.dtype) for array, shape, _ in arrays],
                *[pltpu.VMEM(shape, kind) for shape, kind in outs],
                *scratch,
                pltpu.SemaphoreType.DMA((count,)),
                pltpu.SemaphoreType.DMA((len(outs),)),
            ],
        ),
        out_shape=[jax.ShapeDtypeStruct(shape, kind) for shape, kind in outs],
        compiler_params=pltpu.CompilerParams(vmem_limit_bytes=58 << 20),
        name=name,
    )(info, *[array for array, _, _ in arrays])


def norm_parts(values):
    centred = values - jnp.mean(values, axis=-1, keepdims=True)
    scale = lax.rsqrt(jnp.mean(centred * centred, axis=-1, keepdims=True) + 1e-05)
    return centred * scale, scale


def norm_back(unit, scale, grad, gain):
    back = grad * gain
    return scale * (
        back
        - jnp.mean(back, axis=-1, keepdims=True)
        - unit * jnp.mean(back * unit, axis=-1, keepdims=True)
    )


def in_three(values):
    high = values.astype(BF16).astype(F32)
    rest = values - high
    middle = rest.astype(BF16).astype(F32)
    return high, middle, rest - middle


def put_log(column, values, others):
    high, middle, low = in_three(values)
    out = jnp.where(column == LOG_COL, high, others)
    out = jnp.where(column == LOG_COL + 1, middle, out)
    return jnp.where(column == LOG_COL + 2, low, out)


def aux_column(shape, parity):
    lane = lax.broadcasted_iota(jnp.int32, shape, 1)
    return lane - (1 - parity) * HEAD_DIM


OWNERS = 32
OUT, VALUE, WRITE, DOWN, UP = range(5)
FIELDS = (16, 16, 32, 64, 64)
CUTS = tuple(sum(FIELDS[:k]) for k in range(len(FIELDS) + 1))
PACKED = CUTS[-1]
CHUNKS = 4
PART = FIELDS[UP] // CHUNKS


def flat_rows(block):
    return block.reshape(-1, block.shape[-1])


def take(packed, field):
    return flat_rows(packed[:, CUTS[field] : CUTS[field + 1], :])


def take_up(packed, chunk):
    if isinstance(chunk, int):
        at = CUTS[UP] + chunk * PART
    else:
        at = pl.multiple_of(CUTS[UP] + chunk * PART, PART)
    return flat_rows(packed[:, pl.ds(at, PART), :])


def take_down(packed, chunk):
    count = OWNERS // CHUNKS
    return flat_rows(packed[pl.ds(chunk * count, count), CUTS[DOWN] : CUTS[DOWN + 1], :])


def put(core, kept, away, value, owner, owners, at, rows):
    split = value.reshape(owners // 2, 2, rows, value.shape[-1])
    place = (pl.ds(owner, owners // 2), pl.ds(at, rows), slice(None))
    kept[place] = jnp.where(core == 0, split[:, 0], split[:, 1]).astype(BF16)
    away[place] = jnp.where(core == 0, split[:, 1], split[:, 0]).astype(BF16)


def by_head(out, place, pair, mine, side):
    lane = lax.broadcasted_iota(jnp.int32, mine.shape, 1)
    out[2 * pair, place, :] = jnp.where(lane < HEAD_DIM, mine, side).astype(BF16)
    out[2 * pair + 1, place, :] = jnp.where(lane < HEAD_DIM, side, mine).astype(BF16)


def choose(rank, core, chip, mine, recv, mine_other, recv_other):
    here = jnp.where(rank // 2 == chip, mine, recv)
    there = jnp.where(rank // 2 == chip, mine_other, recv_other)
    return jnp.where(rank % 2 == core, here, there)


def qkv_weight(packed, which):
    pairs = packed.shape[0]
    width = 2 * CORE_WIDTH
    rows = 3 * width // pairs
    if width % rows == 0:
        return flat_rows(packed[which * width // rows : (which + 1) * width // rows, :rows, :])
    return flat_rows(packed[:, :rows, :])[which * width : (which + 1) * width]


def project_step(
    need, give, info, rank, packed, init, gain, sources,
    q_out, k_out, v_out, normed_out, ks_out, vs_out, rows_out, tokens_out, scale_out, w_ref,
):
    core, chip = info[0], info[1]
    rows = normed_out.shape[0] // 4
    shape = (rows, LANES)
    column = lax.broadcasted_iota(jnp.int32, (1, LANES), 1) % HEAD_DIM

    @pl.when(rank == 0)
    def _():
        need(0)
        for which in range(3):
            w_ref[which] = qkv_weight(packed, which)
        for k in range(1, 7):
            need(k)
        slots = rows_out.shape[0]
        part = slots // 4
        for k in range(4):
            rows_out[k * part : (k + 1) * part, :] = choose(
                k, core, chip, *[ref[rows:, :] for ref in sources]
            )
        source = jnp.concatenate([rows_out[...], init[...]], axis=0)
        shape = (2 * slots, LANES)
        start = (lax.broadcasted_iota(jnp.int32, shape, 0) >= slots).astype(jnp.int32)
        ones = jnp.where((column >= LOG_COL) & (column < LOG_COL + 3), 1.0, 0.0)
        side = jnp.where(column == RESET_COL + start, MASKED, ones)
        keys = dot(source, w_ref[1])
        values = dot(source, w_ref[2])
        whole = slice(0, 2 * slots)
        for pair in range(CORE_HEADS // 2):
            lanes = slice(pair * LANES, (pair + 1) * LANES)
            by_head(ks_out, whole, pair, keys[:, lanes], side)
            by_head(vs_out, whole, pair, values[:, lanes], jnp.ones(shape, F32))
        for k in (KS, VS, ROWS):
            give(k)

    values = choose(rank, core, chip, *[ref[:rows, :] for ref in sources])

    @pl.when(rank % 2 == core)
    def _():
        tokens_out[rank // 2] = values
        give(TOKENS, rank // 2)

    unit, scale = norm_parts(values.astype(F32))
    normed = (unit * gain[0:1, :].astype(F32)).astype(BF16)
    place = pl.ds(pl.multiple_of(rank * rows, rows), rows)
    normed_out[place, :] = normed
    give(NORMED, place)
    scale_out[place, :] = jnp.broadcast_to(scale, (rows, LANES))
    give(SCALES, place)
    low = jnp.zeros((1, LANES), jnp.int32)
    high = jnp.zeros((1, LANES), jnp.int32)
    for k in range(8):
        low = jnp.where(column == k, info[1 + k] if k else 0, low)
        high = jnp.where(column == k, info[2 + k], high)
    reset = info[10 + (rank * rows) // SEGMENT]
    position = rank * rows + lax.broadcasted_iota(jnp.int32, shape, 0)
    here = (position >= low) & (position < high)
    fixed = jnp.where(column == RESET_COL + 1 - reset, 1.0, 0.0)
    q_side = jnp.where(here, 1.0, jnp.broadcast_to(fixed, shape))
    ones = jnp.where((column >= LOG_COL) & (column < LOG_COL + 3), 1.0, 0.0)
    others = jnp.where(column < 8, MASKED, ones)
    k_side = jnp.where(here, 0.0, jnp.broadcast_to(others, shape))
    for which, out, side in ((0, q_out, q_side), (1, k_out, k_side), (2, v_out, jnp.ones(shape, F32))):
        result = dot(normed, w_ref[which])
        for pair in range(CORE_HEADS // 2):
            by_head(out, place, pair, result[:, pair * LANES : (pair + 1) * LANES], side)


    @pl.when(rank == 3)
    def _():
        give(K)
        give(V)


Q_LOG, K, V, KS, VS, NORMED, TOKENS, ROWS, O, O_AWAY, SCALES, SHARES = range(12)
KEY_BLOCK = 256


def attend_step(block, give, info, head, q_ref, k_ref, v_ref, ks_ref, vs_ref, q_out, o_ref, away):
    core = info[0]
    length = q_ref.shape[1]
    rows = away.shape[2]
    pair, parity = head // 2, head % 2
    column = aux_column((block, LANES), parity)
    keep = (column < 0) | (column >= HEAD_DIM)
    row = lax.broadcasted_iota(jnp.int32, (block, block), 0)
    key = lax.broadcasted_iota(jnp.int32, (block, block), 1)
    for i in range(length // block):
        low, high = i * block, (i + 1) * block
        q = q_ref[head, low:high, :]
        slot = dot(q, ks_ref[head], NT)
        scores = dot(q, k_ref[head, :high, :], NT)
        last = jnp.where(row >= key, scores[:, low:], MASKED)
        scores = jnp.concatenate([scores[:, :low], last], axis=1) if i else last
        top = jnp.maximum(
            jnp.max(scores, axis=1, keepdims=True), jnp.max(slot, axis=1, keepdims=True)
        )
        share = jnp.exp2((scores - top) * EXP).astype(BF16)
        slot_share = jnp.exp2((slot - top) * EXP).astype(BF16)
        total = dot(share, v_ref[head, :high, :]) + dot(slot_share, vs_ref[head])
        count = jnp.where(parity == 0, total[:, HEAD_DIM : HEAD_DIM + 1], total[:, 0:1])
        o_ref[pair, low:high, :] = jnp.where(
            keep, (total / count).astype(BF16), o_ref[pair, low:high, :]
        )
        log = top + jnp.log2(count) * (1.0 / EXP)
        q_out[head, low:high, :] = put_log(column, -log, q.astype(F32)).astype(BF16)
    give(Q_LOG, head)

    @pl.when(parity == 1)
    def _():
        for rank in range(4):

            @pl.when(core != rank % 2)
            def _():
                away[rank // 2, pair] = o_ref[pair, rank * rows : (rank + 1) * rows, :]

        give(O, pair)
        give(O_AWAY, slice(None), pair)


def share_blocks(slots, length):
    return [(slots, length), *[(KEY_BLOCK, length - low) for low in range(0, length, KEY_BLOCK)]]


def shares_step(give, head, q_log, k_ref, ks_ref, shares):
    q = q_log[head]
    shares[0][head] = jnp.exp2(dot(ks_ref[head], q, NT) * EXP).astype(BF16)
    for j in range(len(shares) - 1):
        low = j * KEY_BLOCK
        scores = dot(k_ref[head, low : low + KEY_BLOCK, :], q[low:, :], NT)
        share = jnp.exp2(scores * EXP)
        key = lax.broadcasted_iota(jnp.int32, (KEY_BLOCK, KEY_BLOCK), 0)
        position = lax.broadcasted_iota(jnp.int32, (KEY_BLOCK, KEY_BLOCK), 1)
        first = jnp.where(key <= position, share[:, :KEY_BLOCK], 0.0)
        shares[j + 1][head, :, :KEY_BLOCK] = first.astype(BF16)
        if share.shape[1] > KEY_BLOCK:
            shares[j + 1][head, :, KEY_BLOCK:] = share[:, KEY_BLOCK:].astype(BF16)
    for j in range(len(shares)):
        give(SHARES + j, head)


def read_kernel(
    need, give, info, packed, init, gain, mine, recv, mine_other, recv_other,
    q_log, k, v, ks, vs, normed, tokens, rows, o, o_away, scales, *refs,
):
    shares, q, w_ref = refs[:-2], refs[-2], refs[-1]
    step = pl.program_id(0)

    @pl.when(step < 4)
    def _():
        project_step(
            need, give, info, step, packed, init, gain, (mine, recv, mine_other, recv_other),
            q, k, v, normed, ks, vs, rows, tokens, scales, w_ref,
        )

    @pl.when((step >= 4) & (step < 4 + CORE_HEADS))
    def _():
        attend_step(256, give, info, step - 4, q, k, v, ks, vs, q_log, o, o_away)

    @pl.when(step >= 4 + CORE_HEADS)
    def _():
        shares_step(give, step - 4 - CORE_HEADS, q_log, k, ks, shares)


def read(info, sources, packed, init, gains, rows):
    total, width = sources[0].shape
    slots = 4 * (total - rows)
    length = 4 * rows
    heads = ((CORE_HEADS, length, LANES), BF16)
    slot = ((CORE_HEADS, 2 * slots, LANES), BF16)
    return streamed(
        read_kernel, "read", info, (packed, init, gains, *sources),
        (heads, heads, heads, slot, slot, ((length, width), BF16), ((2, rows, width), BF16),
         ((slots, width), BF16), ((2, length, LANES), BF16), ((2, 2, rows, LANES), BF16), ((length, LANES), F32),
         *[((CORE_HEADS, *block), BF16) for block in share_blocks(2 * slots, length)]),
        [pltpu.VMEM((CORE_HEADS, length, LANES), BF16), pltpu.VMEM((3, width, CORE_WIDTH), BF16)],
        grid=(4 + 2 * CORE_HEADS,),
    )


def attend_back_kernel(
    qb, first_head, info, own_ref, other_ref, o_ref, q_ref, k_ref, v_ref, ks_ref, vs_ref, shares,
    dq_ref, dk_ref, dv_ref, dks_ref, dvs_ref, d_ref, acc_ref, wait=lambda _: None,
):
    length = q_ref.shape[1]
    step = pl.program_id(0)
    head = first_head + step
    pair, parity = head // 2, head % 2
    core = info[0]
    rows = own_ref.shape[2]
    column = aux_column((rows, LANES), parity)
    inside = (column < 0) | (column >= HEAD_DIM)
    for r in range(length // rows):
        low, high = r * rows, (r + 1) * rows
        d = jnp.where(core == r % 2, own_ref[r // 2, pair], other_ref[r // 2, pair]).astype(F32)
        delta = jnp.sum(
            jnp.where(inside, d * o_ref[pair, low:high, :].astype(F32), 0.0), axis=1, keepdims=True
        )
        d_ref[low:high, :] = jnp.where(
            inside, d, put_log(column, -delta, jnp.zeros_like(d))
        ).astype(BF16)
    acc_ref[...] = jnp.zeros_like(acc_ref)

    def tiles(k, v, shares, first):
        turned = k.astype(F32).T.astype(BF16)
        dk = jnp.zeros((k.shape[0], LANES), F32)
        dv = jnp.zeros((k.shape[0], LANES), F32)
        low = first
        while low < length:
            high = min((low // qb + 1) * qb, length)
            q = q_ref[step, low:high, :]
            d = d_ref[low:high, :]
            share = shares[step, :, low - first : high - first]
            ds = (share.astype(F32) * dot(v, d, NT)).astype(BF16)
            dv = dv + dot(share, d)
            dk = dk + dot(ds, q)
            acc_ref[:, low:high] += dot(turned, ds)
            low = high
        return dk, dv

    wait(0)
    dk, dv = tiles(ks_ref[step], vs_ref[step], shares[0], 0)
    dks_ref[step] = (dk * SCALE).astype(BF16)
    dvs_ref[step] = dv.astype(BF16)
    for j in range(len(shares) - 1):
        low = j * KEY_BLOCK
        place = slice(low, low + KEY_BLOCK)
        wait(j + 1)
        dk, dv = tiles(k_ref[step, place, :], v_ref[step, place, :], shares[j + 1], low)
        dk_ref[step, place, :] = (dk * SCALE).astype(BF16)
        dv_ref[step, place, :] = dv.astype(BF16)
    dq_ref[step] = (acc_ref[...].T * SCALE).astype(BF16)


def back_scratch(length):
    return [pltpu.VMEM((length, LANES), BF16), pltpu.VMEM((LANES, length), F32)]


def of_heads(array, first, heads):
    shape = (heads, *array.shape[1:])
    return array, shape, [((first + j,), (j,)) for j in range(heads)]


def of_pairs(array, axis, first, heads):
    before = (slice(None),) * axis
    pieces = [((*before, p),) * 2 for p in range(first // 2, (first + heads - 1) // 2 + 1)]
    return array, array.shape, pieces


def head_arrays(first, heads, q, k, v, ks, vs, shares, own, other, o):
    return [
        of_pairs(own, 1, first, heads), of_pairs(other, 1, first, heads),
        of_pairs(o, 0, first, heads),
        *[of_heads(array, first, heads) for array in (q, k, v, ks, vs, *shares)],
    ]


def need_heads(need, first, heads, arrays):
    for k in range(3):
        for j in range((first + heads - 1) // 2 - first // 2 + 1):
            need(k, j)
    for j in range(heads):

        @pl.when(pl.program_id(0) == j)
        def _():
            for k in range(3, arrays):
                need(k, j, None)


def some_heads_kernel(first, heads, need, give, info, *refs):
    count = len(refs) - 7
    wait = lambda _: None
    if heads == 1:
        for k in range(3):
            need(k, 0, None)

        def wait(j):
            for k in (8 + j,) if j else range(3, 9):
                need(k, 0, None)
    else:
        need_heads(need, first, heads, count)
    attend_back_kernel(1024, first, info, *refs[:8], refs[8:count], *refs[count:], wait=wait)
    for k in range(5):
        give(k, pl.program_id(0))


def attend_back(info, first, heads, q, k, v, ks, vs, shares, own, other, o):
    _, length, _ = q.shape
    out = ((heads, length, LANES), BF16)
    slot_out = ((heads, ks.shape[1], LANES), BF16)
    return streamed(
        functools.partial(some_heads_kernel, first, heads), "attend_back", info,
        head_arrays(first, heads, q, k, v, ks, vs, shares, own, other, o),
        (out, out, out, slot_out, slot_out), back_scratch(length), grid=(heads,),
        by_piece=True,
    )


def side_by_side(tiles):
    return jnp.concatenate(tiles, axis=1)


MIDDLE, NORMED_TWO, ACT, SLOPE, RESULT, KEYS, VALUES, AWAY, WQ, SK, SV, STATS = range(12)


def forward_kernel(
    need, give, info, own, other, tokens_ref, gains, packed, memory,
    middle_out, normed_out, act_out, slope_out, result_out, keys_out, values_out, away_out,
    query_out, key_out, value_out, stats,
):
    refs = (
        own, other, tokens_ref, gains, packed, memory, middle_out, normed_out, act_out, slope_out,
        result_out, keys_out, values_out, away_out,
    )
    step = pl.program_id(0)
    pl.when(step == 0)(lambda: forward_step(lambda k, j=0: need(k, j, None), give, info, *refs))
    pl.when(step > 0)(lambda: forward_step(lambda *_: None, give, info, *refs))

    @pl.when(step == pl.num_programs(0) - 1)
    def _():
        write_step(keys_out, values_out, memory, packed, query_out, key_out, value_out, stats)
        for k in (WQ, SK, SV, STATS):
            give(k)


def forward_step(
    need, give, info, own, other, tokens_ref, gains, packed, memory,
    middle_out, normed_out, act_out, slope_out, result_out, keys_out, values_out, away_out,
):
    core, chip = info[0], info[1]
    half = CORE_WIDTH // FIELDS[OUT]
    for k in range(4):
        need(k)
    need(4, FORWARD.index(OUT))
    w_own = flat_rows(packed[pl.ds(core * half, half), : FIELDS[OUT], :])
    w_other = flat_rows(packed[pl.ds((1 - core) * half, half), : FIELDS[OUT], :])
    step = pl.program_id(0)
    rows = normed_out.shape[1]
    block = 2 * rows // pl.num_programs(0)
    which, at = step // (rows // block), pl.multiple_of(step % (rows // block) * block, block)
    place = (which, pl.ds(at, block))
    tokens = tokens_ref[place]
    start = pl.multiple_of((2 * which + core) * rows + at, block)
    o_own = side_by_side([own[pair, pl.ds(start, block), :] for pair in range(2)])
    o_other = side_by_side([other[which, pair, pl.ds(at, block), :] for pair in range(2)])
    middle = tokens.astype(F32) + (dot(o_own, w_own) + dot(o_other, w_other))
    middle_out[place] = middle
    unit, _ = norm_parts(middle)
    normed = (unit * gains[1:2, :].astype(F32)).astype(BF16)
    normed_out[place] = normed
    width = normed.shape[1]
    for k in range(CHUNKS):
        need(4, FORWARD.index(UP + k))
        pre = dot(normed, take_up(packed, k))
        square = pre * pre
        half = 0.5 + 0.5 * jnp.tanh(pre * (GELU_A + (GELU_A * GELU_B) * square))
        turn = (half - half * half) * (2.0 * GELU_A + (6.0 * GELU_A * GELU_B) * square)
        act_out[(k, *place)] = (pre * half).astype(BF16)
        slope_out[(k, *place)] = (half + pre * turn).astype(BF16)
    acts = side_by_side([act_out[(k, *place)] for k in range(CHUNKS)])
    need(4, FORWARD.index(DOWN))
    low = (middle + dot(acts, take(packed, DOWN))).astype(BF16)
    result_out[place] = low

    @pl.when(which != chip)
    def _():
        away_out[pl.ds(at, block), :] = low
        give(AWAY, pl.ds(at, block))

    need(4, FORWARD.index(WRITE))
    need(4, FORWARD.index(VALUE))
    need(5)
    keys_out[place] = dot(low, flat_rows(packed[OWNERS // 2 :, CUTS[WRITE] : CUTS[WRITE + 1], :])).astype(BF16)
    values_out[place] = dot(low, take(packed, VALUE)).astype(BF16)


    for k in (MIDDLE, NORMED_TWO, RESULT, KEYS, VALUES):
        give(k, *place)
    for k in (ACT, SLOPE):
        give(k, slice(None), *place)


def fields_of(packed, order):
    cuts = [*CUTS[:UP], *[CUTS[UP] + k * PART for k in range(CHUNKS + 1)]]
    pieces = [(slice(None), slice(cuts[k], cuts[k + 1])) for k in order]
    return packed, packed.shape, [(piece, piece) for piece in pieces]


UPS = tuple(UP + k for k in range(CHUNKS))
FORWARD = (OUT, *UPS, DOWN, WRITE, VALUE)
BACKWARD = (WRITE, VALUE, DOWN, *UPS, OUT)


def forward(info, tokens, o, other, packed, gains, memory):
    _, rows, width = tokens.shape
    slots = memory.shape[0]
    small = ((2, rows, width), BF16)
    wide = ((CHUNKS, 2, rows, FF // CHUNKS), BF16)
    slot = ((slots, width), BF16)
    return streamed(
        forward_kernel, "feed_forward", info, (o, other, tokens, gains, fields_of(packed, FORWARD), memory),
        (((2, rows, width), F32), small, wide, wide, small, small, small, ((rows, width), BF16),
         slot, slot, slot, ((3, slots, width), F32)),
        grid=(4,),
    )


KEPT, SENT, D_MIDDLE, D_OWN, D_OTHER, G_GAIN, D_MEMORY, NEW_ROWS = range(8)


def backward_kernel(
    need, give, info, stats, stats_other, query, key, value, rows_ref, cot_mine, cot_recv,
    cot_other, keys, values, packed, result, normed, act, slope, middle, own, other, gains,
    kept, away, d_middle_out, d_own, d_other, g_gain, d_memory, new_out,
    d_keys, d_values, d_query, d_self_key, d_self_value, mem_cot,
    d_result_ref, d_update_ref, d_normed_ref,
):
    step = pl.program_id(0)
    core, chip = info[0], info[1]
    count, rows, width = result.shape
    total = count * rows
    half = CORE_WIDTH // FIELDS[OUT]

    @pl.when(step == 0)
    def _():
        for k in range(11):
            need(k)
        write_back_step(
            info, stats, stats_other, query, key, value, rows_ref, cot_mine, cot_recv, cot_other,
            keys, values, new_out, d_keys, d_values, d_query, d_self_key, d_self_value, mem_cot,
        )
        give(NEW_ROWS)
        need(11, BACKWARD.index(WRITE))
        need(11, BACKWARD.index(VALUE))
        need(12)

    @pl.when(step == 0)
    def _():
        dk = d_keys[...].reshape(total, width)
        dv = d_values[...].reshape(total, width)
        w_query = flat_rows(packed[: OWNERS // 2, CUTS[WRITE] : CUTS[WRITE + 1], :])
        w_key = flat_rows(packed[OWNERS // 2 :, CUTS[WRITE] : CUTS[WRITE + 1], :])
        w_value = take(packed, VALUE)
        first, second = cot_mine[:rows, :].astype(F32), cot_recv[:rows, :].astype(F32)
        cot = jnp.concatenate(
            [jnp.where(chip == 0, first, second), jnp.where(chip == 0, second, first)], axis=0
        )
        d_result = cot + (dot(dk, w_key, NT) + dot(dv, w_value, NT))
        d_result_ref[...] = d_result
        d_update_ref[...] = d_result.astype(BF16)
        d_normed_ref[...] = jnp.zeros_like(d_normed_ref)
        out = result[...].reshape(total, width)
        memory = rows_ref[...]
        put(core, kept, away, dot(memory, d_query[...], TN), 0, OWNERS // 2, CUTS[WRITE], FIELDS[WRITE])
        put(
            core, kept, away, dot(out, dk, TN) + dot(memory, d_self_key[...], TN),
            OWNERS // 4, OWNERS // 2, CUTS[WRITE], FIELDS[WRITE],
        )
        put(
            core, kept, away, dot(out, dv, TN) + dot(memory, d_self_value[...], TN),
            0, OWNERS, CUTS[VALUE], FIELDS[VALUE],
        )
        d_memory[...] = mem_cot[...] + (
            dot(d_query[...], w_query, NT)
            + dot(d_self_key[...], w_key, NT)
            + dot(d_self_value[...], w_value, NT)
        )
        give(D_MEMORY)
        for k in (SENT, KEPT):
            give(k, slice(None), slice(CUTS[VALUE], CUTS[WRITE + 1]))
        need(11, BACKWARD.index(DOWN))
        for k in range(CHUNKS):
            need(11, BACKWARD.index(UP + k))
        need(13)

    for j in range(CHUNKS):
        need(14, j, j)
        need(15, j, j)
    d_update = d_update_ref[...]
    d_act = dot(d_update, take_down(packed, step), NT)
    d_hidden = (d_act * slope[step].reshape(total, -1).astype(F32)).astype(BF16)
    g_down = dot(act[step].reshape(total, -1), d_update, TN)
    owners = OWNERS // CHUNKS
    put(core, kept, away, g_down, step * (owners // 2), owners, CUTS[DOWN], FIELDS[DOWN])
    g_up = dot(normed[...].reshape(total, width), d_hidden, TN)
    at = pl.multiple_of(CUTS[UP] + step * PART, PART)
    put(core, kept, away, g_up, 0, OWNERS, at, PART)
    for k in (SENT, KEPT):
        give(k, slice(None), pl.ds(at, PART))
        give(k, pl.ds(step * (owners // 2), owners // 2), slice(CUTS[DOWN], CUTS[DOWN + 1]))
    d_normed_ref[...] += dot(d_hidden, take_up(packed, step), NT)

    @pl.when(step == pl.num_programs(0) - 1)
    def _():
        for k in (16, 17, 18, 19):
            need(k, 0, CHUNKS - 1)
        need(11, BACKWARD.index(OUT), CHUNKS - 1)
        gain = gains[1:2, :].astype(F32)
        unit, scale = norm_parts(middle[...].reshape(total, width))
        d_normed = d_normed_ref[...]
        g_gain[...] = jnp.sum(d_normed * unit, axis=0, keepdims=True)
        d_middle = d_result_ref[...] + norm_back(unit, scale, d_normed, gain)
        d_middle_out[...] = d_middle.reshape(count, rows, width)
        give(D_MIDDLE)
        give(G_GAIN)
        d_branch = d_middle.astype(BF16)
        for start, out in ((core * half, d_own), ((1 - core) * half, d_other)):
            weight = flat_rows(packed[pl.ds(start, half), : FIELDS[OUT], :])
            back = dot(d_branch, weight, NT).astype(BF16)
            for k in range(count):
                for pair in range(2):
                    lanes = slice(pair * LANES, (pair + 1) * LANES)
                    out[k, pair] = back[k * rows : (k + 1) * rows, lanes]
        give(D_OWN)
        give(D_OTHER)
        own_rows = jnp.concatenate(
            [
                side_by_side(
                    [
                        own[pair, pl.ds(pl.multiple_of((2 * k + core) * rows, rows), rows), :]
                        for pair in range(2)
                    ]
                )
                for k in range(count)
            ],
            axis=0,
        )
        other_rows = jnp.concatenate([side_by_side([other[k, 0], other[k, 1]]) for k in range(count)], axis=0)
        g_own = dot(own_rows, d_branch, TN)
        g_other = dot(other_rows, d_branch, TN)
        put(core, kept, away, g_own, core * (half // 2), half, 0, FIELDS[OUT])
        put(core, kept, away, g_other, (1 - core) * (half // 2), half, 0, FIELDS[OUT])
        for k in (SENT, KEPT):
            give(k, slice(None), slice(CUTS[OUT], CUTS[OUT + 1]))


def by_chunk(array):
    return array, array.shape, [((j,), (j,)) for j in range(CHUNKS)]


def backward(info, stats, stats_other, writer, memory, cots, cot_other, keys, values, packed,
             result, normed, act, slope, middle, o, other, gains):
    _, rows, width = result.shape
    slots = memory.shape[0]
    grads = ((OWNERS // 2, PACKED, width), BF16)
    half = ((2, 2, rows, LANES), BF16)
    slot = pltpu.VMEM((slots, width), BF16)
    return streamed(
        backward_kernel, "feed_forward_back", info,
        (stats, stats_other, *writer, memory, *cots, cot_other, keys, values, fields_of(packed, BACKWARD),
         result, normed, by_chunk(act), by_chunk(slope), middle, o, other, gains),
        (grads, grads, ((2, rows, width), F32), half, half, ((1, width), F32),
         ((slots, width), F32), ((slots, width), BF16)),
        [pltpu.VMEM((2, rows, width), BF16), pltpu.VMEM((2, rows, width), BF16), slot, slot, slot,
         pltpu.VMEM((slots, width), F32),
         pltpu.VMEM((2 * rows, width), F32), pltpu.VMEM((2 * rows, width), BF16),
         pltpu.VMEM((2 * rows, width), F32)],
        grid=(CHUNKS,),
    )


def head_mask(shape, head):
    lane = lax.broadcasted_iota(jnp.int32, shape, 1)
    return (lane >= head * HEAD_DIM) & (lane < (head + 1) * HEAD_DIM)


def stacked_heads(values):
    return jnp.concatenate(
        [jnp.where(head_mask(values.shape, h), values, 0.0) for h in range(HEADS)], axis=0
    )


def joined_heads(stacked, slots):
    out = None
    for h in range(HEADS):
        part = stacked[h * slots : (h + 1) * slots, :]
        shape = (slots, HEADS * HEAD_DIM)
        part = jnp.broadcast_to(part, shape)
        out = part if out is None else jnp.where(head_mask(shape, h), part, out)
    return out


def column_of_heads(values):
    return jnp.concatenate(
        [values[:, h * HEAD_DIM : h * HEAD_DIM + 1] for h in range(HEADS)], axis=0
    )


def head_sums(values):
    return jnp.concatenate(
        [
            jnp.sum(jnp.where(head_mask(values.shape, h), values, 0.0), axis=1, keepdims=True)
            for h in range(HEADS)
        ],
        axis=0,
    )


def write_step(keys, values, memory, packed, query_out, key_out, value_out, stats):
    slots = memory.shape[0]
    total = keys.shape[0] * keys.shape[1]
    rows = memory[...]
    w_write = take(packed, WRITE)
    query = dot(rows, w_write[: w_write.shape[0] // 2]).astype(BF16)
    query_out[...] = query
    key_out[...] = dot(rows, w_write[w_write.shape[0] // 2 :]).astype(BF16)
    value_out[...] = dot(rows, take(packed, VALUE)).astype(BF16)
    stacked = stacked_heads(query.astype(F32)).astype(BF16)
    scores = dot(stacked, keys[...].reshape(total, -1), NT)
    top = jnp.max(scores, axis=1, keepdims=True)
    share = jnp.exp2((scores - top) * EXP)
    stats[0] = joined_heads(top, slots)
    stats[1] = joined_heads(jnp.sum(share, axis=1, keepdims=True), slots)
    stats[2] = joined_heads(dot(share.astype(BF16), values[...].reshape(total, -1)), slots)


def write_back_step(
    info, own, other, query, key, value, memory, cot_mine, cot_recv, cot_other, keys, values,
    new_out, d_keys, d_values, d_query, d_key, d_value, cot_out,
):
    core, chip = info[0], info[1]
    slots, width = memory.shape
    part = slots // 4
    rows = keys.shape[1]
    total = keys.shape[0] * rows
    sources = (cot_mine[rows:, :], cot_recv[rows:, :], cot_other[:part, :], cot_other[part:, :])
    cot = jnp.concatenate([choose(k, core, chip, *sources) for k in range(4)], axis=0).astype(F32)
    q = query[...].astype(F32)
    sk = key[...].astype(F32)
    sv = value[...].astype(F32)
    self_column = head_sums(q * sk)
    self_scores = joined_heads(self_column, slots)
    top = jnp.maximum(jnp.maximum(own[0], other[0]), self_scores)
    own_share = jnp.exp2((own[0] - top) * EXP)
    other_share = jnp.exp2((other[0] - top) * EXP)
    self_share = jnp.exp2((self_scores - top) * EXP)
    count = own[1] * own_share + other[1] * other_share + self_share
    written = (
        own[2] * own_share + other[2] * other_share + self_share.astype(BF16).astype(F32) * sv
    ) / count
    new_out[...] = (memory[...].astype(F32) + written).astype(BF16)
    log = top + jnp.log2(count) * (1.0 / EXP)
    log_column = column_of_heads(log)
    delta_column = head_sums(cot * written)
    delta = joined_heads(delta_column, slots)
    stacked = stacked_heads(q).astype(BF16)
    stacked_cot = stacked_heads(cot).astype(BF16)
    flat_keys = keys[...].reshape(total, width)
    share = jnp.exp2((dot(stacked, flat_keys, NT) - log_column) * EXP)
    d_share = dot(stacked_cot, values[...].reshape(total, width), NT)
    d_scores = (share * (d_share - delta_column)).astype(BF16)
    d_values[...] = dot(share.astype(BF16), stacked_cot, TN).astype(BF16).reshape(d_values.shape)
    d_keys[...] = (dot(d_scores, stacked, TN) * SCALE).astype(BF16).reshape(d_keys.shape)
    d_query_part = joined_heads(dot(d_scores, flat_keys), slots) * SCALE
    mine = (lax.broadcasted_iota(jnp.int32, (slots, width), 0) // part) % 2 == core
    self_probs = jnp.exp2((self_scores - log) * EXP)
    self_dp = joined_heads(head_sums(cot * sv), slots)
    self_ds = (self_probs * (self_dp - delta)).astype(BF16).astype(F32) * SCALE
    self_ds = jnp.where(mine, self_ds, 0.0)
    d_query[...] = (d_query_part + self_ds * sk).astype(BF16)
    d_key[...] = (self_ds * q).astype(BF16)
    d_value[...] = jnp.where(mine, self_probs.astype(BF16).astype(F32) * cot, 0.0).astype(BF16)
    cot_out[...] = jnp.where(mine, cot, 0.0)


def merged_heads(heads, place):
    tiles = [ref[k, place, :] for ref in heads for k in range(ref.shape[0])]
    lane = lax.broadcasted_iota(jnp.int32, tiles[0].shape, 1)
    return side_by_side(
        [jnp.where(lane < HEAD_DIM, tiles[2 * p], tiles[2 * p + 1]) for p in range(len(tiles) // 2)]
    )


def inputs_back_step(
    info, dq_parts, dk_parts, dv_parts, packed, normed, scales, gain, d_middle,
    mine_out, away_out, g_gain, merged,
):
    core = info[0]
    rows = mine_out.shape[1]
    weights = [qkv_weight(packed, k) for k in range(3)]
    gain = gain[0:1, :].astype(F32)
    gain_sum = None
    for rank in range(4):
        place = pl.ds(rank * rows, rows)
        total = None
        for k, parts in enumerate((dq_parts, dk_parts, dv_parts)):
            grads = merged_heads(parts, place)
            merged[k, place, :] = grads
            term = dot(grads, weights[k], NT)
            total = term if total is None else total + term
        unit = normed[place, :].astype(F32) * (1.0 / gain)
        part = jnp.sum(total * unit, axis=0, keepdims=True)
        gain_sum = part if gain_sum is None else gain_sum + part
        back = norm_back(unit, scales[place, 0:1], total, gain)

        @pl.when(core == rank % 2)
        def _():
            mine_out[rank // 2] = d_middle[rank // 2] + back

        @pl.when(core != rank % 2)
        def _():
            away_out[rank // 2] = back.astype(BF16)

    g_gain[...] = gain_sum


ATTN_ROWS, INIT_ROWS, GAIN_ROWS, SMALL_ROWS = 96, 8, 4, 112


def weights_back_step(
    info, normed, merged, packed, memory, init, d_memory, g_gain, g_gain_two, dks_parts, dvs_parts,
    small, d_mine, d_away, g_ref, misc,
):
    source = jnp.concatenate([memory[...], init[...]], axis=0)
    everything = slice(0, source.shape[0])
    dks = merged_heads(dks_parts, everything)
    dvs = merged_heads(dvs_parts, everything)
    d_slots = dot(dks, qkv_weight(packed, 1), NT) + dot(dvs, qkv_weight(packed, 2), NT)
    slots = memory.shape[0]
    part = slots // 4
    total = d_memory[...] + d_slots[:slots]
    for k in range(2):
        even = total[2 * k * part : (2 * k + 1) * part]
        odd = total[(2 * k + 1) * part : (2 * k + 2) * part]
        d_mine[k * part : (k + 1) * part, :] = jnp.where(info[0] == 0, even, odd)
        d_away[k * part : (k + 1) * part, :] = jnp.where(info[0] == 0, odd, even)
    rows = normed[...]
    width = rows.shape[1]
    g_ref[:width, :] = dot(rows, merged[0], TN).astype(BF16)
    g_ref[width : 2 * width, :] = (dot(rows, merged[1], TN) + dot(source, dks, TN)).astype(BF16)
    g_ref[2 * width :, :] = (dot(rows, merged[2], TN) + dot(source, dvs, TN)).astype(BF16)
    pairs = OWNERS // 2
    small[:, :ATTN_ROWS, :] = g_ref[...].reshape(pairs, ATTN_ROWS, CORE_WIDTH)
    misc[...] = jnp.zeros_like(misc)
    each = slots // pairs
    for h in range(2):
        lanes = slice(h * CORE_WIDTH, (h + 1) * CORE_WIDTH)
        for k in range(slots):
            misc[k // each, 2 * (k % each) + h : 2 * (k % each) + h + 1, :] = d_slots[
                slots + k : slots + k + 1, lanes
            ]
        for k, gain in enumerate((g_gain, g_gain_two)):
            at = INIT_ROWS + 2 * k + h
            misc[:, at : at + 1, :] = jnp.broadcast_to(gain[:, lanes][None], (pairs, 1, CORE_WIDTH))
    small[:, ATTN_ROWS:, :] = misc[...].astype(BF16)


def last_heads_kernel(first, count, arrays, need, give, info, *refs):
    heads, refs = refs[:arrays], refs[arrays:]
    packed, refs = refs[0], refs[1:]
    earlier, refs = refs[:5], refs[5:]
    normed, scales, gain, d_middle, memory, init, d_memory, g_gain_two, refs = *refs[:8], refs[8:]
    d_mine, d_away, small, m_mine, m_away, refs = *refs[:5], refs[5:]
    results, merged, g_gain, g_ref, misc, scratch = refs[:5], *refs[5:9], refs[9:]
    need_heads(need, first, count, arrays)
    attend_back_kernel(1024, first, info, *heads[:8], heads[8:], *results, *scratch)

    @pl.when(pl.program_id(0) == pl.num_programs(0) - 1)
    def _():
        for k in range(arrays, arrays + 14):
            need(k, 0, pl.num_programs(0) - 1)
        parts = [(earlier[k], results[k]) for k in range(5)]
        inputs_back_step(
            info, *parts[:3], packed, normed, scales, gain, d_middle, d_mine, d_away, g_gain, merged
        )
        for k in range(2):
            give(k)
        weights_back_step(
            info, normed, merged, packed, memory, init, d_memory, g_gain, g_gain_two, *parts[3:],
            small, m_mine, m_away, g_ref, misc,
        )
        for k in range(2, 5):
            give(k)


def last_heads(info, first, heads, q, k, v, ks, vs, shares, own, other, o, packed, earlier,
               normed, scales, gains, d_middle, memory, init, d_memory, g_gain_two):
    length, width = normed.shape
    slots = memory.shape[0]
    part = (d_middle.shape, F32)
    away = (d_middle.shape, BF16)
    half = ((slots // 2, width), F32)
    out = pltpu.VMEM((heads, length, LANES), BF16)
    slot_out = pltpu.VMEM((heads, ks.shape[1], LANES), BF16)
    count = 8 + len(shares)
    return streamed(
        functools.partial(last_heads_kernel, first, heads, count), "last_heads", info,
        (*head_arrays(first, heads, q, k, v, ks, vs, shares, own, other, o), packed, *earlier,
         normed, scales, gains, d_middle, memory, init, d_memory, g_gain_two),
        (part, away, ((OWNERS // 2, SMALL_ROWS, CORE_WIDTH), BF16), half, half),
        [out, out, out, slot_out, slot_out, pltpu.VMEM((3, length, CORE_WIDTH), BF16),
         pltpu.VMEM((1, width), F32), pltpu.VMEM((3 * width, CORE_WIDTH), BF16),
         pltpu.VMEM((OWNERS // 2, SMALL_ROWS - ATTN_ROWS, CORE_WIDTH), F32), *back_scratch(length)],
        grid=(heads,), late=range(count, count + 14), by_piece=True,
    )


def inputs_back_kernel(
    need, give, info, mine, other, mem_mine, mem_other, new_rows, d_out, away_out, mem_out
):
    core, chip = info[0], info[1]
    count, rows, _ = mine.shape
    for k in range(count):
        need(0, k)
        need(1, k)
        back = (mine[k] + other[k].astype(F32)).astype(BF16)
        d_out[k] = back
        give(0, k)

        @pl.when(chip != k)
        def _():
            away_out[:rows, :] = back

    for j in range(2, 5):
        need(j)
    part = mem_mine.shape[0] // 2
    grads = (mem_mine[...] + mem_other[...]).astype(BF16)
    news = [
        jnp.where(
            core == 0,
            new_rows[2 * k * part : (2 * k + 1) * part, :],
            new_rows[(2 * k + 1) * part : (2 * k + 2) * part, :],
        )
        for k in range(2)
    ]
    first, second = grads[:part], grads[part:]
    mem_out[:part, :] = jnp.where(chip == 0, first, second)
    mem_out[part:, :] = jnp.where(chip == 0, news[0], news[1])
    away_out[rows : rows + part, :] = jnp.where(chip == 0, second, first)
    away_out[rows + part :, :] = jnp.where(chip == 0, news[1], news[0])
    for k in (1, 2):
        give(k)


def inputs_back(info, mine, other, mem_mine, mem_other, new_rows):
    _, rows, width = mine.shape
    slots = new_rows.shape[0]
    halves = [(array, array.shape, [((j,), (j,)) for j in range(2)]) for array in (mine, other)]
    return streamed(
        inputs_back_kernel, "inputs_back", info, (*halves, mem_mine, mem_other, new_rows),
        ((mine.shape, BF16), ((rows + slots // 2, width), BF16), ((slots // 2, width), BF16)),
    )


def swap(value, over_batch, over_seq):
    batch, seq = lax.axis_size("batch"), lax.axis_size("seq")
    pairs = [
        (i * seq + j, (i ^ over_batch) * seq + (j ^ over_seq))
        for i in range(batch)
        for j in range(seq)
    ]
    return lax.ppermute(value, ("batch", "seq"), pairs)


def chip_groups():
    batch = lax.axis_index("batch")
    chip = lax.axis_index("seq") // 2
    stages = [(4, 2 * (batch & 1) + chip, lambda k: (k >> 1, 2 * (k & 1)))]
    bits = lax.axis_size("batch").bit_length() - 1
    at = 1
    while at < bits:
        count = min(2, bits - at)
        stages.append(
            (1 << count, (batch >> at) & ((1 << count) - 1), lambda k, at=at: (k << at, 0))
        )
        at += count
    return stages


def in_order(pieces, own):
    bit = 1
    while bit < len(pieces):
        turned = (own & bit) > 0
        pieces = [jnp.where(turned, pieces[k ^ bit], pieces[k]) for k in range(len(pieces))]
        bit *= 2
    return jnp.stack(pieces)


def gather_chips(piece):
    stages = chip_groups()
    shape = piece.shape
    for size, own, peer in reversed(stages):
        piece = in_order([piece] + [swap(piece, *peer(k)) for k in range(1, size)], own)
    count = len(stages)
    piece = piece.transpose(*reversed(range(count)), *range(count, piece.ndim))
    return piece.reshape(-1, *shape)


def square_groups():
    batch, seq = lax.axis_size("batch"), lax.axis_size("seq")
    return [
        [(2 * r + y) * seq + 2 * x + core for y in range(2) for x in range(2)]
        for r in range(batch // 2)
        for core in range(2)
    ]


def line_groups():
    batch, seq = lax.axis_size("batch"), lax.axis_size("seq")
    return [
        [(2 * r + y) * seq + s for r in range(batch // 2)] for y in range(2) for s in range(seq)
    ]


def sent_lines(rows, stages):
    parts = [rows]
    for stage in stages[1:]:
        parts = sent(spread(added(parts, BF16), stage), stage)
    return parts


def sum_scattered(rows, groups):
    return lax.psum_scatter(
        rows, ("batch", "seq"), scatter_dimension=0, tiled=True, axis_index_groups=groups
    )


def spread(pieces, stage):
    size, own, _ = stage
    pieces = pieces.reshape(-1, size, *pieces.shape[-2:])
    return [lax.dynamic_index_in_dim(pieces, own ^ j, 1, keepdims=False) for j in range(size)]


def sent(parts, stage):
    size, _, peer = stage
    return [parts[0]] + [swap(parts[j], *peer(j)) for j in range(1, size)]


def added(parts, kind):
    total = parts[0].astype(F32)
    for part in parts[1:]:
        total = total + part.astype(F32)
    return total.astype(kind)


def after(values, *others):
    return lax.optimization_barrier((values, others))[0]


def by_core(core, mine, other, axis=0):
    return jnp.where(
        core == 0,
        jnp.concatenate([mine, other], axis=axis),
        jnp.concatenate([other, mine], axis=axis),
    )


def by_chip(chip, mine, other):
    return jnp.where(chip == 0, jnp.stack([mine, other]), jnp.stack([other, mine]))


def pick(array, index, axis=0):
    return lax.dynamic_index_in_dim(array, index, axis, keepdims=False)


def to_owners(fields, devices):
    many = devices // OWNERS
    out = []
    for k, field in enumerate(fields):
        if many > 1:
            groups = CHUNKS if k == UP else 1
            field = field.reshape(OWNERS, many, groups, -1, field.shape[-1])
            field = field.transpose(0, 2, 1, 3, 4).reshape(OWNERS, -1, field.shape[-1])
        out.append(field)
    return jnp.concatenate(out, axis=1)


def from_owners(packed, devices):
    many = devices // OWNERS
    out = []
    for k in range(len(FIELDS)):
        field = packed[:, CUTS[k] : CUTS[k + 1]]
        groups = CHUNKS if k == UP else 1
        field = field.reshape(OWNERS, groups, many, -1, field.shape[-1])
        out.append(field.transpose(0, 2, 1, 3, 4).reshape(devices, -1, field.shape[-1]))
    return jnp.concatenate(out, axis=1)


def per_device(
    tokens, memory, lengths, resets, attn_in, attn_out, ffn_in, ffn_out, writer_in, writer_value,
    norm_gains, memory_init, out_cotangent, memory_cotangent,
):
    _, rows, width = tokens.shape
    devices = lax.axis_size("batch") * lax.axis_size("seq")
    rank = lax.axis_index("seq")
    chip, core = rank // 2, rank % 2
    slot_part = memory.shape[1]
    slots = 4 * slot_part
    stages = chip_groups()

    ends = jnp.cumsum(pick(lengths, chip))
    info = jnp.concatenate([jnp.stack([core, chip]), ends, pick(resets, chip)]).astype(jnp.int32)

    def to_chip(big, small):
        mine = jnp.concatenate([pick(big, chip), pick(small, chip)], axis=0)
        away = jnp.concatenate([pick(big, 1 - chip), pick(small, 1 - chip)], axis=0)
        return mine, swap(away, 0, 2)

    misc = jnp.concatenate([memory_init, norm_gains])
    misc_rows = -(-misc.shape[0] // CORE_WIDTH)
    misc = jnp.pad(misc, (0, misc_rows * CORE_WIDTH - misc.shape[0])).reshape(misc_rows, CORE_WIDTH)
    attn_rows = attn_in.reshape(-1, 2, CORE_WIDTH)
    own_rows = attn_rows.shape[0]
    mine = jnp.concatenate([pick(attn_rows, core, 1), misc], axis=0)
    theirs = swap(jnp.concatenate([pick(attn_rows, 1 - core, 1), misc], axis=0), 0, 1)
    piece = jnp.concatenate(
        [
            by_core(core, mine[:own_rows], theirs[:own_rows]),
            by_core(core, mine[own_rows:], theirs[own_rows:]),
        ],
        axis=0,
    )
    gathered = gather_chips(piece)
    misc = gathered[:, 2 * own_rows :].reshape(devices, -1)
    init = misc[:, : memory_init.shape[0]].reshape(slots, width)
    gains = misc[:, memory_init.shape[0] :][:, : norm_gains.shape[0]].reshape(2, width)
    w_qkv = gathered
    if devices != OWNERS:
        w_qkv = gathered[:, : 2 * own_rows].reshape(OWNERS // 2, -1, CORE_WIDTH)

    columns = ffn_in.reshape(-1, CHUNKS, width).transpose(1, 0, 2).reshape(-1, width)
    fields = [attn_out, writer_value, writer_in, ffn_out, ffn_in]
    sizes = [field.shape[0] // width for field in fields]
    parts = [jnp.concatenate(fields[:UP]).reshape(-1, width), columns]
    cuts = [sum(sizes[:k]) for k in range(len(sizes) + 1)]
    packed = lax.all_gather(jnp.concatenate(parts, axis=0), ("batch", "seq"), axis=0)
    if devices != OWNERS:
        packed = to_owners([packed[:, cuts[k] : cuts[k + 1]] for k in range(len(sizes))], devices)

    own, recv = to_chip(tokens, memory)
    sources = (own, recv, swap(own, 0, 1), swap(recv, 0, 1))
    q_log, k, v, ks, vs, normed, own_tokens, mem_rows, o, o_away, scales, *shares = read(
        info, sources, w_qkv, init, gains, rows
    )
    out_cotangent, memory_cotangent = after((out_cotangent, memory_cotangent), recv)
    cots = to_chip(out_cotangent, memory_cotangent)
    cot_other = swap(jnp.concatenate([cot[rows:] for cot in after(cots, o)], axis=0), 0, 1)
    o_other = swap(o_away, 0, 1)
    middle, normed_two, act, slope, result, keys, values, result_away, *writer, stats = forward(
        info, own_tokens, o, o_other, packed, gains, mem_rows
    )
    came = swap(result_away, 0, 2)
    stats_other = swap(stats, 0, 1)
    kept, away, d_middle, d_own, d_away, g_gain_two, d_memory, new_rows = backward(
        info, stats, stats_other, writer, mem_rows, cots, cot_other, keys, values, packed, result,
        normed_two, act, slope, middle, o, o_other, gains,
    )
    d_other, came = after((swap(d_away, 0, 1), came), came)
    if devices != OWNERS:
        both = by_core(core, kept[:, None], away[:, None], axis=1).reshape(OWNERS, PACKED, width)
        both = from_owners(both, devices).reshape(devices // 2, 2, -1, width)
        kept, away = pick(both, core, 1), pick(both, 1 - core, 1)
    arrived = swap(after(away, d_other), 0, 1)

    heads = (q_log, k, v, ks, vs, shares)
    grads_a = attend_back(info, 0, 1, *heads, d_own, d_other, o)
    kept, arrived = after((kept, arrived), grads_a)
    square = [
        added(pair, BF16) for pair in zip(spread(kept, stages[0])[1:], spread(arrived, stages[0])[1:])
    ]
    d_own = after(d_own, square)
    square = [swap(part, *stages[0][2](k + 1)) for k, part in enumerate(square)]
    d_mine, d_away, small, mem_mine, mem_away = last_heads(
        info, 1, 3, *heads, d_own, d_other, o, w_qkv, grads_a, normed, scales, gains,
        d_middle, mem_rows, init, d_memory, g_gain_two,
    )
    d_sent = swap(d_away, 0, 1)
    m_sent = swap(mem_away, 0, 1)

    init_size = memory_init.shape[0]
    init_rows = 2 * init_size // CORE_WIDTH
    cut_init, cut_gain = 2 * own_rows, 2 * own_rows + init_rows
    if devices != OWNERS:
        pairs = devices // 2
        small = jnp.concatenate(
            [
                small[:, :ATTN_ROWS].reshape(pairs, -1, CORE_WIDTH),
                small[:, ATTN_ROWS : ATTN_ROWS + INIT_ROWS].reshape(pairs, -1, CORE_WIDTH),
                jnp.repeat(small[:, ATTN_ROWS + INIT_ROWS :], pairs // (OWNERS // 2), axis=0),
            ],
            axis=1,
        )
    small_parts = sent(spread(small, stages[0]), stages[0])
    square, kept, arrived = after((square, kept, arrived), small)
    own = [spread(array, stages[0])[0] for array in (kept, arrived)]
    parts = sent_lines(added(own + square, BF16), stages)
    d_sent = after(d_sent, parts[0])
    d_tokens, d_tokens_away, mem_out = inputs_back(info, d_mine, d_sent, mem_mine, m_sent, new_rows)
    home = swap(after(d_tokens_away, small_parts), 0, 2)
    parts, small_parts = after(parts, d_tokens), after(small_parts, d_tokens)
    result, came = after((result, came), small_parts)
    for stage in stages[1:]:
        small_parts = sent(spread(added(small_parts, BF16), stage), stage)
    small_parts = after(small_parts, home)
    summed = added(parts, F32).reshape(-1, width)
    small = added(small_parts, F32).reshape(-1, CORE_WIDTH)
    big = [summed[cuts[k] : cuts[k + 1]] for k in range(len(sizes))]
    big[UP] = big[UP].reshape(CHUNKS, -1, width).transpose(1, 0, 2)
    small_attn = small[:cut_init].reshape(2, own_rows, CORE_WIDTH)
    small_init = small[cut_init:cut_gain].reshape(2, init_size)
    if init_rows % 2 == 0:
        small_init = small[cut_init:cut_gain].reshape(2, init_rows // 2, CORE_WIDTH)
    small_gain = small[cut_gain : cut_gain + GAIN_ROWS]
    if init_rows % 2 == 0:
        back = swap(
            jnp.concatenate(
                [pick(small_attn, 1 - core), pick(small_init, 1 - core), small_gain], axis=0
            ),
            0, 1,
        )
        init_back = back[own_rows : own_rows + init_rows // 2]
        gain_back = back[own_rows + init_rows // 2 :]
    else:
        back = swap(pick(small_attn, 1 - core), 0, 1)
        init_back = swap(pick(small_init, 1 - core), 0, 1)
        gain_back = swap(small_gain, 0, 1)
    attn_grad = by_core(core, pick(small_attn, core), back[:own_rows], axis=1)
    init_grad = (pick(small_init, core) + init_back).reshape(-1)
    device = lax.axis_index("batch") * lax.axis_size("seq") + rank
    gain_size = norm_gains.shape[0]
    gain_grad = lax.dynamic_slice_in_dim(
        (small_gain + gain_back).reshape(-1), device * gain_size, gain_size, 0
    )

    def at_home(both, new):
        return lax.dynamic_update_index_in_dim(both, new, 1 - chip, 0)

    mem_came = home[rows:]
    return (
        at_home(result, came),
        by_chip(chip, mem_out[slot_part:], mem_came[slot_part:]),
        at_home(d_tokens, home[:rows]),
        by_chip(chip, mem_out[:slot_part], mem_came[:slot_part]),
        attn_grad.reshape(-1),
        *[big[k].reshape(-1) for k in (OUT, UP, DOWN, WRITE, VALUE)],
        gain_grad,
        init_grad,
    )


def solution(mesh):
    rows = P("batch", "seq", None)
    table = P("batch", None)
    flat = P(("batch", "seq"))
    return jax.shard_map(
        per_device,
        mesh=mesh,
        in_specs=(rows, rows, table, table, *[flat] * 8, rows, rows),
        out_specs=(rows, rows, rows, rows, *[flat] * 8),
        check_vma=False,
    )
```

```python
import functools
import math

import jax
import jax.numpy as jnp
from jax import lax
from jax.experimental import pallas as pl
from jax.experimental.pallas import tpu as pltpu
from jax.sharding import PartitionSpec as P

HEADS = 8
HEAD_DIM = 64
FF = 2048
SEGMENT = 512
MASKED = -1e30
LANES = 128
CORE_HEADS = HEADS // 2
CORE_WIDTH = CORE_HEADS * HEAD_DIM
SCALE = HEAD_DIM ** (-0.5)
EXP = math.log2(math.e) * SCALE
LOG2E = math.log2(math.e)
RESET_COL = 8
LOG_COL = 10
NT = (((1,), (1,)), ((), ()))
NN = (((1,), (0,)), ((), ()))
TN = (((0,), (0,)), ((), ()))
GELU_A = math.sqrt(2.0 / math.pi)
GELU_B = 0.044715
BF16 = jnp.bfloat16
F32 = jnp.float32


def dot(left, right, dims=NN):
    return lax.dot_general(left, right, dims, preferred_element_type=F32)


def streamed(kernel, name, info, arrays, outs, scratch=(), grid=(1,), late=(), by_piece=False):
    arrays = [a if isinstance(a, tuple) else (a, a.shape, [((), ())]) for a in arrays]
    count = sum(len(pieces) for _, _, pieces in arrays)

    def at(ref, place):
        return ref.at[place] if place else ref

    def body(info, *refs):
        n, m = len(arrays), len(outs)
        far, far_out, refs = refs[:n], refs[n : n + m], refs[n + m :]
        near, near_out, refs = refs[:n], refs[n : n + m], refs[n + m :]
        own, sems, out_sems = refs[:-2], refs[-2], refs[-1]
        step = pl.program_id(0)
        copies = []
        for k, (_, _, pieces) in enumerate(arrays):
            first = sum(map(len, copies))
            copies.append(
                [
                    pltpu.make_async_copy(at(far[k], a), at(near[k], b), sems.at[first + j])
                    for j, (a, b) in enumerate(pieces)
                ]
            )

        @pl.when(step == 0)
        def _():
            ranked = [
                (100 * (k in late) + j * by_piece, k, j) for k in range(n) for j in range(len(copies[k]))
            ]
            for _, k, j in sorted(ranked):
                copies[k][j].start()

        def need(k, j=0, when=0):
            if when is None:
                copies[k][j].wait()
            else:
                pl.when(step == when)(copies[k][j].wait)

        def give(k, *place):
            pltpu.make_async_copy(
                at(near_out[k], place), at(far_out[k], place), out_sems.at[k]
            ).start()

        kernel(need, give, info, *near, *near_out, *own)

        @pl.when(step == pl.num_programs(0) - 1)
        def _():
            for k in range(m):
                pltpu.make_async_copy(near_out[k], far_out[k], out_sems.at[k]).wait()

    space = pl.BlockSpec(memory_space=pl.ANY)
    return pl.pallas_call(
        body,
        grid_spec=pltpu.PrefetchScalarGridSpec(
            num_scalar_prefetch=1,
            grid=grid,
            in_specs=[space] * len(arrays),
            out_specs=[space] * len(outs),
            scratch_shapes=[
                *[pltpu.VMEM(shape, array.dtype) for array, shape, _ in arrays],
                *[pltpu.VMEM(shape, kind) for shape, kind in outs],
                *scratch,
                pltpu.SemaphoreType.DMA((count,)),
                pltpu.SemaphoreType.DMA((len(outs),)),
            ],
        ),
        out_shape=[jax.ShapeDtypeStruct(shape, kind) for shape, kind in outs],
        compiler_params=pltpu.CompilerParams(vmem_limit_bytes=58 << 20),
        name=name,
    )(info, *[array for array, _, _ in arrays])


def norm_parts(values):
    centred = values - jnp.mean(values, axis=-1, keepdims=True)
    scale = lax.rsqrt(jnp.mean(centred * centred, axis=-1, keepdims=True) + 1e-05)
    return centred * scale, scale


def norm_back(unit, scale, grad, gain):
    back = grad * gain
    return scale * (
        back
        - jnp.mean(back, axis=-1, keepdims=True)
        - unit * jnp.mean(back * unit, axis=-1, keepdims=True)
    )


def in_three(values):
    high = values.astype(BF16).astype(F32)
    rest = values - high
    middle = rest.astype(BF16).astype(F32)
    return high, middle, rest - middle


def put_log(column, values, others):
    high, middle, low = in_three(values)
    out = jnp.where(column == LOG_COL, high, others)
    out = jnp.where(column == LOG_COL + 1, middle, out)
    return jnp.where(column == LOG_COL + 2, low, out)


def aux_column(shape, parity):
    lane = lax.broadcasted_iota(jnp.int32, shape, 1)
    return lane - (1 - parity) * HEAD_DIM


OWNERS = 32
OUT, VALUE, WRITE, DOWN, UP = range(5)
FIELDS = (16, 16, 32, 64, 64)
CUTS = tuple(sum(FIELDS[:k]) for k in range(len(FIELDS) + 1))
PACKED = CUTS[-1]
CHUNKS = 4
PART = FIELDS[UP] // CHUNKS


def flat_rows(block):
    return block.reshape(-1, block.shape[-1])


def take(packed, field):
    return flat_rows(packed[:, CUTS[field] : CUTS[field + 1], :])


def take_up(packed, chunk):
    if isinstance(chunk, int):
        at = CUTS[UP] + chunk * PART
    else:
        at = pl.multiple_of(CUTS[UP] + chunk * PART, PART)
    return flat_rows(packed[:, pl.ds(at, PART), :])


def take_down(packed, chunk):
    count = OWNERS // CHUNKS
    return flat_rows(packed[pl.ds(chunk * count, count), CUTS[DOWN] : CUTS[DOWN + 1], :])


def put(core, kept, away, value, owner, owners, at, rows):
    split = value.reshape(owners // 2, 2, rows, value.shape[-1])
    place = (pl.ds(owner, owners // 2), pl.ds(at, rows), slice(None))
    kept[place] = jnp.where(core == 0, split[:, 0], split[:, 1]).astype(BF16)
    away[place] = jnp.where(core == 0, split[:, 1], split[:, 0]).astype(BF16)


def by_head(out, place, pair, mine, side):
    lane = lax.broadcasted_iota(jnp.int32, mine.shape, 1)
    out[2 * pair, place, :] = jnp.where(lane < HEAD_DIM, mine, side).astype(BF16)
    out[2 * pair + 1, place, :] = jnp.where(lane < HEAD_DIM, side, mine).astype(BF16)


def choose(rank, core, chip, mine, recv, mine_other, recv_other):
    here = jnp.where(rank // 2 == chip, mine, recv)
    there = jnp.where(rank // 2 == chip, mine_other, recv_other)
    return jnp.where(rank % 2 == core, here, there)


def qkv_weight(packed, which):
    pairs = packed.shape[0]
    width = 2 * CORE_WIDTH
    rows = 3 * width // pairs
    if width % rows == 0:
        return flat_rows(packed[which * width // rows : (which + 1) * width // rows, :rows, :])
    return flat_rows(packed[:, :rows, :])[which * width : (which + 1) * width]


def project_step(
    need, give, info, rank, packed, init, gain, sources,
    q_out, k_out, v_out, normed_out, ks_out, vs_out, rows_out, tokens_out, scale_out, w_ref,
):
    core, chip = info[0], info[1]
    rows = normed_out.shape[0] // 4
    shape = (rows, LANES)
    column = lax.broadcasted_iota(jnp.int32, (1, LANES), 1) % HEAD_DIM

    @pl.when(rank == 0)
    def _():
        need(0)
        for which in range(3):
            w_ref[which] = qkv_weight(packed, which)
        for k in range(1, 7):
            need(k)
        slots = rows_out.shape[0]
        part = slots // 4
        for k in range(4):
            rows_out[k * part : (k + 1) * part, :] = choose(
                k, core, chip, *[ref[rows:, :] for ref in sources]
            )
        source = jnp.concatenate([rows_out[...], init[...]], axis=0)
        shape = (2 * slots, LANES)
        start = (lax.broadcasted_iota(jnp.int32, shape, 0) >= slots).astype(jnp.int32)
        ones = jnp.where((column >= LOG_COL) & (column < LOG_COL + 3), 1.0, 0.0)
        side = jnp.where(column == RESET_COL + start, MASKED, ones)
        keys = dot(source, w_ref[1])
        values = dot(source, w_ref[2])
        whole = slice(0, 2 * slots)
        for pair in range(CORE_HEADS // 2):
            lanes = slice(pair * LANES, (pair + 1) * LANES)
            by_head(ks_out, whole, pair, keys[:, lanes], side)
            by_head(vs_out, whole, pair, values[:, lanes], jnp.ones(shape, F32))
        for k in (KS, VS, ROWS):
            give(k)

    values = choose(rank, core, chip, *[ref[:rows, :] for ref in sources])

    @pl.when(rank % 2 == core)
    def _():
        tokens_out[rank // 2] = values
        give(TOKENS, rank // 2)

    unit, scale = norm_parts(values.astype(F32))
    normed = (unit * gain[0:1, :].astype(F32)).astype(BF16)
    place = pl.ds(pl.multiple_of(rank * rows, rows), rows)
    normed_out[place, :] = normed
    give(NORMED, place)
    scale_out[place, :] = jnp.broadcast_to(scale, (rows, LANES))
    give(SCALES, place)
    low = jnp.zeros((1, LANES), jnp.int32)
    high = jnp.zeros((1, LANES), jnp.int32)
    for k in range(8):
        low = jnp.where(column == k, info[1 + k] if k else 0, low)
        high = jnp.where(column == k, info[2 + k], high)
    reset = info[10 + (rank * rows) // SEGMENT]
    position = rank * rows + lax.broadcasted_iota(jnp.int32, shape, 0)
    here = (position >= low) & (position < high)
    fixed = jnp.where(column == RESET_COL + 1 - reset, 1.0, 0.0)
    q_side = jnp.where(here, 1.0, jnp.broadcast_to(fixed, shape))
    ones = jnp.where((column >= LOG_COL) & (column < LOG_COL + 3), 1.0, 0.0)
    others = jnp.where(column < 8, MASKED, ones)
    k_side = jnp.where(here, 0.0, jnp.broadcast_to(others, shape))
    for which, out, side in ((0, q_out, q_side), (1, k_out, k_side), (2, v_out, jnp.ones(shape, F32))):
        result = dot(normed, w_ref[which])
        for pair in range(CORE_HEADS // 2):
            by_head(out, place, pair, result[:, pair * LANES : (pair + 1) * LANES], side)


    @pl.when(rank == 3)
    def _():
        give(K)
        give(V)


Q_LOG, K, V, KS, VS, NORMED, TOKENS, ROWS, O, O_AWAY, SCALES = range(11)


def attend_step(block, give, info, head, q_ref, k_ref, v_ref, ks_ref, vs_ref, q_out, o_ref, away):
    core = info[0]
    length = q_ref.shape[1]
    rows = away.shape[2]
    pair, parity = head // 2, head % 2
    column = aux_column((block, LANES), parity)
    keep = (column < 0) | (column >= HEAD_DIM)
    row = lax.broadcasted_iota(jnp.int32, (block, block), 0)
    key = lax.broadcasted_iota(jnp.int32, (block, block), 1)
    for i in range(length // block):
        low, high = i * block, (i + 1) * block
        q = q_ref[head, low:high, :]
        slot = dot(q, ks_ref[head], NT)
        scores = dot(q, k_ref[head, :high, :], NT)
        last = jnp.where(row >= key, scores[:, low:], MASKED)
        scores = jnp.concatenate([scores[:, :low], last], axis=1) if i else last
        top = jnp.maximum(
            jnp.max(scores, axis=1, keepdims=True), jnp.max(slot, axis=1, keepdims=True)
        )
        share = jnp.exp2((scores - top) * EXP).astype(BF16)
        slot_share = jnp.exp2((slot - top) * EXP).astype(BF16)
        total = dot(share, v_ref[head, :high, :]) + dot(slot_share, vs_ref[head])
        count = jnp.where(parity == 0, total[:, HEAD_DIM : HEAD_DIM + 1], total[:, 0:1])
        o_ref[pair, low:high, :] = jnp.where(
            keep, (total / count).astype(BF16), o_ref[pair, low:high, :]
        )
        log = top + jnp.log2(count) * (1.0 / EXP)
        q_out[head, low:high, :] = put_log(column, -log, q.astype(F32)).astype(BF16)
    give(Q_LOG, head)

    @pl.when(parity == 1)
    def _():
        for rank in range(4):

            @pl.when(core != rank % 2)
            def _():
                away[rank // 2, pair] = o_ref[pair, rank * rows : (rank + 1) * rows, :]

        give(O, pair)
        give(O_AWAY, slice(None), pair)


def read_kernel(
    need, give, info, packed, init, gain, mine, recv, mine_other, recv_other,
    q_log, k, v, ks, vs, normed, tokens, rows, o, o_away, scales, q, w_ref,
):
    step = pl.program_id(0)

    @pl.when(step < 4)
    def _():
        project_step(
            need, give, info, step, packed, init, gain, (mine, recv, mine_other, recv_other),
            q, k, v, normed, ks, vs, rows, tokens, scales, w_ref,
        )

    @pl.when(step >= 4)
    def _():
        attend_step(256, give, info, step - 4, q, k, v, ks, vs, q_log, o, o_away)


def read(info, sources, packed, init, gains, rows):
    total, width = sources[0].shape
    slots = 4 * (total - rows)
    length = 4 * rows
    heads = ((CORE_HEADS, length, LANES), BF16)
    slot = ((CORE_HEADS, 2 * slots, LANES), BF16)
    return streamed(
        read_kernel, "read", info, (packed, init, gains, *sources),
        (heads, heads, heads, slot, slot, ((length, width), BF16), ((2, rows, width), BF16),
         ((slots, width), BF16), ((2, length, LANES), BF16), ((2, 2, rows, LANES), BF16), ((length, LANES), F32)),
        [pltpu.VMEM((CORE_HEADS, length, LANES), BF16), pltpu.VMEM((3, width, CORE_WIDTH), BF16)],
        grid=(4 + CORE_HEADS,),
    )


def attend_back_kernel(
    kb, qb, first_head, info, own_ref, other_ref, o_ref, q_ref, k_ref, v_ref, ks_ref, vs_ref,
    dq_ref, dk_ref, dv_ref, dks_ref, dvs_ref, d_ref, acc_ref,
):
    length = q_ref.shape[1]
    step = pl.program_id(0)
    head = first_head + step
    pair, parity = head // 2, head % 2
    core = info[0]
    rows = own_ref.shape[2]
    column = aux_column((rows, LANES), parity)
    inside = (column < 0) | (column >= HEAD_DIM)
    for r in range(length // rows):
        low, high = r * rows, (r + 1) * rows
        d = jnp.where(core == r % 2, own_ref[r // 2, pair], other_ref[r // 2, pair]).astype(F32)
        delta = jnp.sum(
            jnp.where(inside, d * o_ref[pair, low:high, :].astype(F32), 0.0), axis=1, keepdims=True
        )
        d_ref[low:high, :] = jnp.where(
            inside, d, put_log(column, -delta, jnp.zeros_like(d))
        ).astype(BF16)
    acc_ref[...] = jnp.zeros_like(acc_ref)

    def tiles(k, v, first, low, stop):
        turned = k.astype(F32).T.astype(BF16)
        dk = jnp.zeros((k.shape[0], LANES), F32)
        dv = jnp.zeros((k.shape[0], LANES), F32)
        while low < stop:
            high = min((low // qb + 1) * qb, stop)
            q = q_ref[step, low:high, :]
            d = d_ref[low:high, :]
            scores = dot(k, q, NT)
            share = jnp.exp2(scores * EXP)
            if first is not None and low < first + k.shape[0]:
                key = first + lax.broadcasted_iota(jnp.int32, scores.shape, 0)
                position = low + lax.broadcasted_iota(jnp.int32, scores.shape, 1)
                share = jnp.where(key <= position, share, 0.0)
            ds = (share * dot(v, d, NT)).astype(BF16)
            dv = dv + dot(share.astype(BF16), d)
            dk = dk + dot(ds, q)
            acc_ref[:, low:high] += dot(turned, ds)
            low = high
        return dk, dv

    dk, dv = tiles(ks_ref[step], vs_ref[step], None, 0, length)
    dks_ref[step] = (dk * SCALE).astype(BF16)
    dvs_ref[step] = dv.astype(BF16)
    for low in range(0, length, kb):
        place = slice(low, low + kb)
        dk, dv = tiles(k_ref[step, place, :], v_ref[step, place, :], low, low, length)
        dk_ref[step, place, :] = (dk * SCALE).astype(BF16)
        dv_ref[step, place, :] = dv.astype(BF16)
    dq_ref[step] = (acc_ref[...].T * SCALE).astype(BF16)


def back_scratch(length):
    return [pltpu.VMEM((length, LANES), BF16), pltpu.VMEM((LANES, length), F32)]


def of_heads(array, first, heads):
    shape = (heads, *array.shape[1:])
    return array, shape, [((first + j,), (j,)) for j in range(heads)]


def of_pairs(array, axis, first, heads):
    before = (slice(None),) * axis
    pieces = [((*before, p),) * 2 for p in range(first // 2, (first + heads - 1) // 2 + 1)]
    return array, array.shape, pieces


def head_arrays(first, heads, q, k, v, ks, vs, own, other, o):
    return [
        of_pairs(own, 1, first, heads), of_pairs(other, 1, first, heads),
        of_pairs(o, 0, first, heads), *[of_heads(array, first, heads) for array in (q, k, v, ks, vs)],
    ]


def need_heads(need, first, heads):
    for k in range(3):
        for j in range((first + heads - 1) // 2 - first // 2 + 1):
            need(k, j)
    for k in range(3, 8):
        for j in range(heads):
            need(k, j, j)


def some_heads_kernel(first, heads, need, give, info, *refs):
    need_heads(need, first, heads)
    attend_back_kernel(256, 1024, first, info, *refs)
    for k in range(5):
        give(k, pl.program_id(0))


def attend_back(info, first, heads, q, k, v, ks, vs, own, other, o):
    _, length, _ = q.shape
    out = ((heads, length, LANES), BF16)
    slot_out = ((heads, ks.shape[1], LANES), BF16)
    return streamed(
        functools.partial(some_heads_kernel, first, heads), "attend_back", info,
        head_arrays(first, heads, q, k, v, ks, vs, own, other, o),
        (out, out, out, slot_out, slot_out), back_scratch(length), grid=(heads,),
        by_piece=True,
    )


def side_by_side(tiles):
    return jnp.concatenate(tiles, axis=1)


MIDDLE, NORMED_TWO, ACT, SLOPE, RESULT, KEYS, VALUES, AWAY, WQ, SK, SV, STATS = range(12)


def forward_kernel(
    need, give, info, own, other, tokens_ref, gains, packed, memory,
    middle_out, normed_out, act_out, slope_out, result_out, keys_out, values_out, away_out,
    query_out, key_out, value_out, stats,
):
    refs = (
        own, other, tokens_ref, gains, packed, memory, middle_out, normed_out, act_out, slope_out,
        result_out, keys_out, values_out, away_out,
    )
    step = pl.program_id(0)
    pl.when(step == 0)(lambda: forward_step(lambda k, j=0: need(k, j, None), give, info, *refs))
    pl.when(step > 0)(lambda: forward_step(lambda *_: None, give, info, *refs))

    @pl.when(step == pl.num_programs(0) - 1)
    def _():
        write_step(keys_out, values_out, memory, packed, query_out, key_out, value_out, stats)
        for k in (WQ, SK, SV, STATS):
            give(k)


def forward_step(
    need, give, info, own, other, tokens_ref, gains, packed, memory,
    middle_out, normed_out, act_out, slope_out, result_out, keys_out, values_out, away_out,
):
    core, chip = info[0], info[1]
    half = CORE_WIDTH // FIELDS[OUT]
    for k in range(4):
        need(k)
    need(4, FORWARD.index(OUT))
    w_own = flat_rows(packed[pl.ds(core * half, half), : FIELDS[OUT], :])
    w_other = flat_rows(packed[pl.ds((1 - core) * half, half), : FIELDS[OUT], :])
    step = pl.program_id(0)
    rows = normed_out.shape[1]
    block = 2 * rows // pl.num_programs(0)
    which, at = step // (rows // block), pl.multiple_of(step % (rows // block) * block, block)
    place = (which, pl.ds(at, block))
    tokens = tokens_ref[place]
    start = pl.multiple_of((2 * which + core) * rows + at, block)
    o_own = side_by_side([own[pair, pl.ds(start, block), :] for pair in range(2)])
    o_other = side_by_side([other[which, pair, pl.ds(at, block), :] for pair in range(2)])
    middle = tokens.astype(F32) + (dot(o_own, w_own) + dot(o_other, w_other))
    middle_out[place] = middle
    unit, _ = norm_parts(middle)
    normed = (unit * gains[1:2, :].astype(F32)).astype(BF16)
    normed_out[place] = normed
    width = normed.shape[1]
    for k in range(CHUNKS):
        need(4, FORWARD.index(UP + k))
        pre = dot(normed, take_up(packed, k))
        square = pre * pre
        half = 0.5 + 0.5 * jnp.tanh(pre * (GELU_A + (GELU_A * GELU_B) * square))
        turn = (half - half * half) * (2.0 * GELU_A + (6.0 * GELU_A * GELU_B) * square)
        act_out[(k, *place)] = (pre * half).astype(BF16)
        slope_out[(k, *place)] = (half + pre * turn).astype(BF16)
    acts = side_by_side([act_out[(k, *place)] for k in range(CHUNKS)])
    need(4, FORWARD.index(DOWN))
    low = (middle + dot(acts, take(packed, DOWN))).astype(BF16)
    result_out[place] = low

    @pl.when(which != chip)
    def _():
        away_out[pl.ds(at, block), :] = low
        give(AWAY, pl.ds(at, block))

    need(4, FORWARD.index(WRITE))
    need(4, FORWARD.index(VALUE))
    need(5)
    keys_out[place] = dot(low, flat_rows(packed[OWNERS // 2 :, CUTS[WRITE] : CUTS[WRITE + 1], :])).astype(BF16)
    values_out[place] = dot(low, take(packed, VALUE)).astype(BF16)


    for k in (MIDDLE, NORMED_TWO, RESULT, KEYS, VALUES):
        give(k, *place)
    for k in (ACT, SLOPE):
        give(k, slice(None), *place)


def fields_of(packed, order):
    cuts = [*CUTS[:UP], *[CUTS[UP] + k * PART for k in range(CHUNKS + 1)]]
    pieces = [(slice(None), slice(cuts[k], cuts[k + 1])) for k in order]
    return packed, packed.shape, [(piece, piece) for piece in pieces]


UPS = tuple(UP + k for k in range(CHUNKS))
FORWARD = (OUT, *UPS, DOWN, WRITE, VALUE)
BACKWARD = (WRITE, VALUE, DOWN, *UPS, OUT)


def forward(info, tokens, o, other, packed, gains, memory):
    _, rows, width = tokens.shape
    slots = memory.shape[0]
    small = ((2, rows, width), BF16)
    wide = ((CHUNKS, 2, rows, FF // CHUNKS), BF16)
    slot = ((slots, width), BF16)
    return streamed(
        forward_kernel, "feed_forward", info, (o, other, tokens, gains, fields_of(packed, FORWARD), memory),
        (((2, rows, width), F32), small, wide, wide, small, small, small, ((rows, width), BF16),
         slot, slot, slot, ((3, slots, width), F32)),
        grid=(4,),
    )


KEPT, SENT, D_MIDDLE, D_OWN, D_OTHER, G_GAIN, D_MEMORY, NEW_ROWS = range(8)


def backward_kernel(
    need, give, info, stats, stats_other, query, key, value, rows_ref, cot_mine, cot_recv,
    cot_other, keys, values, packed, result, normed, act, slope, middle, own, other, gains,
    kept, away, d_middle_out, d_own, d_other, g_gain, d_memory, new_out,
    d_keys, d_values, d_query, d_self_key, d_self_value, mem_cot,
    d_result_ref, d_update_ref, d_normed_ref,
):
    step = pl.program_id(0)
    core, chip = info[0], info[1]
    count, rows, width = result.shape
    total = count * rows
    half = CORE_WIDTH // FIELDS[OUT]

    @pl.when(step == 0)
    def _():
        for k in range(11):
            need(k)
        write_back_step(
            info, stats, stats_other, query, key, value, rows_ref, cot_mine, cot_recv, cot_other,
            keys, values, new_out, d_keys, d_values, d_query, d_self_key, d_self_value, mem_cot,
        )
        give(NEW_ROWS)
        need(11, BACKWARD.index(WRITE))
        need(11, BACKWARD.index(VALUE))
        need(12)

    @pl.when(step == 0)
    def _():
        dk = d_keys[...].reshape(total, width)
        dv = d_values[...].reshape(total, width)
        w_query = flat_rows(packed[: OWNERS // 2, CUTS[WRITE] : CUTS[WRITE + 1], :])
        w_key = flat_rows(packed[OWNERS // 2 :, CUTS[WRITE] : CUTS[WRITE + 1], :])
        w_value = take(packed, VALUE)
        first, second = cot_mine[:rows, :].astype(F32), cot_recv[:rows, :].astype(F32)
        cot = jnp.concatenate(
            [jnp.where(chip == 0, first, second), jnp.where(chip == 0, second, first)], axis=0
        )
        d_result = cot + (dot(dk, w_key, NT) + dot(dv, w_value, NT))
        d_result_ref[...] = d_result
        d_update_ref[...] = d_result.astype(BF16)
        d_normed_ref[...] = jnp.zeros_like(d_normed_ref)
        out = result[...].reshape(total, width)
        memory = rows_ref[...]
        put(core, kept, away, dot(memory, d_query[...], TN), 0, OWNERS // 2, CUTS[WRITE], FIELDS[WRITE])
        put(
            core, kept, away, dot(out, dk, TN) + dot(memory, d_self_key[...], TN),
            OWNERS // 4, OWNERS // 2, CUTS[WRITE], FIELDS[WRITE],
        )
        put(
            core, kept, away, dot(out, dv, TN) + dot(memory, d_self_value[...], TN),
            0, OWNERS, CUTS[VALUE], FIELDS[VALUE],
        )
        d_memory[...] = mem_cot[...] + (
            dot(d_query[...], w_query, NT)
            + dot(d_self_key[...], w_key, NT)
            + dot(d_self_value[...], w_value, NT)
        )
        give(D_MEMORY)
        for k in (SENT, KEPT):
            give(k, slice(None), slice(CUTS[VALUE], CUTS[WRITE + 1]))
        need(11, BACKWARD.index(DOWN))
        for k in range(CHUNKS):
            need(11, BACKWARD.index(UP + k))
        need(13)

    for j in range(CHUNKS):
        need(14, j, j)
        need(15, j, j)
    d_update = d_update_ref[...]
    d_act = dot(d_update, take_down(packed, step), NT)
    d_hidden = (d_act * slope[step].reshape(total, -1).astype(F32)).astype(BF16)
    g_down = dot(act[step].reshape(total, -1), d_update, TN)
    owners = OWNERS // CHUNKS
    put(core, kept, away, g_down, step * (owners // 2), owners, CUTS[DOWN], FIELDS[DOWN])
    g_up = dot(normed[...].reshape(total, width), d_hidden, TN)
    at = pl.multiple_of(CUTS[UP] + step * PART, PART)
    put(core, kept, away, g_up, 0, OWNERS, at, PART)
    for k in (SENT, KEPT):
        give(k, slice(None), pl.ds(at, PART))
        give(k, pl.ds(step * (owners // 2), owners // 2), slice(CUTS[DOWN], CUTS[DOWN + 1]))
    d_normed_ref[...] += dot(d_hidden, take_up(packed, step), NT)

    @pl.when(step == pl.num_programs(0) - 1)
    def _():
        for k in (16, 17, 18, 19):
            need(k, 0, CHUNKS - 1)
        need(11, BACKWARD.index(OUT), CHUNKS - 1)
        gain = gains[1:2, :].astype(F32)
        unit, scale = norm_parts(middle[...].reshape(total, width))
        d_normed = d_normed_ref[...]
        g_gain[...] = jnp.sum(d_normed * unit, axis=0, keepdims=True)
        d_middle = d_result_ref[...] + norm_back(unit, scale, d_normed, gain)
        d_middle_out[...] = d_middle.reshape(count, rows, width)
        give(D_MIDDLE)
        give(G_GAIN)
        d_branch = d_middle.astype(BF16)
        for start, out in ((core * half, d_own), ((1 - core) * half, d_other)):
            weight = flat_rows(packed[pl.ds(start, half), : FIELDS[OUT], :])
            back = dot(d_branch, weight, NT).astype(BF16)
            for k in range(count):
                for pair in range(2):
                    lanes = slice(pair * LANES, (pair + 1) * LANES)
                    out[k, pair] = back[k * rows : (k + 1) * rows, lanes]
        give(D_OWN)
        give(D_OTHER)
        own_rows = jnp.concatenate(
            [
                side_by_side(
                    [
                        own[pair, pl.ds(pl.multiple_of((2 * k + core) * rows, rows), rows), :]
                        for pair in range(2)
                    ]
                )
                for k in range(count)
            ],
            axis=0,
        )
        other_rows = jnp.concatenate([side_by_side([other[k, 0], other[k, 1]]) for k in range(count)], axis=0)
        g_own = dot(own_rows, d_branch, TN)
        g_other = dot(other_rows, d_branch, TN)
        put(core, kept, away, g_own, core * (half // 2), half, 0, FIELDS[OUT])
        put(core, kept, away, g_other, (1 - core) * (half // 2), half, 0, FIELDS[OUT])
        for k in (SENT, KEPT):
            give(k, slice(None), slice(CUTS[OUT], CUTS[OUT + 1]))


def by_chunk(array):
    return array, array.shape, [((j,), (j,)) for j in range(CHUNKS)]


def backward(info, stats, stats_other, writer, memory, cots, cot_other, keys, values, packed,
             result, normed, act, slope, middle, o, other, gains):
    _, rows, width = result.shape
    slots = memory.shape[0]
    grads = ((OWNERS // 2, PACKED, width), BF16)
    half = ((2, 2, rows, LANES), BF16)
    slot = pltpu.VMEM((slots, width), BF16)
    return streamed(
        backward_kernel, "feed_forward_back", info,
        (stats, stats_other, *writer, memory, *cots, cot_other, keys, values, fields_of(packed, BACKWARD),
         result, normed, by_chunk(act), by_chunk(slope), middle, o, other, gains),
        (grads, grads, ((2, rows, width), F32), half, half, ((1, width), F32),
         ((slots, width), F32), ((slots, width), BF16)),
        [pltpu.VMEM((2, rows, width), BF16), pltpu.VMEM((2, rows, width), BF16), slot, slot, slot,
         pltpu.VMEM((slots, width), F32),
         pltpu.VMEM((2 * rows, width), F32), pltpu.VMEM((2 * rows, width), BF16),
         pltpu.VMEM((2 * rows, width), F32)],
        grid=(CHUNKS,),
    )


def head_mask(shape, head):
    lane = lax.broadcasted_iota(jnp.int32, shape, 1)
    return (lane >= head * HEAD_DIM) & (lane < (head + 1) * HEAD_DIM)


def stacked_heads(values):
    return jnp.concatenate(
        [jnp.where(head_mask(values.shape, h), values, 0.0) for h in range(HEADS)], axis=0
    )


def joined_heads(stacked, slots):
    out = None
    for h in range(HEADS):
        part = stacked[h * slots : (h + 1) * slots, :]
        shape = (slots, HEADS * HEAD_DIM)
        part = jnp.broadcast_to(part, shape)
        out = part if out is None else jnp.where(head_mask(shape, h), part, out)
    return out


def column_of_heads(values):
    return jnp.concatenate(
        [values[:, h * HEAD_DIM : h * HEAD_DIM + 1] for h in range(HEADS)], axis=0
    )


def head_sums(values):
    return jnp.concatenate(
        [
            jnp.sum(jnp.where(head_mask(values.shape, h), values, 0.0), axis=1, keepdims=True)
            for h in range(HEADS)
        ],
        axis=0,
    )


def write_step(keys, values, memory, packed, query_out, key_out, value_out, stats):
    slots = memory.shape[0]
    total = keys.shape[0] * keys.shape[1]
    rows = memory[...]
    w_write = take(packed, WRITE)
    query = dot(rows, w_write[: w_write.shape[0] // 2]).astype(BF16)
    query_out[...] = query
    key_out[...] = dot(rows, w_write[w_write.shape[0] // 2 :]).astype(BF16)
    value_out[...] = dot(rows, take(packed, VALUE)).astype(BF16)
    stacked = stacked_heads(query.astype(F32)).astype(BF16)
    scores = dot(stacked, keys[...].reshape(total, -1), NT)
    top = jnp.max(scores, axis=1, keepdims=True)
    share = jnp.exp2((scores - top) * EXP)
    stats[0] = joined_heads(top, slots)
    stats[1] = joined_heads(jnp.sum(share, axis=1, keepdims=True), slots)
    stats[2] = joined_heads(dot(share.astype(BF16), values[...].reshape(total, -1)), slots)


def write_back_step(
    info, own, other, query, key, value, memory, cot_mine, cot_recv, cot_other, keys, values,
    new_out, d_keys, d_values, d_query, d_key, d_value, cot_out,
):
    core, chip = info[0], info[1]
    slots, width = memory.shape
    part = slots // 4
    rows = keys.shape[1]
    total = keys.shape[0] * rows
    sources = (cot_mine[rows:, :], cot_recv[rows:, :], cot_other[:part, :], cot_other[part:, :])
    cot = jnp.concatenate([choose(k, core, chip, *sources) for k in range(4)], axis=0).astype(F32)
    q = query[...].astype(F32)
    sk = key[...].astype(F32)
    sv = value[...].astype(F32)
    self_column = head_sums(q * sk)
    self_scores = joined_heads(self_column, slots)
    top = jnp.maximum(jnp.maximum(own[0], other[0]), self_scores)
    own_share = jnp.exp2((own[0] - top) * EXP)
    other_share = jnp.exp2((other[0] - top) * EXP)
    self_share = jnp.exp2((self_scores - top) * EXP)
    count = own[1] * own_share + other[1] * other_share + self_share
    written = (
        own[2] * own_share + other[2] * other_share + self_share.astype(BF16).astype(F32) * sv
    ) / count
    new_out[...] = (memory[...].astype(F32) + written).astype(BF16)
    log = top + jnp.log2(count) * (1.0 / EXP)
    log_column = column_of_heads(log)
    delta_column = head_sums(cot * written)
    delta = joined_heads(delta_column, slots)
    stacked = stacked_heads(q).astype(BF16)
    stacked_cot = stacked_heads(cot).astype(BF16)
    flat_keys = keys[...].reshape(total, width)
    share = jnp.exp2((dot(stacked, flat_keys, NT) - log_column) * EXP)
    d_share = dot(stacked_cot, values[...].reshape(total, width), NT)
    d_scores = (share * (d_share - delta_column)).astype(BF16)
    d_values[...] = dot(share.astype(BF16), stacked_cot, TN).astype(BF16).reshape(d_values.shape)
    d_keys[...] = (dot(d_scores, stacked, TN) * SCALE).astype(BF16).reshape(d_keys.shape)
    d_query_part = joined_heads(dot(d_scores, flat_keys), slots) * SCALE
    mine = (lax.broadcasted_iota(jnp.int32, (slots, width), 0) // part) % 2 == core
    self_probs = jnp.exp2((self_scores - log) * EXP)
    self_dp = joined_heads(head_sums(cot * sv), slots)
    self_ds = (self_probs * (self_dp - delta)).astype(BF16).astype(F32) * SCALE
    self_ds = jnp.where(mine, self_ds, 0.0)
    d_query[...] = (d_query_part + self_ds * sk).astype(BF16)
    d_key[...] = (self_ds * q).astype(BF16)
    d_value[...] = jnp.where(mine, self_probs.astype(BF16).astype(F32) * cot, 0.0).astype(BF16)
    cot_out[...] = jnp.where(mine, cot, 0.0)


def merged_heads(heads, place):
    tiles = [ref[k, place, :] for ref in heads for k in range(ref.shape[0])]
    lane = lax.broadcasted_iota(jnp.int32, tiles[0].shape, 1)
    return side_by_side(
        [jnp.where(lane < HEAD_DIM, tiles[2 * p], tiles[2 * p + 1]) for p in range(len(tiles) // 2)]
    )


def inputs_back_step(
    info, dq_parts, dk_parts, dv_parts, packed, normed, scales, gain, d_middle,
    mine_out, away_out, g_gain, merged,
):
    core = info[0]
    rows = mine_out.shape[1]
    weights = [qkv_weight(packed, k) for k in range(3)]
    gain = gain[0:1, :].astype(F32)
    gain_sum = None
    for rank in range(4):
        place = pl.ds(rank * rows, rows)
        total = None
        for k, parts in enumerate((dq_parts, dk_parts, dv_parts)):
            grads = merged_heads(parts, place)
            merged[k, place, :] = grads
            term = dot(grads, weights[k], NT)
            total = term if total is None else total + term
        unit = normed[place, :].astype(F32) * (1.0 / gain)
        part = jnp.sum(total * unit, axis=0, keepdims=True)
        gain_sum = part if gain_sum is None else gain_sum + part
        back = norm_back(unit, scales[place, 0:1], total, gain)

        @pl.when(core == rank % 2)
        def _():
            mine_out[rank // 2] = d_middle[rank // 2] + back

        @pl.when(core != rank % 2)
        def _():
            away_out[rank // 2] = back.astype(BF16)

    g_gain[...] = gain_sum


ATTN_ROWS, INIT_ROWS, GAIN_ROWS, SMALL_ROWS = 96, 8, 4, 112


def weights_back_step(
    info, normed, merged, packed, memory, init, d_memory, g_gain, g_gain_two, dks_parts, dvs_parts,
    small, d_mine, d_away, g_ref, misc,
):
    source = jnp.concatenate([memory[...], init[...]], axis=0)
    everything = slice(0, source.shape[0])
    dks = merged_heads(dks_parts, everything)
    dvs = merged_heads(dvs_parts, everything)
    d_slots = dot(dks, qkv_weight(packed, 1), NT) + dot(dvs, qkv_weight(packed, 2), NT)
    slots = memory.shape[0]
    part = slots // 4
    total = d_memory[...] + d_slots[:slots]
    for k in range(2):
        even = total[2 * k * part : (2 * k + 1) * part]
        odd = total[(2 * k + 1) * part : (2 * k + 2) * part]
        d_mine[k * part : (k + 1) * part, :] = jnp.where(info[0] == 0, even, odd)
        d_away[k * part : (k + 1) * part, :] = jnp.where(info[0] == 0, odd, even)
    rows = normed[...]
    width = rows.shape[1]
    g_ref[:width, :] = dot(rows, merged[0], TN).astype(BF16)
    g_ref[width : 2 * width, :] = (dot(rows, merged[1], TN) + dot(source, dks, TN)).astype(BF16)
    g_ref[2 * width :, :] = (dot(rows, merged[2], TN) + dot(source, dvs, TN)).astype(BF16)
    pairs = OWNERS // 2
    small[:, :ATTN_ROWS, :] = g_ref[...].reshape(pairs, ATTN_ROWS, CORE_WIDTH)
    misc[...] = jnp.zeros_like(misc)
    each = slots // pairs
    for h in range(2):
        lanes = slice(h * CORE_WIDTH, (h + 1) * CORE_WIDTH)
        for k in range(slots):
            misc[k // each, 2 * (k % each) + h : 2 * (k % each) + h + 1, :] = d_slots[
                slots + k : slots + k + 1, lanes
            ]
        for k, gain in enumerate((g_gain, g_gain_two)):
            at = INIT_ROWS + 2 * k + h
            misc[:, at : at + 1, :] = jnp.broadcast_to(gain[:, lanes][None], (pairs, 1, CORE_WIDTH))
    small[:, ATTN_ROWS:, :] = misc[...].astype(BF16)


def last_heads_kernel(first, count, need, give, info, *refs):
    heads, refs = refs[:8], refs[8:]
    packed, refs = refs[0], refs[1:]
    earlier, refs = refs[:5], refs[5:]
    normed, scales, gain, d_middle, memory, init, d_memory, g_gain_two, refs = *refs[:8], refs[8:]
    d_mine, d_away, small, m_mine, m_away, refs = *refs[:5], refs[5:]
    results, merged, g_gain, g_ref, misc, scratch = refs[:5], *refs[5:9], refs[9:]
    need_heads(need, first, count)
    attend_back_kernel(256, 1024, first, info, *heads, *results, *scratch)

    @pl.when(pl.program_id(0) == pl.num_programs(0) - 1)
    def _():
        for k in range(8, 22):
            need(k, 0, pl.num_programs(0) - 1)
        parts = [(earlier[k], results[k]) for k in range(5)]
        inputs_back_step(
            info, *parts[:3], packed, normed, scales, gain, d_middle, d_mine, d_away, g_gain, merged
        )
        for k in range(2):
            give(k)
        weights_back_step(
            info, normed, merged, packed, memory, init, d_memory, g_gain, g_gain_two, *parts[3:],
            small, m_mine, m_away, g_ref, misc,
        )
        for k in range(2, 5):
            give(k)


def last_heads(info, first, heads, q, k, v, ks, vs, own, other, o, packed, earlier,
               normed, scales, gains, d_middle, memory, init, d_memory, g_gain_two):
    length, width = normed.shape
    slots = memory.shape[0]
    part = (d_middle.shape, F32)
    away = (d_middle.shape, BF16)
    half = ((slots // 2, width), F32)
    out = pltpu.VMEM((heads, length, LANES), BF16)
    slot_out = pltpu.VMEM((heads, ks.shape[1], LANES), BF16)
    return streamed(
        functools.partial(last_heads_kernel, first, heads), "last_heads", info,
        (*head_arrays(first, heads, q, k, v, ks, vs, own, other, o), packed, *earlier,
         normed, scales, gains, d_middle, memory, init, d_memory, g_gain_two),
        (part, away, ((OWNERS // 2, SMALL_ROWS, CORE_WIDTH), BF16), half, half),
        [out, out, out, slot_out, slot_out, pltpu.VMEM((3, length, CORE_WIDTH), BF16),
         pltpu.VMEM((1, width), F32), pltpu.VMEM((3 * width, CORE_WIDTH), BF16),
         pltpu.VMEM((OWNERS // 2, SMALL_ROWS - ATTN_ROWS, CORE_WIDTH), F32), *back_scratch(length)],
        grid=(heads,), late=range(8, 22), by_piece=True,
    )


def inputs_back_kernel(
    need, give, info, mine, other, mem_mine, mem_other, new_rows, d_out, away_out, mem_out
):
    core, chip = info[0], info[1]
    count, rows, _ = mine.shape
    for k in range(count):
        need(0, k)
        need(1, k)
        back = (mine[k] + other[k].astype(F32)).astype(BF16)
        d_out[k] = back
        give(0, k)

        @pl.when(chip != k)
        def _():
            away_out[:rows, :] = back

    for j in range(2, 5):
        need(j)
    part = mem_mine.shape[0] // 2
    grads = (mem_mine[...] + mem_other[...]).astype(BF16)
    news = [
        jnp.where(
            core == 0,
            new_rows[2 * k * part : (2 * k + 1) * part, :],
            new_rows[(2 * k + 1) * part : (2 * k + 2) * part, :],
        )
        for k in range(2)
    ]
    first, second = grads[:part], grads[part:]
    mem_out[:part, :] = jnp.where(chip == 0, first, second)
    mem_out[part:, :] = jnp.where(chip == 0, news[0], news[1])
    away_out[rows : rows + part, :] = jnp.where(chip == 0, second, first)
    away_out[rows + part :, :] = jnp.where(chip == 0, news[1], news[0])
    for k in (1, 2):
        give(k)


def inputs_back(info, mine, other, mem_mine, mem_other, new_rows):
    _, rows, width = mine.shape
    slots = new_rows.shape[0]
    halves = [(array, array.shape, [((j,), (j,)) for j in range(2)]) for array in (mine, other)]
    return streamed(
        inputs_back_kernel, "inputs_back", info, (*halves, mem_mine, mem_other, new_rows),
        ((mine.shape, BF16), ((rows + slots // 2, width), BF16), ((slots // 2, width), BF16)),
    )


def swap(value, over_batch, over_seq):
    batch, seq = lax.axis_size("batch"), lax.axis_size("seq")
    pairs = [
        (i * seq + j, (i ^ over_batch) * seq + (j ^ over_seq))
        for i in range(batch)
        for j in range(seq)
    ]
    return lax.ppermute(value, ("batch", "seq"), pairs)


def chip_groups():
    batch = lax.axis_index("batch")
    chip = lax.axis_index("seq") // 2
    stages = [(4, 2 * (batch & 1) + chip, lambda k: (k >> 1, 2 * (k & 1)))]
    bits = lax.axis_size("batch").bit_length() - 1
    at = 1
    while at < bits:
        count = min(2, bits - at)
        stages.append(
            (1 << count, (batch >> at) & ((1 << count) - 1), lambda k, at=at: (k << at, 0))
        )
        at += count
    return stages


def in_order(pieces, own):
    bit = 1
    while bit < len(pieces):
        turned = (own & bit) > 0
        pieces = [jnp.where(turned, pieces[k ^ bit], pieces[k]) for k in range(len(pieces))]
        bit *= 2
    return jnp.stack(pieces)


def gather_chips(piece):
    stages = chip_groups()
    shape = piece.shape
    for size, own, peer in reversed(stages):
        piece = in_order([piece] + [swap(piece, *peer(k)) for k in range(1, size)], own)
    count = len(stages)
    piece = piece.transpose(*reversed(range(count)), *range(count, piece.ndim))
    return piece.reshape(-1, *shape)


def square_groups():
    batch, seq = lax.axis_size("batch"), lax.axis_size("seq")
    return [
        [(2 * r + y) * seq + 2 * x + core for y in range(2) for x in range(2)]
        for r in range(batch // 2)
        for core in range(2)
    ]


def line_groups():
    batch, seq = lax.axis_size("batch"), lax.axis_size("seq")
    return [
        [(2 * r + y) * seq + s for r in range(batch // 2)] for y in range(2) for s in range(seq)
    ]


def sent_lines(rows, stages):
    parts = [rows]
    for stage in stages[1:]:
        parts = sent(spread(added(parts, BF16), stage), stage)
    return parts


def sum_scattered(rows, groups):
    return lax.psum_scatter(
        rows, ("batch", "seq"), scatter_dimension=0, tiled=True, axis_index_groups=groups
    )


def spread(pieces, stage):
    size, own, _ = stage
    pieces = pieces.reshape(-1, size, *pieces.shape[-2:])
    return [lax.dynamic_index_in_dim(pieces, own ^ j, 1, keepdims=False) for j in range(size)]


def sent(parts, stage):
    size, _, peer = stage
    return [parts[0]] + [swap(parts[j], *peer(j)) for j in range(1, size)]


def added(parts, kind):
    total = parts[0].astype(F32)
    for part in parts[1:]:
        total = total + part.astype(F32)
    return total.astype(kind)


def after(values, *others):
    return lax.optimization_barrier((values, others))[0]


def by_core(core, mine, other, axis=0):
    return jnp.where(
        core == 0,
        jnp.concatenate([mine, other], axis=axis),
        jnp.concatenate([other, mine], axis=axis),
    )


def by_chip(chip, mine, other):
    return jnp.where(chip == 0, jnp.stack([mine, other]), jnp.stack([other, mine]))


def pick(array, index, axis=0):
    return lax.dynamic_index_in_dim(array, index, axis, keepdims=False)


def to_owners(fields, devices):
    many = devices // OWNERS
    out = []
    for k, field in enumerate(fields):
        if many > 1:
            groups = CHUNKS if k == UP else 1
            field = field.reshape(OWNERS, many, groups, -1, field.shape[-1])
            field = field.transpose(0, 2, 1, 3, 4).reshape(OWNERS, -1, field.shape[-1])
        out.append(field)
    return jnp.concatenate(out, axis=1)


def from_owners(packed, devices):
    many = devices // OWNERS
    out = []
    for k in range(len(FIELDS)):
        field = packed[:, CUTS[k] : CUTS[k + 1]]
        groups = CHUNKS if k == UP else 1
        field = field.reshape(OWNERS, groups, many, -1, field.shape[-1])
        out.append(field.transpose(0, 2, 1, 3, 4).reshape(devices, -1, field.shape[-1]))
    return jnp.concatenate(out, axis=1)


def per_device(
    tokens, memory, lengths, resets, attn_in, attn_out, ffn_in, ffn_out, writer_in, writer_value,
    norm_gains, memory_init, out_cotangent, memory_cotangent,
):
    _, rows, width = tokens.shape
    devices = lax.axis_size("batch") * lax.axis_size("seq")
    rank = lax.axis_index("seq")
    chip, core = rank // 2, rank % 2
    slot_part = memory.shape[1]
    slots = 4 * slot_part
    stages = chip_groups()

    ends = jnp.cumsum(pick(lengths, chip))
    info = jnp.concatenate([jnp.stack([core, chip]), ends, pick(resets, chip)]).astype(jnp.int32)

    def to_chip(big, small):
        mine = jnp.concatenate([pick(big, chip), pick(small, chip)], axis=0)
        away = jnp.concatenate([pick(big, 1 - chip), pick(small, 1 - chip)], axis=0)
        return mine, swap(away, 0, 2)

    misc = jnp.concatenate([memory_init, norm_gains])
    misc_rows = -(-misc.shape[0] // CORE_WIDTH)
    misc = jnp.pad(misc, (0, misc_rows * CORE_WIDTH - misc.shape[0])).reshape(misc_rows, CORE_WIDTH)
    attn_rows = attn_in.reshape(-1, 2, CORE_WIDTH)
    own_rows = attn_rows.shape[0]
    mine = jnp.concatenate([pick(attn_rows, core, 1), misc], axis=0)
    theirs = swap(jnp.concatenate([pick(attn_rows, 1 - core, 1), misc], axis=0), 0, 1)
    piece = jnp.concatenate(
        [
            by_core(core, mine[:own_rows], theirs[:own_rows]),
            by_core(core, mine[own_rows:], theirs[own_rows:]),
        ],
        axis=0,
    )
    gathered = gather_chips(piece)
    misc = gathered[:, 2 * own_rows :].reshape(devices, -1)
    init = misc[:, : memory_init.shape[0]].reshape(slots, width)
    gains = misc[:, memory_init.shape[0] :][:, : norm_gains.shape[0]].reshape(2, width)
    w_qkv = gathered
    if devices != OWNERS:
        w_qkv = gathered[:, : 2 * own_rows].reshape(OWNERS // 2, -1, CORE_WIDTH)

    columns = ffn_in.reshape(-1, CHUNKS, width).transpose(1, 0, 2).reshape(-1, width)
    fields = [attn_out, writer_value, writer_in, ffn_out, ffn_in]
    sizes = [field.shape[0] // width for field in fields]
    parts = [jnp.concatenate(fields[:UP]).reshape(-1, width), columns]
    cuts = [sum(sizes[:k]) for k in range(len(sizes) + 1)]
    packed = lax.all_gather(jnp.concatenate(parts, axis=0), ("batch", "seq"), axis=0)
    if devices != OWNERS:
        packed = to_owners([packed[:, cuts[k] : cuts[k + 1]] for k in range(len(sizes))], devices)

    own, recv = to_chip(tokens, memory)
    sources = (own, recv, swap(own, 0, 1), swap(recv, 0, 1))
    q_log, k, v, ks, vs, normed, own_tokens, mem_rows, o, o_away, scales = read(
        info, sources, w_qkv, init, gains, rows
    )
    out_cotangent, memory_cotangent = after((out_cotangent, memory_cotangent), recv)
    cots = to_chip(out_cotangent, memory_cotangent)
    cot_other = swap(jnp.concatenate([cot[rows:] for cot in after(cots, o)], axis=0), 0, 1)
    o_other = swap(o_away, 0, 1)
    middle, normed_two, act, slope, result, keys, values, result_away, *writer, stats = forward(
        info, own_tokens, o, o_other, packed, gains, mem_rows
    )
    came = swap(result_away, 0, 2)
    stats_other = swap(stats, 0, 1)
    kept, away, d_middle, d_own, d_away, g_gain_two, d_memory, new_rows = backward(
        info, stats, stats_other, writer, mem_rows, cots, cot_other, keys, values, packed, result,
        normed_two, act, slope, middle, o, o_other, gains,
    )
    d_other, came = after((swap(d_away, 0, 1), came), came)
    if devices != OWNERS:
        both = by_core(core, kept[:, None], away[:, None], axis=1).reshape(OWNERS, PACKED, width)
        both = from_owners(both, devices).reshape(devices // 2, 2, -1, width)
        kept, away = pick(both, core, 1), pick(both, 1 - core, 1)
    arrived = swap(after(away, d_other), 0, 1)

    heads = (q_log, k, v, ks, vs)
    grads_a = attend_back(info, 0, 1, *heads, d_own, d_other, o)
    kept, arrived = after((kept, arrived), grads_a)
    square = [
        added(pair, BF16) for pair in zip(spread(kept, stages[0])[1:], spread(arrived, stages[0])[1:])
    ]
    d_own = after(d_own, square)
    square = [swap(part, *stages[0][2](k + 1)) for k, part in enumerate(square)]
    d_mine, d_away, small, mem_mine, mem_away = last_heads(
        info, 1, 3, *heads, d_own, d_other, o, w_qkv, grads_a, normed, scales, gains,
        d_middle, mem_rows, init, d_memory, g_gain_two,
    )
    d_sent = swap(d_away, 0, 1)
    m_sent = swap(mem_away, 0, 1)

    init_size = memory_init.shape[0]
    init_rows = 2 * init_size // CORE_WIDTH
    cut_init, cut_gain = 2 * own_rows, 2 * own_rows + init_rows
    if devices != OWNERS:
        pairs = devices // 2
        small = jnp.concatenate(
            [
                small[:, :ATTN_ROWS].reshape(pairs, -1, CORE_WIDTH),
                small[:, ATTN_ROWS : ATTN_ROWS + INIT_ROWS].reshape(pairs, -1, CORE_WIDTH),
                jnp.repeat(small[:, ATTN_ROWS + INIT_ROWS :], pairs // (OWNERS // 2), axis=0),
            ],
            axis=1,
        )
    small_parts = sent(spread(small, stages[0]), stages[0])
    square, kept, arrived = after((square, kept, arrived), small)
    own = [spread(array, stages[0])[0] for array in (kept, arrived)]
    parts = sent_lines(added(own + square, BF16), stages)
    d_sent = after(d_sent, parts[0])
    d_tokens, d_tokens_away, mem_out = inputs_back(info, d_mine, d_sent, mem_mine, m_sent, new_rows)
    home = swap(after(d_tokens_away, small_parts), 0, 2)
    parts, small_parts = after(parts, d_tokens), after(small_parts, d_tokens)
    result, came = after((result, came), small_parts)
    for stage in stages[1:]:
        small_parts = sent(spread(added(small_parts, BF16), stage), stage)
    small_parts = after(small_parts, home)
    summed = added(parts, F32).reshape(-1, width)
    small = added(small_parts, F32).reshape(-1, CORE_WIDTH)
    big = [summed[cuts[k] : cuts[k + 1]] for k in range(len(sizes))]
    big[UP] = big[UP].reshape(CHUNKS, -1, width).transpose(1, 0, 2)
    small_attn = small[:cut_init].reshape(2, own_rows, CORE_WIDTH)
    small_init = small[cut_init:cut_gain].reshape(2, init_size)
    if init_rows % 2 == 0:
        small_init = small[cut_init:cut_gain].reshape(2, init_rows // 2, CORE_WIDTH)
    small_gain = small[cut_gain : cut_gain + GAIN_ROWS]
    if init_rows % 2 == 0:
        back = swap(
            jnp.concatenate(
                [pick(small_attn, 1 - core), pick(small_init, 1 - core), small_gain], axis=0
            ),
            0, 1,
        )
        init_back = back[own_rows : own_rows + init_rows // 2]
        gain_back = back[own_rows + init_rows // 2 :]
    else:
        back = swap(pick(small_attn, 1 - core), 0, 1)
        init_back = swap(pick(small_init, 1 - core), 0, 1)
        gain_back = swap(small_gain, 0, 1)
    attn_grad = by_core(core, pick(small_attn, core), back[:own_rows], axis=1)
    init_grad = (pick(small_init, core) + init_back).reshape(-1)
    device = lax.axis_index("batch") * lax.axis_size("seq") + rank
    gain_size = norm_gains.shape[0]
    gain_grad = lax.dynamic_slice_in_dim(
        (small_gain + gain_back).reshape(-1), device * gain_size, gain_size, 0
    )

    def at_home(both, new):
        return lax.dynamic_update_index_in_dim(both, new, 1 - chip, 0)

    mem_came = home[rows:]
    return (
        at_home(result, came),
        by_chip(chip, mem_out[slot_part:], mem_came[slot_part:]),
        at_home(d_tokens, home[:rows]),
        by_chip(chip, mem_out[:slot_part], mem_came[:slot_part]),
        attn_grad.reshape(-1),
        *[big[k].reshape(-1) for k in (OUT, UP, DOWN, WRITE, VALUE)],
        gain_grad,
        init_grad,
    )


def solution(mesh):
    rows = P("batch", "seq", None)
    table = P("batch", None)
    flat = P(("batch", "seq"))
    return jax.shard_map(
        per_device,
        mesh=mesh,
        in_specs=(rows, rows, table, table, *[flat] * 8, rows, rows),
        out_specs=(rows, rows, rows, rows, *[flat] * 8),
        check_vma=False,
    )
```

```python
import functools
import math

import jax
import jax.numpy as jnp
from jax import lax
from jax.experimental import pallas as pl
from jax.experimental.pallas import tpu as pltpu
from jax.sharding import PartitionSpec as P

HEADS = 8
HEAD_DIM = 64
FF = 2048
SEGMENT = 512
MASKED = -1e30
LANES = 128
CORE_HEADS = HEADS // 2
CORE_WIDTH = CORE_HEADS * HEAD_DIM
SCALE = HEAD_DIM ** (-0.5)
EXP = math.log2(math.e) * SCALE
LOG2E = math.log2(math.e)
RESET_COL = 8
LOG_COL = 10
NT = (((1,), (1,)), ((), ()))
NN = (((1,), (0,)), ((), ()))
TN = (((0,), (0,)), ((), ()))
GELU_A = math.sqrt(2.0 / math.pi)
GELU_B = 0.044715
BF16 = jnp.bfloat16
F32 = jnp.float32


def dot(left, right, dims=NN):
    return lax.dot_general(left, right, dims, preferred_element_type=F32)


def streamed(kernel, name, info, arrays, outs, scratch=(), grid=(1,), late=(), by_piece=False):
    arrays = [a if isinstance(a, tuple) else (a, a.shape, [((), ())]) for a in arrays]
    count = sum(len(pieces) for _, _, pieces in arrays)

    def at(ref, place):
        return ref.at[place] if place else ref

    def body(info, *refs):
        n, m = len(arrays), len(outs)
        far, far_out, refs = refs[:n], refs[n : n + m], refs[n + m :]
        near, near_out, refs = refs[:n], refs[n : n + m], refs[n + m :]
        own, sems, out_sems = refs[:-2], refs[-2], refs[-1]
        step = pl.program_id(0)
        copies = []
        for k, (_, _, pieces) in enumerate(arrays):
            first = sum(map(len, copies))
            copies.append(
                [
                    pltpu.make_async_copy(at(far[k], a), at(near[k], b), sems.at[first + j])
                    for j, (a, b) in enumerate(pieces)
                ]
            )

        @pl.when(step == 0)
        def _():
            ranked = [
                (100 * (k in late) + j * by_piece, k, j) for k in range(n) for j in range(len(copies[k]))
            ]
            for _, k, j in sorted(ranked):
                copies[k][j].start()

        def need(k, j=0, when=0):
            if when is None:
                copies[k][j].wait()
            else:
                pl.when(step == when)(copies[k][j].wait)

        def give(k, *place):
            pltpu.make_async_copy(
                at(near_out[k], place), at(far_out[k], place), out_sems.at[k]
            ).start()

        kernel(need, give, info, *near, *near_out, *own)

        @pl.when(step == pl.num_programs(0) - 1)
        def _():
            for k in range(m):
                pltpu.make_async_copy(near_out[k], far_out[k], out_sems.at[k]).wait()

    space = pl.BlockSpec(memory_space=pl.ANY)
    return pl.pallas_call(
        body,
        grid_spec=pltpu.PrefetchScalarGridSpec(
            num_scalar_prefetch=1,
            grid=grid,
            in_specs=[space] * len(arrays),
            out_specs=[space] * len(outs),
            scratch_shapes=[
                *[pltpu.VMEM(shape, array.dtype) for array, shape, _ in arrays],
                *[pltpu.VMEM(shape, kind) for shape, kind in outs],
                *scratch,
                pltpu.SemaphoreType.DMA((count,)),
                pltpu.SemaphoreType.DMA((len(outs),)),
            ],
        ),
        out_shape=[jax.ShapeDtypeStruct(shape, kind) for shape, kind in outs],
        compiler_params=pltpu.CompilerParams(vmem_limit_bytes=58 << 20),
        name=name,
    )(info, *[array for array, _, _ in arrays])


def norm_parts(values):
    centred = values - jnp.mean(values, axis=-1, keepdims=True)
    scale = lax.rsqrt(jnp.mean(centred * centred, axis=-1, keepdims=True) + 1e-05)
    return centred * scale, scale


def norm_back(unit, scale, grad, gain):
    back = grad * gain
    return scale * (
        back
        - jnp.mean(back, axis=-1, keepdims=True)
        - unit * jnp.mean(back * unit, axis=-1, keepdims=True)
    )


def in_three(values):
    high = values.astype(BF16).astype(F32)
    rest = values - high
    middle = rest.astype(BF16).astype(F32)
    return high, middle, rest - middle


def put_log(column, values, others):
    high, middle, low = in_three(values)
    out = jnp.where(column == LOG_COL, high, others)
    out = jnp.where(column == LOG_COL + 1, middle, out)
    return jnp.where(column == LOG_COL + 2, low, out)


def aux_column(shape, parity):
    lane = lax.broadcasted_iota(jnp.int32, shape, 1)
    return lane - (1 - parity) * HEAD_DIM


OWNERS = 32
OUT, VALUE, WRITE, DOWN, UP = range(5)
FIELDS = (16, 16, 32, 64, 64)
CUTS = tuple(sum(FIELDS[:k]) for k in range(len(FIELDS) + 1))
PACKED = CUTS[-1]
CHUNKS = 4
PART = FIELDS[UP] // CHUNKS


def flat_rows(block):
    return block.reshape(-1, block.shape[-1])


def take(packed, field):
    return flat_rows(packed[:, CUTS[field] : CUTS[field + 1], :])


def take_up(packed, chunk):
    if isinstance(chunk, int):
        at = CUTS[UP] + chunk * PART
    else:
        at = pl.multiple_of(CUTS[UP] + chunk * PART, PART)
    return flat_rows(packed[:, pl.ds(at, PART), :])


def take_down(packed, chunk):
    count = OWNERS // CHUNKS
    return flat_rows(packed[pl.ds(chunk * count, count), CUTS[DOWN] : CUTS[DOWN + 1], :])


def put(core, kept, away, value, owner, owners, at, rows):
    split = value.reshape(owners // 2, 2, rows, value.shape[-1])
    place = (pl.ds(owner, owners // 2), pl.ds(at, rows), slice(None))
    kept[place] = jnp.where(core == 0, split[:, 0], split[:, 1]).astype(BF16)
    away[place] = jnp.where(core == 0, split[:, 1], split[:, 0]).astype(BF16)


def by_head(out, place, pair, mine, side):
    lane = lax.broadcasted_iota(jnp.int32, mine.shape, 1)
    out[2 * pair, place, :] = jnp.where(lane < HEAD_DIM, mine, side).astype(BF16)
    out[2 * pair + 1, place, :] = jnp.where(lane < HEAD_DIM, side, mine).astype(BF16)


def choose(rank, core, chip, mine, recv, mine_other, recv_other):
    here = jnp.where(rank // 2 == chip, mine, recv)
    there = jnp.where(rank // 2 == chip, mine_other, recv_other)
    return jnp.where(rank % 2 == core, here, there)


def qkv_weight(packed, which):
    pairs = packed.shape[0]
    width = 2 * CORE_WIDTH
    rows = 3 * width // pairs
    if width % rows == 0:
        return flat_rows(packed[which * width // rows : (which + 1) * width // rows, :rows, :])
    return flat_rows(packed[:, :rows, :])[which * width : (which + 1) * width]


def project_step(
    need, give, info, rank, packed, init, gain, sources,
    q_out, k_out, v_out, normed_out, ks_out, vs_out, rows_out, tokens_out, scale_out, w_ref,
):
    core, chip = info[0], info[1]
    rows = normed_out.shape[0] // 4
    shape = (rows, LANES)
    column = lax.broadcasted_iota(jnp.int32, (1, LANES), 1) % HEAD_DIM

    @pl.when(rank == 0)
    def _():
        need(0)
        for which in range(3):
            w_ref[which] = qkv_weight(packed, which)
        for k in range(1, 7):
            need(k)
        slots = rows_out.shape[0]
        part = slots // 4
        for k in range(4):
            rows_out[k * part : (k + 1) * part, :] = choose(
                k, core, chip, *[ref[rows:, :] for ref in sources]
            )
        source = jnp.concatenate([rows_out[...], init[...]], axis=0)
        shape = (2 * slots, LANES)
        start = (lax.broadcasted_iota(jnp.int32, shape, 0) >= slots).astype(jnp.int32)
        ones = jnp.where((column >= LOG_COL) & (column < LOG_COL + 3), 1.0, 0.0)
        side = jnp.where(column == RESET_COL + start, MASKED, ones)
        keys = dot(source, w_ref[1])
        values = dot(source, w_ref[2])
        whole = slice(0, 2 * slots)
        for pair in range(CORE_HEADS // 2):
            lanes = slice(pair * LANES, (pair + 1) * LANES)
            by_head(ks_out, whole, pair, keys[:, lanes], side)
            by_head(vs_out, whole, pair, values[:, lanes], jnp.ones(shape, F32))
        for k in (KS, VS, ROWS):
            give(k)

    values = choose(rank, core, chip, *[ref[:rows, :] for ref in sources])

    @pl.when(rank % 2 == core)
    def _():
        tokens_out[rank // 2] = values
        give(TOKENS, rank // 2)

    unit, scale = norm_parts(values.astype(F32))
    normed = (unit * gain[0:1, :].astype(F32)).astype(BF16)
    place = pl.ds(pl.multiple_of(rank * rows, rows), rows)
    normed_out[place, :] = normed
    give(NORMED, place)
    scale_out[place, :] = jnp.broadcast_to(scale, (rows, LANES))
    give(SCALES, place)
    low = jnp.zeros((1, LANES), jnp.int32)
    high = jnp.zeros((1, LANES), jnp.int32)
    for k in range(8):
        low = jnp.where(column == k, info[1 + k] if k else 0, low)
        high = jnp.where(column == k, info[2 + k], high)
    reset = info[10 + (rank * rows) // SEGMENT]
    position = rank * rows + lax.broadcasted_iota(jnp.int32, shape, 0)
    here = (position >= low) & (position < high)
    fixed = jnp.where(column == RESET_COL + 1 - reset, 1.0, 0.0)
    q_side = jnp.where(here, 1.0, jnp.broadcast_to(fixed, shape))
    ones = jnp.where((column >= LOG_COL) & (column < LOG_COL + 3), 1.0, 0.0)
    others = jnp.where(column < 8, MASKED, ones)
    k_side = jnp.where(here, 0.0, jnp.broadcast_to(others, shape))
    for which, out, side in ((0, q_out, q_side), (1, k_out, k_side), (2, v_out, jnp.ones(shape, F32))):
        result = dot(normed, w_ref[which])
        for pair in range(CORE_HEADS // 2):
            by_head(out, place, pair, result[:, pair * LANES : (pair + 1) * LANES], side)


    @pl.when(rank == 3)
    def _():
        give(K)
        give(V)


Q_LOG, K, V, KS, VS, NORMED, TOKENS, ROWS, O, O_AWAY, SCALES, SHARES = range(12)
KEY_BLOCK = 256


def attend_step(block, give, info, head, q_ref, k_ref, v_ref, ks_ref, vs_ref, q_out, o_ref, away):
    core = info[0]
    length = q_ref.shape[1]
    rows = away.shape[2]
    pair, parity = head // 2, head % 2
    column = aux_column((block, LANES), parity)
    keep = (column < 0) | (column >= HEAD_DIM)
    row = lax.broadcasted_iota(jnp.int32, (block, block), 0)
    key = lax.broadcasted_iota(jnp.int32, (block, block), 1)
    for i in range(length // block):
        low, high = i * block, (i + 1) * block
        q = q_ref[head, low:high, :]
        slot = dot(q, ks_ref[head], NT)
        scores = dot(q, k_ref[head, :high, :], NT)
        last = jnp.where(row >= key, scores[:, low:], MASKED)
        scores = jnp.concatenate([scores[:, :low], last], axis=1) if i else last
        top = jnp.maximum(
            jnp.max(scores, axis=1, keepdims=True), jnp.max(slot, axis=1, keepdims=True)
        )
        share = jnp.exp2((scores - top) * EXP).astype(BF16)
        slot_share = jnp.exp2((slot - top) * EXP).astype(BF16)
        total = dot(share, v_ref[head, :high, :]) + dot(slot_share, vs_ref[head])
        count = jnp.where(parity == 0, total[:, HEAD_DIM : HEAD_DIM + 1], total[:, 0:1])
        o_ref[pair, low:high, :] = jnp.where(
            keep, (total / count).astype(BF16), o_ref[pair, low:high, :]
        )
        log = top + jnp.log2(count) * (1.0 / EXP)
        q_out[head, low:high, :] = put_log(column, -log, q.astype(F32)).astype(BF16)
    give(Q_LOG, head)

    @pl.when(parity == 1)
    def _():
        for rank in range(4):

            @pl.when(core != rank % 2)
            def _():
                away[rank // 2, pair] = o_ref[pair, rank * rows : (rank + 1) * rows, :]

        give(O, pair)
        give(O_AWAY, slice(None), pair)


def share_blocks(slots, length):
    return [(slots, length), *[(KEY_BLOCK, length - low) for low in range(0, length, KEY_BLOCK)]]


def shares_step(give, head, q_log, k_ref, ks_ref, shares):
    q = q_log[head]
    shares[0][head] = jnp.exp2(dot(ks_ref[head], q, NT) * EXP).astype(BF16)
    for j in range(len(shares) - 1):
        low = j * KEY_BLOCK
        scores = dot(k_ref[head, low : low + KEY_BLOCK, :], q[low:, :], NT)
        share = jnp.exp2(scores * EXP)
        key = lax.broadcasted_iota(jnp.int32, (KEY_BLOCK, KEY_BLOCK), 0)
        position = lax.broadcasted_iota(jnp.int32, (KEY_BLOCK, KEY_BLOCK), 1)
        first = jnp.where(key <= position, share[:, :KEY_BLOCK], 0.0)
        shares[j + 1][head, :, :KEY_BLOCK] = first.astype(BF16)
        if share.shape[1] > KEY_BLOCK:
            shares[j + 1][head, :, KEY_BLOCK:] = share[:, KEY_BLOCK:].astype(BF16)
    for j in range(len(shares)):
        give(SHARES + j, head)


def read_kernel(
    need, give, info, packed, init, gain, mine, recv, mine_other, recv_other,
    q_log, k, v, ks, vs, normed, tokens, rows, o, o_away, scales, *refs,
):
    shares, q, w_ref = refs[:-2], refs[-2], refs[-1]
    step = pl.program_id(0)

    @pl.when(step < 4)
    def _():
        project_step(
            need, give, info, step, packed, init, gain, (mine, recv, mine_other, recv_other),
            q, k, v, normed, ks, vs, rows, tokens, scales, w_ref,
        )

    @pl.when((step >= 4) & (step < 4 + CORE_HEADS))
    def _():
        attend_step(256, give, info, step - 4, q, k, v, ks, vs, q_log, o, o_away)

    @pl.when(step >= 4 + CORE_HEADS)
    def _():
        shares_step(give, step - 4 - CORE_HEADS, q_log, k, ks, shares)


def read(info, sources, packed, init, gains, rows):
    total, width = sources[0].shape
    slots = 4 * (total - rows)
    length = 4 * rows
    heads = ((CORE_HEADS, length, LANES), BF16)
    slot = ((CORE_HEADS, 2 * slots, LANES), BF16)
    return streamed(
        read_kernel, "read", info, (packed, init, gains, *sources),
        (heads, heads, heads, slot, slot, ((length, width), BF16), ((2, rows, width), BF16),
         ((slots, width), BF16), ((2, length, LANES), BF16), ((2, 2, rows, LANES), BF16), ((length, LANES), F32),
         *[((CORE_HEADS, *block), BF16) for block in share_blocks(2 * slots, length)]),
        [pltpu.VMEM((CORE_HEADS, length, LANES), BF16), pltpu.VMEM((3, width, CORE_WIDTH), BF16)],
        grid=(4 + 2 * CORE_HEADS,),
    )


def attend_back_kernel(
    qb, first_head, info, own_ref, other_ref, o_ref, q_ref, k_ref, v_ref, ks_ref, vs_ref, shares,
    dq_ref, dk_ref, dv_ref, dks_ref, dvs_ref, d_ref, acc_ref, wait=lambda _: None,
):
    length = q_ref.shape[1]
    step = pl.program_id(0)
    head = first_head + step
    pair, parity = head // 2, head % 2
    core = info[0]
    rows = own_ref.shape[2]
    column = aux_column((rows, LANES), parity)
    inside = (column < 0) | (column >= HEAD_DIM)
    for r in range(length // rows):
        low, high = r * rows, (r + 1) * rows
        d = jnp.where(core == r % 2, own_ref[r // 2, pair], other_ref[r // 2, pair]).astype(F32)
        delta = jnp.sum(
            jnp.where(inside, d * o_ref[pair, low:high, :].astype(F32), 0.0), axis=1, keepdims=True
        )
        d_ref[low:high, :] = jnp.where(
            inside, d, put_log(column, -delta, jnp.zeros_like(d))
        ).astype(BF16)
    acc_ref[...] = jnp.zeros_like(acc_ref)

    def tiles(k, v, shares, first):
        turned = k.astype(F32).T.astype(BF16)
        dk = jnp.zeros((k.shape[0], LANES), F32)
        dv = jnp.zeros((k.shape[0], LANES), F32)
        low = first
        while low < length:
            high = min((low // qb + 1) * qb, length)
            q = q_ref[step, low:high, :]
            d = d_ref[low:high, :]
            share = shares[step, :, low - first : high - first]
            ds = (share.astype(F32) * dot(v, d, NT)).astype(BF16)
            dv = dv + dot(share, d)
            dk = dk + dot(ds, q)
            acc_ref[:, low:high] += dot(turned, ds)
            low = high
        return dk, dv

    wait(0)
    dk, dv = tiles(ks_ref[step], vs_ref[step], shares[0], 0)
    dks_ref[step] = (dk * SCALE).astype(BF16)
    dvs_ref[step] = dv.astype(BF16)
    for j in range(len(shares) - 1):
        low = j * KEY_BLOCK
        place = slice(low, low + KEY_BLOCK)
        wait(j + 1)
        dk, dv = tiles(k_ref[step, place, :], v_ref[step, place, :], shares[j + 1], low)
        dk_ref[step, place, :] = (dk * SCALE).astype(BF16)
        dv_ref[step, place, :] = dv.astype(BF16)
    dq_ref[step] = (acc_ref[...].T * SCALE).astype(BF16)


def back_scratch(length):
    return [pltpu.VMEM((length, LANES), BF16), pltpu.VMEM((LANES, length), F32)]


def of_heads(array, first, heads):
    shape = (heads, *array.shape[1:])
    return array, shape, [((first + j,), (j,)) for j in range(heads)]


def of_pairs(array, axis, first, heads):
    before = (slice(None),) * axis
    pieces = [((*before, p),) * 2 for p in range(first // 2, (first + heads - 1) // 2 + 1)]
    return array, array.shape, pieces


def head_arrays(first, heads, q, k, v, ks, vs, shares, own, other, o):
    return [
        of_pairs(own, 1, first, heads), of_pairs(other, 1, first, heads),
        of_pairs(o, 0, first, heads),
        *[of_heads(array, first, heads) for array in (q, k, v, ks, vs, *shares)],
    ]


def need_heads(need, first, heads, arrays):
    for k in range(3):
        for j in range((first + heads - 1) // 2 - first // 2 + 1):
            need(k, j)
    for j in range(heads):

        @pl.when(pl.program_id(0) == j)
        def _():
            for k in range(3, arrays):
                need(k, j, None)


def some_heads_kernel(first, heads, need, give, info, *refs):
    count = len(refs) - 7
    wait = lambda _: None
    if heads == 1:
        for k in range(3):
            need(k, 0, None)

        def wait(j):
            for k in (8 + j,) if j else range(3, 9):
                need(k, 0, None)
    else:
        need_heads(need, first, heads, count)
    attend_back_kernel(1024, first, info, *refs[:8], refs[8:count], *refs[count:], wait=wait)
    for k in range(5):
        give(k, pl.program_id(0))


def attend_back(info, first, heads, q, k, v, ks, vs, shares, own, other, o):
    _, length, _ = q.shape
    out = ((heads, length, LANES), BF16)
    slot_out = ((heads, ks.shape[1], LANES), BF16)
    return streamed(
        functools.partial(some_heads_kernel, first, heads), "attend_back", info,
        head_arrays(first, heads, q, k, v, ks, vs, shares, own, other, o),
        (out, out, out, slot_out, slot_out), back_scratch(length), grid=(heads,),
        by_piece=True,
    )


def side_by_side(tiles):
    return jnp.concatenate(tiles, axis=1)


MIDDLE, NORMED_TWO, ACT, SLOPE, RESULT, KEYS, VALUES, AWAY, WQ, SK, SV, STATS = range(12)


def forward_kernel(
    need, give, info, own, other, tokens_ref, gains, packed, memory,
    middle_out, normed_out, act_out, slope_out, result_out, keys_out, values_out, away_out,
    query_out, key_out, value_out, stats,
):
    refs = (
        own, other, tokens_ref, gains, packed, memory, middle_out, normed_out, act_out, slope_out,
        result_out, keys_out, values_out, away_out,
    )
    step = pl.program_id(0)
    pl.when(step == 0)(lambda: forward_step(lambda k, j=0: need(k, j, None), give, info, *refs))
    pl.when(step > 0)(lambda: forward_step(lambda *_: None, give, info, *refs))

    @pl.when(step == pl.num_programs(0) - 1)
    def _():
        write_step(keys_out, values_out, memory, packed, query_out, key_out, value_out, stats)
        for k in (WQ, SK, SV, STATS):
            give(k)


def forward_step(
    need, give, info, own, other, tokens_ref, gains, packed, memory,
    middle_out, normed_out, act_out, slope_out, result_out, keys_out, values_out, away_out,
):
    core, chip = info[0], info[1]
    half = CORE_WIDTH // FIELDS[OUT]
    for k in range(4):
        need(k)
    need(4, FORWARD.index(OUT))
    w_own = flat_rows(packed[pl.ds(core * half, half), : FIELDS[OUT], :])
    w_other = flat_rows(packed[pl.ds((1 - core) * half, half), : FIELDS[OUT], :])
    step = pl.program_id(0)
    rows = normed_out.shape[1]
    block = 2 * rows // pl.num_programs(0)
    which, at = step // (rows // block), pl.multiple_of(step % (rows // block) * block, block)
    place = (which, pl.ds(at, block))
    tokens = tokens_ref[place]
    start = pl.multiple_of((2 * which + core) * rows + at, block)
    o_own = side_by_side([own[pair, pl.ds(start, block), :] for pair in range(2)])
    o_other = side_by_side([other[which, pair, pl.ds(at, block), :] for pair in range(2)])
    middle = tokens.astype(F32) + (dot(o_own, w_own) + dot(o_other, w_other))
    middle_out[place] = middle
    unit, _ = norm_parts(middle)
    normed = (unit * gains[1:2, :].astype(F32)).astype(BF16)
    normed_out[place] = normed
    width = normed.shape[1]
    for k in range(CHUNKS):
        need(4, FORWARD.index(UP + k))
        pre = dot(normed, take_up(packed, k))
        square = pre * pre
        half = 0.5 + 0.5 * jnp.tanh(pre * (GELU_A + (GELU_A * GELU_B) * square))
        turn = (half - half * half) * (2.0 * GELU_A + (6.0 * GELU_A * GELU_B) * square)
        act_out[(k, *place)] = (pre * half).astype(BF16)
        slope_out[(k, *place)] = (half + pre * turn).astype(BF16)
    acts = side_by_side([act_out[(k, *place)] for k in range(CHUNKS)])
    need(4, FORWARD.index(DOWN))
    low = (middle + dot(acts, take(packed, DOWN))).astype(BF16)
    result_out[place] = low

    @pl.when(which != chip)
    def _():
        away_out[pl.ds(at, block), :] = low
        give(AWAY, pl.ds(at, block))

    need(4, FORWARD.index(WRITE))
    need(4, FORWARD.index(VALUE))
    need(5)
    keys_out[place] = dot(low, flat_rows(packed[OWNERS // 2 :, CUTS[WRITE] : CUTS[WRITE + 1], :])).astype(BF16)
    values_out[place] = dot(low, take(packed, VALUE)).astype(BF16)


    for k in (MIDDLE, NORMED_TWO, RESULT, KEYS, VALUES):
        give(k, *place)
    for k in (ACT, SLOPE):
        give(k, slice(None), *place)


def fields_of(packed, order):
    cuts = [*CUTS[:UP], *[CUTS[UP] + k * PART for k in range(CHUNKS + 1)]]
    pieces = [(slice(None), slice(cuts[k], cuts[k + 1])) for k in order]
    return packed, packed.shape, [(piece, piece) for piece in pieces]


UPS = tuple(UP + k for k in range(CHUNKS))
FORWARD = (OUT, *UPS, DOWN, WRITE, VALUE)
BACKWARD = (WRITE, VALUE, DOWN, *UPS, OUT)


def forward(info, tokens, o, other, packed, gains, memory):
    _, rows, width = tokens.shape
    slots = memory.shape[0]
    small = ((2, rows, width), BF16)
    wide = ((CHUNKS, 2, rows, FF // CHUNKS), BF16)
    slot = ((slots, width), BF16)
    return streamed(
        forward_kernel, "feed_forward", info, (o, other, tokens, gains, fields_of(packed, FORWARD), memory),
        (((2, rows, width), F32), small, wide, wide, small, small, small, ((rows, width), BF16),
         slot, slot, slot, ((3, slots, width), F32)),
        grid=(4,),
    )


KEPT, SENT, D_MIDDLE, D_OWN, D_OTHER, G_GAIN, D_MEMORY, NEW_ROWS = range(8)


def backward_kernel(
    need, give, info, stats, stats_other, query, key, value, rows_ref, cot_mine, cot_recv,
    cot_other, keys, values, packed, result, normed, act, slope, middle, own, other, gains,
    kept, away, d_middle_out, d_own, d_other, g_gain, d_memory, new_out,
    d_keys, d_values, d_query, d_self_key, d_self_value, mem_cot,
    d_result_ref, d_update_ref, d_normed_ref,
):
    step = pl.program_id(0)
    core, chip = info[0], info[1]
    count, rows, width = result.shape
    total = count * rows
    half = CORE_WIDTH // FIELDS[OUT]

    @pl.when(step == 0)
    def _():
        for k in range(11):
            need(k)
        write_back_step(
            info, stats, stats_other, query, key, value, rows_ref, cot_mine, cot_recv, cot_other,
            keys, values, new_out, d_keys, d_values, d_query, d_self_key, d_self_value, mem_cot,
        )
        give(NEW_ROWS)
        need(11, BACKWARD.index(WRITE))
        need(11, BACKWARD.index(VALUE))
        need(12)

    @pl.when(step == 0)
    def _():
        dk = d_keys[...].reshape(total, width)
        dv = d_values[...].reshape(total, width)
        w_query = flat_rows(packed[: OWNERS // 2, CUTS[WRITE] : CUTS[WRITE + 1], :])
        w_key = flat_rows(packed[OWNERS // 2 :, CUTS[WRITE] : CUTS[WRITE + 1], :])
        w_value = take(packed, VALUE)
        first, second = cot_mine[:rows, :].astype(F32), cot_recv[:rows, :].astype(F32)
        cot = jnp.concatenate(
            [jnp.where(chip == 0, first, second), jnp.where(chip == 0, second, first)], axis=0
        )
        d_result = cot + (dot(dk, w_key, NT) + dot(dv, w_value, NT))
        d_result_ref[...] = d_result
        d_update_ref[...] = d_result.astype(BF16)
        d_normed_ref[...] = jnp.zeros_like(d_normed_ref)
        out = result[...].reshape(total, width)
        memory = rows_ref[...]
        put(core, kept, away, dot(memory, d_query[...], TN), 0, OWNERS // 2, CUTS[WRITE], FIELDS[WRITE])
        put(
            core, kept, away, dot(out, dk, TN) + dot(memory, d_self_key[...], TN),
            OWNERS // 4, OWNERS // 2, CUTS[WRITE], FIELDS[WRITE],
        )
        put(
            core, kept, away, dot(out, dv, TN) + dot(memory, d_self_value[...], TN),
            0, OWNERS, CUTS[VALUE], FIELDS[VALUE],
        )
        d_memory[...] = mem_cot[...] + (
            dot(d_query[...], w_query, NT)
            + dot(d_self_key[...], w_key, NT)
            + dot(d_self_value[...], w_value, NT)
        )
        give(D_MEMORY)
        for k in (SENT, KEPT):
            give(k, slice(None), slice(CUTS[VALUE], CUTS[WRITE + 1]))
        need(11, BACKWARD.index(DOWN))
        for k in range(CHUNKS):
            need(11, BACKWARD.index(UP + k))
        need(13)

    for j in range(CHUNKS):
        need(14, j, j)
        need(15, j, j)
    d_update = d_update_ref[...]
    d_act = dot(d_update, take_down(packed, step), NT)
    d_hidden = (d_act * slope[step].reshape(total, -1).astype(F32)).astype(BF16)
    g_down = dot(act[step].reshape(total, -1), d_update, TN)
    owners = OWNERS // CHUNKS
    put(core, kept, away, g_down, step * (owners // 2), owners, CUTS[DOWN], FIELDS[DOWN])
    g_up = dot(normed[...].reshape(total, width), d_hidden, TN)
    at = pl.multiple_of(CUTS[UP] + step * PART, PART)
    put(core, kept, away, g_up, 0, OWNERS, at, PART)
    for k in (SENT, KEPT):
        give(k, slice(None), pl.ds(at, PART))
        give(k, pl.ds(step * (owners // 2), owners // 2), slice(CUTS[DOWN], CUTS[DOWN + 1]))
    d_normed_ref[...] += dot(d_hidden, take_up(packed, step), NT)

    @pl.when(step == pl.num_programs(0) - 1)
    def _():
        for k in (16, 17, 18, 19):
            need(k, 0, CHUNKS - 1)
        need(11, BACKWARD.index(OUT), CHUNKS - 1)
        gain = gains[1:2, :].astype(F32)
        unit, scale = norm_parts(middle[...].reshape(total, width))
        d_normed = d_normed_ref[...]
        g_gain[...] = jnp.sum(d_normed * unit, axis=0, keepdims=True)
        d_middle = d_result_ref[...] + norm_back(unit, scale, d_normed, gain)
        d_middle_out[...] = d_middle.reshape(count, rows, width)
        give(D_MIDDLE)
        give(G_GAIN)
        d_branch = d_middle.astype(BF16)
        for start, out in ((core * half, d_own), ((1 - core) * half, d_other)):
            weight = flat_rows(packed[pl.ds(start, half), : FIELDS[OUT], :])
            back = dot(d_branch, weight, NT).astype(BF16)
            for k in range(count):
                for pair in range(2):
                    lanes = slice(pair * LANES, (pair + 1) * LANES)
                    out[k, pair] = back[k * rows : (k + 1) * rows, lanes]
        give(D_OWN)
        give(D_OTHER)
        own_rows = jnp.concatenate(
            [
                side_by_side(
                    [
                        own[pair, pl.ds(pl.multiple_of((2 * k + core) * rows, rows), rows), :]
                        for pair in range(2)
                    ]
                )
                for k in range(count)
            ],
            axis=0,
        )
        other_rows = jnp.concatenate([side_by_side([other[k, 0], other[k, 1]]) for k in range(count)], axis=0)
        g_own = dot(own_rows, d_branch, TN)
        g_other = dot(other_rows, d_branch, TN)
        put(core, kept, away, g_own, core * (half // 2), half, 0, FIELDS[OUT])
        put(core, kept, away, g_other, (1 - core) * (half // 2), half, 0, FIELDS[OUT])
        for k in (SENT, KEPT):
            give(k, slice(None), slice(CUTS[OUT], CUTS[OUT + 1]))


def by_chunk(array):
    return array, array.shape, [((j,), (j,)) for j in range(CHUNKS)]


def backward(info, stats, stats_other, writer, memory, cots, cot_other, keys, values, packed,
             result, normed, act, slope, middle, o, other, gains):
    _, rows, width = result.shape
    slots = memory.shape[0]
    grads = ((OWNERS // 2, PACKED, width), BF16)
    half = ((2, 2, rows, LANES), BF16)
    slot = pltpu.VMEM((slots, width), BF16)
    return streamed(
        backward_kernel, "feed_forward_back", info,
        (stats, stats_other, *writer, memory, *cots, cot_other, keys, values, fields_of(packed, BACKWARD),
         result, normed, by_chunk(act), by_chunk(slope), middle, o, other, gains),
        (grads, grads, ((2, rows, width), F32), half, half, ((1, width), F32),
         ((slots, width), F32), ((slots, width), BF16)),
        [pltpu.VMEM((2, rows, width), BF16), pltpu.VMEM((2, rows, width), BF16), slot, slot, slot,
         pltpu.VMEM((slots, width), F32),
         pltpu.VMEM((2 * rows, width), F32), pltpu.VMEM((2 * rows, width), BF16),
         pltpu.VMEM((2 * rows, width), F32)],
        grid=(CHUNKS,),
    )


def head_mask(shape, head):
    lane = lax.broadcasted_iota(jnp.int32, shape, 1)
    return (lane >= head * HEAD_DIM) & (lane < (head + 1) * HEAD_DIM)


def stacked_heads(values):
    return jnp.concatenate(
        [jnp.where(head_mask(values.shape, h), values, 0.0) for h in range(HEADS)], axis=0
    )


def joined_heads(stacked, slots):
    out = None
    for h in range(HEADS):
        part = stacked[h * slots : (h + 1) * slots, :]
        shape = (slots, HEADS * HEAD_DIM)
        part = jnp.broadcast_to(part, shape)
        out = part if out is None else jnp.where(head_mask(shape, h), part, out)
    return out


def column_of_heads(values):
    return jnp.concatenate(
        [values[:, h * HEAD_DIM : h * HEAD_DIM + 1] for h in range(HEADS)], axis=0
    )


def head_sums(values):
    return jnp.concatenate(
        [
            jnp.sum(jnp.where(head_mask(values.shape, h), values, 0.0), axis=1, keepdims=True)
            for h in range(HEADS)
        ],
        axis=0,
    )


def write_step(keys, values, memory, packed, query_out, key_out, value_out, stats):
    slots = memory.shape[0]
    total = keys.shape[0] * keys.shape[1]
    rows = memory[...]
    w_write = take(packed, WRITE)
    query = dot(rows, w_write[: w_write.shape[0] // 2]).astype(BF16)
    query_out[...] = query
    key_out[...] = dot(rows, w_write[w_write.shape[0] // 2 :]).astype(BF16)
    value_out[...] = dot(rows, take(packed, VALUE)).astype(BF16)
    stacked = stacked_heads(query.astype(F32)).astype(BF16)
    scores = dot(stacked, keys[...].reshape(total, -1), NT)
    top = jnp.max(scores, axis=1, keepdims=True)
    share = jnp.exp2((scores - top) * EXP)
    stats[0] = joined_heads(top, slots)
    stats[1] = joined_heads(jnp.sum(share, axis=1, keepdims=True), slots)
    stats[2] = joined_heads(dot(share.astype(BF16), values[...].reshape(total, -1)), slots)


def write_back_step(
    info, own, other, query, key, value, memory, cot_mine, cot_recv, cot_other, keys, values,
    new_out, d_keys, d_values, d_query, d_key, d_value, cot_out,
):
    core, chip = info[0], info[1]
    slots, width = memory.shape
    part = slots // 4
    rows = keys.shape[1]
    total = keys.shape[0] * rows
    sources = (cot_mine[rows:, :], cot_recv[rows:, :], cot_other[:part, :], cot_other[part:, :])
    cot = jnp.concatenate([choose(k, core, chip, *sources) for k in range(4)], axis=0).astype(F32)
    q = query[...].astype(F32)
    sk = key[...].astype(F32)
    sv = value[...].astype(F32)
    self_column = head_sums(q * sk)
    self_scores = joined_heads(self_column, slots)
    top = jnp.maximum(jnp.maximum(own[0], other[0]), self_scores)
    own_share = jnp.exp2((own[0] - top) * EXP)
    other_share = jnp.exp2((other[0] - top) * EXP)
    self_share = jnp.exp2((self_scores - top) * EXP)
    count = own[1] * own_share + other[1] * other_share + self_share
    written = (
        own[2] * own_share + other[2] * other_share + self_share.astype(BF16).astype(F32) * sv
    ) / count
    new_out[...] = (memory[...].astype(F32) + written).astype(BF16)
    log = top + jnp.log2(count) * (1.0 / EXP)
    log_column = column_of_heads(log)
    delta_column = head_sums(cot * written)
    delta = joined_heads(delta_column, slots)
    stacked = stacked_heads(q).astype(BF16)
    stacked_cot = stacked_heads(cot).astype(BF16)
    flat_keys = keys[...].reshape(total, width)
    share = jnp.exp2((dot(stacked, flat_keys, NT) - log_column) * EXP)
    d_share = dot(stacked_cot, values[...].reshape(total, width), NT)
    d_scores = (share * (d_share - delta_column)).astype(BF16)
    d_values[...] = dot(share.astype(BF16), stacked_cot, TN).astype(BF16).reshape(d_values.shape)
    d_keys[...] = (dot(d_scores, stacked, TN) * SCALE).astype(BF16).reshape(d_keys.shape)
    d_query_part = joined_heads(dot(d_scores, flat_keys), slots) * SCALE
    mine = (lax.broadcasted_iota(jnp.int32, (slots, width), 0) // part) % 2 == core
    self_probs = jnp.exp2((self_scores - log) * EXP)
    self_dp = joined_heads(head_sums(cot * sv), slots)
    self_ds = (self_probs * (self_dp - delta)).astype(BF16).astype(F32) * SCALE
    self_ds = jnp.where(mine, self_ds, 0.0)
    d_query[...] = (d_query_part + self_ds * sk).astype(BF16)
    d_key[...] = (self_ds * q).astype(BF16)
    d_value[...] = jnp.where(mine, self_probs.astype(BF16).astype(F32) * cot, 0.0).astype(BF16)
    cot_out[...] = jnp.where(mine, cot, 0.0)


def merged_heads(heads, place):
    tiles = [ref[k, place, :] for ref in heads for k in range(ref.shape[0])]
    lane = lax.broadcasted_iota(jnp.int32, tiles[0].shape, 1)
    return side_by_side(
        [jnp.where(lane < HEAD_DIM, tiles[2 * p], tiles[2 * p + 1]) for p in range(len(tiles) // 2)]
    )


def inputs_back_step(
    info, dq_parts, dk_parts, dv_parts, packed, normed, scales, gain, d_middle,
    mine_out, away_out, g_gain, merged,
):
    core = info[0]
    rows = mine_out.shape[1]
    weights = [qkv_weight(packed, k) for k in range(3)]
    gain = gain[0:1, :].astype(F32)
    gain_sum = None
    for rank in range(4):
        place = pl.ds(rank * rows, rows)
        total = None
        for k, parts in enumerate((dq_parts, dk_parts, dv_parts)):
            grads = merged_heads(parts, place)
            merged[k, place, :] = grads
            term = dot(grads, weights[k], NT)
            total = term if total is None else total + term
        unit = normed[place, :].astype(F32) * (1.0 / gain)
        part = jnp.sum(total * unit, axis=0, keepdims=True)
        gain_sum = part if gain_sum is None else gain_sum + part
        back = norm_back(unit, scales[place, 0:1], total, gain)

        @pl.when(core == rank % 2)
        def _():
            mine_out[rank // 2] = d_middle[rank // 2] + back

        @pl.when(core != rank % 2)
        def _():
            away_out[rank // 2] = back.astype(BF16)

    g_gain[...] = gain_sum


ATTN_ROWS, INIT_ROWS, GAIN_ROWS, SMALL_ROWS = 96, 8, 4, 112


def weights_back_step(
    info, normed, merged, packed, memory, init, d_memory, g_gain, g_gain_two, dks_parts, dvs_parts,
    small, d_mine, d_away, g_ref, misc,
):
    source = jnp.concatenate([memory[...], init[...]], axis=0)
    everything = slice(0, source.shape[0])
    dks = merged_heads(dks_parts, everything)
    dvs = merged_heads(dvs_parts, everything)
    d_slots = dot(dks, qkv_weight(packed, 1), NT) + dot(dvs, qkv_weight(packed, 2), NT)
    slots = memory.shape[0]
    part = slots // 4
    total = d_memory[...] + d_slots[:slots]
    for k in range(2):
        even = total[2 * k * part : (2 * k + 1) * part]
        odd = total[(2 * k + 1) * part : (2 * k + 2) * part]
        d_mine[k * part : (k + 1) * part, :] = jnp.where(info[0] == 0, even, odd)
        d_away[k * part : (k + 1) * part, :] = jnp.where(info[0] == 0, odd, even)
    rows = normed[...]
    width = rows.shape[1]
    g_ref[:width, :] = dot(rows, merged[0], TN).astype(BF16)
    g_ref[width : 2 * width, :] = (dot(rows, merged[1], TN) + dot(source, dks, TN)).astype(BF16)
    g_ref[2 * width :, :] = (dot(rows, merged[2], TN) + dot(source, dvs, TN)).astype(BF16)
    pairs = OWNERS // 2
    small[:, :ATTN_ROWS, :] = g_ref[...].reshape(pairs, ATTN_ROWS, CORE_WIDTH)
    misc[...] = jnp.zeros_like(misc)
    each = slots // pairs
    for h in range(2):
        lanes = slice(h * CORE_WIDTH, (h + 1) * CORE_WIDTH)
        for k in range(slots):
            misc[k // each, 2 * (k % each) + h : 2 * (k % each) + h + 1, :] = d_slots[
                slots + k : slots + k + 1, lanes
            ]
        for k, gain in enumerate((g_gain, g_gain_two)):
            at = INIT_ROWS + 2 * k + h
            misc[:, at : at + 1, :] = jnp.broadcast_to(gain[:, lanes][None], (pairs, 1, CORE_WIDTH))
    small[:, ATTN_ROWS:, :] = misc[...].astype(BF16)


def last_heads_kernel(first, count, arrays, need, give, info, *refs):
    heads, refs = refs[:arrays], refs[arrays:]
    packed, refs = refs[0], refs[1:]
    earlier, refs = refs[:5], refs[5:]
    normed, scales, gain, d_middle, memory, init, d_memory, g_gain_two, refs = *refs[:8], refs[8:]
    d_mine, d_away, small, m_mine, m_away, refs = *refs[:5], refs[5:]
    results, merged, g_gain, g_ref, misc, scratch = refs[:5], *refs[5:9], refs[9:]
    need_heads(need, first, count, arrays)
    attend_back_kernel(1024, first, info, *heads[:8], heads[8:], *results, *scratch)

    @pl.when(pl.program_id(0) == pl.num_programs(0) - 1)
    def _():
        for k in range(arrays, arrays + 14):
            need(k, 0, pl.num_programs(0) - 1)
        parts = [(earlier[k], results[k]) for k in range(5)]
        inputs_back_step(
            info, *parts[:3], packed, normed, scales, gain, d_middle, d_mine, d_away, g_gain, merged
        )
        for k in range(2):
            give(k)
        weights_back_step(
            info, normed, merged, packed, memory, init, d_memory, g_gain, g_gain_two, *parts[3:],
            small, m_mine, m_away, g_ref, misc,
        )
        for k in range(2, 5):
            give(k)


def last_heads(info, first, heads, q, k, v, ks, vs, shares, own, other, o, packed, earlier,
               normed, scales, gains, d_middle, memory, init, d_memory, g_gain_two):
    length, width = normed.shape
    slots = memory.shape[0]
    part = (d_middle.shape, F32)
    away = (d_middle.shape, BF16)
    half = ((slots // 2, width), F32)
    out = pltpu.VMEM((heads, length, LANES), BF16)
    slot_out = pltpu.VMEM((heads, ks.shape[1], LANES), BF16)
    count = 8 + len(shares)
    return streamed(
        functools.partial(last_heads_kernel, first, heads, count), "last_heads", info,
        (*head_arrays(first, heads, q, k, v, ks, vs, shares, own, other, o), packed, *earlier,
         normed, scales, gains, d_middle, memory, init, d_memory, g_gain_two),
        (part, away, ((OWNERS // 2, SMALL_ROWS, CORE_WIDTH), BF16), half, half),
        [out, out, out, slot_out, slot_out, pltpu.VMEM((3, length, CORE_WIDTH), BF16),
         pltpu.VMEM((1, width), F32), pltpu.VMEM((3 * width, CORE_WIDTH), BF16),
         pltpu.VMEM((OWNERS // 2, SMALL_ROWS - ATTN_ROWS, CORE_WIDTH), F32), *back_scratch(length)],
        grid=(heads,), late=range(count, count + 14), by_piece=True,
    )


def inputs_back_kernel(
    need, give, info, mine, other, mem_mine, mem_other, new_rows, d_out, away_out, mem_out
):
    core, chip = info[0], info[1]
    count, rows, _ = mine.shape
    for k in range(count):
        need(0, k)
        need(1, k)
        back = (mine[k] + other[k].astype(F32)).astype(BF16)
        d_out[k] = back
        give(0, k)

        @pl.when(chip != k)
        def _():
            away_out[:rows, :] = back

    for j in range(2, 5):
        need(j)
    part = mem_mine.shape[0] // 2
    grads = (mem_mine[...] + mem_other[...]).astype(BF16)
    news = [
        jnp.where(
            core == 0,
            new_rows[2 * k * part : (2 * k + 1) * part, :],
            new_rows[(2 * k + 1) * part : (2 * k + 2) * part, :],
        )
        for k in range(2)
    ]
    first, second = grads[:part], grads[part:]
    mem_out[:part, :] = jnp.where(chip == 0, first, second)
    mem_out[part:, :] = jnp.where(chip == 0, news[0], news[1])
    away_out[rows : rows + part, :] = jnp.where(chip == 0, second, first)
    away_out[rows + part :, :] = jnp.where(chip == 0, news[1], news[0])
    for k in (1, 2):
        give(k)


def inputs_back(info, mine, other, mem_mine, mem_other, new_rows):
    _, rows, width = mine.shape
    slots = new_rows.shape[0]
    halves = [(array, array.shape, [((j,), (j,)) for j in range(2)]) for array in (mine, other)]
    return streamed(
        inputs_back_kernel, "inputs_back", info, (*halves, mem_mine, mem_other, new_rows),
        ((mine.shape, BF16), ((rows + slots // 2, width), BF16), ((slots // 2, width), BF16)),
    )


def swap(value, over_batch, over_seq):
    batch, seq = lax.axis_size("batch"), lax.axis_size("seq")
    pairs = [
        (i * seq + j, (i ^ over_batch) * seq + (j ^ over_seq))
        for i in range(batch)
        for j in range(seq)
    ]
    return lax.ppermute(value, ("batch", "seq"), pairs)


def chip_groups():
    batch = lax.axis_index("batch")
    chip = lax.axis_index("seq") // 2
    stages = [(4, 2 * (batch & 1) + chip, lambda k: (k >> 1, 2 * (k & 1)))]
    bits = lax.axis_size("batch").bit_length() - 1
    at = 1
    while at < bits:
        count = min(2, bits - at)
        stages.append(
            (1 << count, (batch >> at) & ((1 << count) - 1), lambda k, at=at: (k << at, 0))
        )
        at += count
    return stages


def in_order(pieces, own):
    bit = 1
    while bit < len(pieces):
        turned = (own & bit) > 0
        pieces = [jnp.where(turned, pieces[k ^ bit], pieces[k]) for k in range(len(pieces))]
        bit *= 2
    return jnp.stack(pieces)


def gather_chips(piece):
    stages = chip_groups()
    shape = piece.shape
    for size, own, peer in reversed(stages):
        piece = in_order([piece] + [swap(piece, *peer(k)) for k in range(1, size)], own)
    count = len(stages)
    piece = piece.transpose(*reversed(range(count)), *range(count, piece.ndim))
    return piece.reshape(-1, *shape)


def square_groups():
    batch, seq = lax.axis_size("batch"), lax.axis_size("seq")
    return [
        [(2 * r + y) * seq + 2 * x + core for y in range(2) for x in range(2)]
        for r in range(batch // 2)
        for core in range(2)
    ]


def line_groups():
    batch, seq = lax.axis_size("batch"), lax.axis_size("seq")
    return [
        [(2 * r + y) * seq + s for r in range(batch // 2)] for y in range(2) for s in range(seq)
    ]


def sent_lines(rows, stages):
    parts = [rows]
    for stage in stages[1:]:
        parts = sent(spread(added(parts, BF16), stage), stage)
    return parts


def sum_scattered(rows, groups):
    return lax.psum_scatter(
        rows, ("batch", "seq"), scatter_dimension=0, tiled=True, axis_index_groups=groups
    )


def spread(pieces, stage):
    size, own, _ = stage
    pieces = pieces.reshape(-1, size, *pieces.shape[-2:])
    return [lax.dynamic_index_in_dim(pieces, own ^ j, 1, keepdims=False) for j in range(size)]


def sent(parts, stage):
    size, _, peer = stage
    return [parts[0]] + [swap(parts[j], *peer(j)) for j in range(1, size)]


def added(parts, kind):
    total = parts[0].astype(F32)
    for part in parts[1:]:
        total = total + part.astype(F32)
    return total.astype(kind)


def after(values, *others):
    return lax.optimization_barrier((values, others))[0]


def by_core(core, mine, other, axis=0):
    return jnp.where(
        core == 0,
        jnp.concatenate([mine, other], axis=axis),
        jnp.concatenate([other, mine], axis=axis),
    )


def by_chip(chip, mine, other):
    return jnp.where(chip == 0, jnp.stack([mine, other]), jnp.stack([other, mine]))


def pick(array, index, axis=0):
    return lax.dynamic_index_in_dim(array, index, axis, keepdims=False)


def to_owners(fields, devices):
    many = devices // OWNERS
    out = []
    for k, field in enumerate(fields):
        if many > 1:
            groups = CHUNKS if k == UP else 1
            field = field.reshape(OWNERS, many, groups, -1, field.shape[-1])
            field = field.transpose(0, 2, 1, 3, 4).reshape(OWNERS, -1, field.shape[-1])
        out.append(field)
    return jnp.concatenate(out, axis=1)


def from_owners(packed, devices):
    many = devices // OWNERS
    out = []
    for k in range(len(FIELDS)):
        field = packed[:, CUTS[k] : CUTS[k + 1]]
        groups = CHUNKS if k == UP else 1
        field = field.reshape(OWNERS, groups, many, -1, field.shape[-1])
        out.append(field.transpose(0, 2, 1, 3, 4).reshape(devices, -1, field.shape[-1]))
    return jnp.concatenate(out, axis=1)


def per_device(
    tokens, memory, lengths, resets, attn_in, attn_out, ffn_in, ffn_out, writer_in, writer_value,
    norm_gains, memory_init, out_cotangent, memory_cotangent,
):
    _, rows, width = tokens.shape
    devices = lax.axis_size("batch") * lax.axis_size("seq")
    rank = lax.axis_index("seq")
    chip, core = rank // 2, rank % 2
    slot_part = memory.shape[1]
    slots = 4 * slot_part
    stages = chip_groups()

    ends = jnp.cumsum(pick(lengths, chip))
    info = jnp.concatenate([jnp.stack([core, chip]), ends, pick(resets, chip)]).astype(jnp.int32)

    def to_chip(big, small):
        mine = jnp.concatenate([pick(big, chip), pick(small, chip)], axis=0)
        away = jnp.concatenate([pick(big, 1 - chip), pick(small, 1 - chip)], axis=0)
        return mine, swap(away, 0, 2)

    misc = jnp.concatenate([memory_init, norm_gains])
    misc_rows = -(-misc.shape[0] // CORE_WIDTH)
    misc = jnp.pad(misc, (0, misc_rows * CORE_WIDTH - misc.shape[0])).reshape(misc_rows, CORE_WIDTH)
    attn_rows = attn_in.reshape(-1, 2, CORE_WIDTH)
    own_rows = attn_rows.shape[0]
    mine = jnp.concatenate([pick(attn_rows, core, 1), misc], axis=0)
    theirs = swap(jnp.concatenate([pick(attn_rows, 1 - core, 1), misc], axis=0), 0, 1)
    piece = jnp.concatenate(
        [
            by_core(core, mine[:own_rows], theirs[:own_rows]),
            by_core(core, mine[own_rows:], theirs[own_rows:]),
        ],
        axis=0,
    )
    gathered = gather_chips(piece)
    misc = gathered[:, 2 * own_rows :].reshape(devices, -1)
    init = misc[:, : memory_init.shape[0]].reshape(slots, width)
    gains = misc[:, memory_init.shape[0] :][:, : norm_gains.shape[0]].reshape(2, width)
    w_qkv = gathered
    if devices != OWNERS:
        w_qkv = gathered[:, : 2 * own_rows].reshape(OWNERS // 2, -1, CORE_WIDTH)

    columns = ffn_in.reshape(-1, CHUNKS, width).transpose(1, 0, 2).reshape(-1, width)
    fields = [attn_out, writer_value, writer_in, ffn_out, ffn_in]
    sizes = [field.shape[0] // width for field in fields]
    parts = [jnp.concatenate(fields[:UP]).reshape(-1, width), columns]
    cuts = [sum(sizes[:k]) for k in range(len(sizes) + 1)]
    packed = lax.all_gather(jnp.concatenate(parts, axis=0), ("batch", "seq"), axis=0)
    if devices != OWNERS:
        packed = to_owners([packed[:, cuts[k] : cuts[k + 1]] for k in range(len(sizes))], devices)

    own, recv = to_chip(tokens, memory)
    sources = (own, recv, swap(own, 0, 1), swap(recv, 0, 1))
    q_log, k, v, ks, vs, normed, own_tokens, mem_rows, o, o_away, scales, *shares = read(
        info, sources, w_qkv, init, gains, rows
    )
    out_cotangent, memory_cotangent = after((out_cotangent, memory_cotangent), recv)
    cots = to_chip(out_cotangent, memory_cotangent)
    cot_other = swap(jnp.concatenate([cot[rows:] for cot in after(cots, o)], axis=0), 0, 1)
    o_other = swap(o_away, 0, 1)
    middle, normed_two, act, slope, result, keys, values, result_away, *writer, stats = forward(
        info, own_tokens, o, o_other, packed, gains, mem_rows
    )
    came = swap(result_away, 0, 2)
    stats_other = swap(stats, 0, 1)
    kept, away, d_middle, d_own, d_away, g_gain_two, d_memory, new_rows = backward(
        info, stats, stats_other, writer, mem_rows, cots, cot_other, keys, values, packed, result,
        normed_two, act, slope, middle, o, o_other, gains,
    )
    d_other, came = after((swap(d_away, 0, 1), came), came)
    if devices != OWNERS:
        both = by_core(core, kept[:, None], away[:, None], axis=1).reshape(OWNERS, PACKED, width)
        both = from_owners(both, devices).reshape(devices // 2, 2, -1, width)
        kept, away = pick(both, core, 1), pick(both, 1 - core, 1)
    arrived = swap(after(away, d_other), 0, 1)

    heads = (q_log, k, v, ks, vs, shares)
    grads_a = attend_back(info, 0, 1, *heads, d_own, d_other, o)
    kept, arrived = after((kept, arrived), grads_a)
    square = [
        added(pair, BF16) for pair in zip(spread(kept, stages[0])[1:], spread(arrived, stages[0])[1:])
    ]
    d_own = after(d_own, square)
    square = [swap(part, *stages[0][2](k + 1)) for k, part in enumerate(square)]
    d_mine, d_away, small, mem_mine, mem_away = last_heads(
        info, 1, 3, *heads, d_own, d_other, o, w_qkv, grads_a, normed, scales, gains,
        d_middle, mem_rows, init, d_memory, g_gain_two,
    )
    d_sent = swap(d_away, 0, 1)
    m_sent = swap(mem_away, 0, 1)

    init_size = memory_init.shape[0]
    init_rows = 2 * init_size // CORE_WIDTH
    cut_init, cut_gain = 2 * own_rows, 2 * own_rows + init_rows
    if devices != OWNERS:
        pairs = devices // 2
        small = jnp.concatenate(
            [
                small[:, :ATTN_ROWS].reshape(pairs, -1, CORE_WIDTH),
                small[:, ATTN_ROWS : ATTN_ROWS + INIT_ROWS].reshape(pairs, -1, CORE_WIDTH),
                jnp.repeat(small[:, ATTN_ROWS + INIT_ROWS :], pairs // (OWNERS // 2), axis=0),
            ],
            axis=1,
        )
    small_parts = sent(spread(small, stages[0]), stages[0])
    square, kept, arrived = after((square, kept, arrived), small)
    own = [spread(array, stages[0])[0] for array in (kept, arrived)]
    parts = sent_lines(added(own + square, BF16), stages)
    d_sent = after(d_sent, parts[0])
    d_tokens, d_tokens_away, mem_out = inputs_back(info, d_mine, d_sent, mem_mine, m_sent, new_rows)
    home = swap(after(d_tokens_away, small_parts), 0, 2)
    parts, small_parts = after(parts, d_tokens), after(small_parts, d_tokens)
    result, came = after((result, came), small_parts)
    for stage in stages[1:]:
        small_parts = sent(spread(added(small_parts, BF16), stage), stage)
    small_parts = after(small_parts, home)
    summed = added(parts, F32).reshape(-1, width)
    small = added(small_parts, F32).reshape(-1, CORE_WIDTH)
    big = [summed[cuts[k] : cuts[k + 1]] for k in range(len(sizes))]
    big[UP] = big[UP].reshape(CHUNKS, -1, width).transpose(1, 0, 2)
    small_attn = small[:cut_init].reshape(2, own_rows, CORE_WIDTH)
    small_init = small[cut_init:cut_gain].reshape(2, init_size)
    if init_rows % 2 == 0:
        small_init = small[cut_init:cut_gain].reshape(2, init_rows // 2, CORE_WIDTH)
    small_gain = small[cut_gain : cut_gain + GAIN_ROWS]
    if init_rows % 2 == 0:
        back = swap(
            jnp.concatenate(
                [pick(small_attn, 1 - core), pick(small_init, 1 - core), small_gain], axis=0
            ),
            0, 1,
        )
        init_back = back[own_rows : own_rows + init_rows // 2]
        gain_back = back[own_rows + init_rows // 2 :]
    else:
        back = swap(pick(small_attn, 1 - core), 0, 1)
        init_back = swap(pick(small_init, 1 - core), 0, 1)
        gain_back = swap(small_gain, 0, 1)
    attn_grad = by_core(core, pick(small_attn, core), back[:own_rows], axis=1)
    init_grad = (pick(small_init, core) + init_back).reshape(-1)
    device = lax.axis_index("batch") * lax.axis_size("seq") + rank
    gain_size = norm_gains.shape[0]
    gain_rows = (small_gain + gain_back).reshape(devices, gain_size)
    ours = jnp.arange(devices, dtype=jnp.int32)[:, None] == device
    gain_grad = jnp.sum(jnp.where(ours, gain_rows, 0.0), axis=0)

    def at_home(both, new):
        return lax.dynamic_update_index_in_dim(both, new, 1 - chip, 0)

    mem_came = home[rows:]
    return (
        at_home(result, came),
        by_chip(chip, mem_out[slot_part:], mem_came[slot_part:]),
        at_home(d_tokens, home[:rows]),
        by_chip(chip, mem_out[:slot_part], mem_came[:slot_part]),
        attn_grad.reshape(-1),
        *[big[k].reshape(-1) for k in (OUT, UP, DOWN, WRITE, VALUE)],
        gain_grad,
        init_grad,
    )


def solution(mesh):
    rows = P("batch", "seq", None)
    table = P("batch", None)
    flat = P(("batch", "seq"))
    return jax.shard_map(
        per_device,
        mesh=mesh,
        in_specs=(rows, rows, table, table, *[flat] * 8, rows, rows),
        out_specs=(rows, rows, rows, rows, *[flat] * 8),
        check_vma=False,
    )
```
